32 devices in a mesh: dp: 8 (over z, y), code: 4 (over x, core).
Axes of the slice: x: 2, y: 2, z: 4, core: 2. Of those that a mesh axis runs over, the one named last changes fastest.
Arguments:
- codebook: bfloat16 [25088, 768], P(('dp', 'code')), may hold values from -6 to 6
- projector: bfloat16 [768, 256], replicated, may hold values from -0.21875 to 0.21875
- latents: bfloat16 [64, 16, 16, 256], P(('dp', 'code')), may hold values from -6 to 6
- wanted: int32 [32, 32, 8], P(('dp', 'code')), may hold values from 0 to 783
- wanted_count: int32 [32, 32], P(('dp', 'code')), may hold values from 1 to 8, as said below
- token_pick: int32 [64, 16, 16], P(('dp', 'code')), may hold values from 0 to 255
- kernel: bfloat16 [3, 3, 256, 512], replicated, may hold values from -0.125 to 0.125
- bias: bfloat16 [512], replicated, may hold values from -3 to 3
- cotangent: bfloat16 [64, 16, 16, 512], P(('dp', 'code')), may hold values from -6 to 6
Outputs:
- hidden: bfloat16 [64, 16, 16, 512], P(('dp', 'code'))
- grad_latents: bfloat16 [64, 16, 16, 256], P(('dp', 'code'))
- proj_step: float32 [768, 256], replicated
- kernel_step: float32 [3, 3, 256, 512], replicated
- bias_step: float32 [512], replicated
The draws below stay inside these ranges and needn't reach their ends.
Inputs may be any that keep to these rules, and one draw needn't show every extreme that they name: `wanted_count`: for one owner chosen in each draw every requester's list is full; the others hold 1 to 8 live entries. `wanted`: offsets into the owner's 784 entries; entries past the live count are unused.
All inputs are finite; a program needn't handle non-finite values.
Results may differ from the reference program's by a relative error of at most 0.0046.
Values may be sent and summed in bfloat16 or wider, within the bound.
No kernel may reach another device: no remote copies, remote signals or barrier semaphores. Data moves between devices by JAX's collectives and lax.ppermute only.
A program may use at most 64 MiB of HBM per device.

```python
import math
import jax
import jax.numpy as jnp
import numpy as np
from jax import lax

FEAT = 768
ZCH = 256
CH = 512
GRID = 16
ROWS_DEV = 784
CAP = 8
IMG_DEV = 2
VOCAB = 25088
IMAGES = 64
N_DP = 8
N_CODE = 4


def draw_wanted_count(key, part):
    key = jax.random.fold_in(key, 7)
    first, second = jax.random.split(key)
    owners = N_DP * N_CODE
    counts = jax.random.randint(first, (owners, owners), 1, CAP + 1)
    hottest = jax.random.randint(second, (), 0, owners)
    column = jnp.arange(owners, dtype=jnp.int32)[None, :]
    return jnp.where(column == hottest, CAP, counts).astype(jnp.int32)


def set_ends(result, stream_key, low, largest):
    longest = result.shape.index(max(result.shape))
    spots = []
    for shift in (0, 1):
        where = [jax.random.randint(jax.random.fold_in(stream_key, axis), (), 0, length) for axis, length in enumerate(result.shape)]
        where[longest] = (where[longest] + shift) % result.shape[longest]
        spots.append(tuple(where))
    return result.at[spots[0]].set(low).at[spots[1]].set(largest)


def level_of(key, dims, pieces, low, largest):
    gain = 1.0
    for dim, shards_of in pieces:
        steps = jax.random.uniform(jax.random.fold_in(jax.random.fold_in(key, 6), dim), (shards_of,), jnp.float32, low / len(pieces), largest / len(pieces))
        gain = gain * jnp.repeat(jnp.exp(steps), dims[dim] // shards_of).reshape((-1,) + (1,) * (len(dims) - 1 - dim))
    return gain


def rank_bounds(number_of, slope):
    weights = [(1 << 20) // math.isqrt(standing ** slope) + 1 for standing in range(1, number_of + 1)]
    scale = 1 + sum(weights) // (1 << 30)
    return np.cumsum(np.array([max(1, weight // scale) for weight in weights]))


def skewed_ids(own_key, extent, count, skew):
    listing = rank_bounds(count, skew)
    ticket = jax.random.randint(jax.random.fold_in(own_key, 1), extent, 0, int(listing[count - 1]))
    grade = jnp.searchsorted(jnp.asarray(listing, jnp.int32), ticket, side="right")
    return jax.random.permutation(jax.random.fold_in(own_key, 2), count)[grade].astype(jnp.int32)


def bell_draw(own_key, extent, width, most, pieces=(), kind=jnp.bfloat16):
    values = jax.random.normal(own_key, extent, jnp.float32) * width
    if len(pieces) > 0:
        values = level_of(own_key, extent, pieces, -0.22, 0.18) * values
    return jnp.clip(values, min=-most, max=most).astype(kind)


def setup_inputs(seed: int = 0) -> dict:
    splits = jax.random.split(jax.random.key(seed), 10)
    codebook = bell_draw(splits[0], (VOCAB, FEAT), 1.0, 6.0, ((0, 32),))
    projector = bell_draw(splits[1], (FEAT, ZCH), FEAT ** -0.5, 0.21875)
    latents = bell_draw(splits[2], (IMAGES, GRID, GRID, ZCH), 1.0, 6.0, ((0, 32),))
    wanted = set_ends(jax.random.randint(splits[3], (N_DP * N_CODE, N_DP * N_CODE, CAP), 0, ROWS_DEV), jax.random.fold_in(splits[3], 1), 0, ROWS_DEV - 1).astype(jnp.int32)
    wanted_count = draw_wanted_count(jax.random.fold_in(splits[9], 71), 0)
    token_pick = set_ends(skewed_ids(splits[5], (IMAGES, GRID, GRID), N_DP * N_CODE * CAP, 2), jax.random.fold_in(splits[5], 3), 0, (N_DP * N_CODE * CAP) - 1).astype(jnp.int32)
    kernel = bell_draw(splits[6], (3, 3, ZCH, CH), (9 * ZCH) ** -0.5, 0.125)
    bias = bell_draw(splits[7], (CH,), 0.5, 3.0)
    cotangent = bell_draw(splits[8], (IMAGES, GRID, GRID, CH), 1.0, 6.0, ((0, 32),))
    return {"codebook": codebook, "projector": projector, "latents": latents, "wanted": wanted, "wanted_count": wanted_count, "token_pick": token_pick, "kernel": kernel, "bias": bias, "cotangent": cotangent}


commit_weight = 0.25
norm_eps = 1e-06

def unit_scale(values):
    return values / jnp.sqrt(jnp.mean(values * values) + norm_eps)

def conv_same(inputs, weights):
    return lax.conv_general_dilated(inputs, weights, (1, 1), 'SAME', dimension_numbers=('NHWC', 'HWIO', 'NHWC'), precision=lax.Precision.HIGHEST)

def reference(codebook, projector, latents, wanted, wanted_count, token_pick, kernel, bias, cotangent):
    codes = jnp.dot(codebook, projector, preferred_element_type=jnp.float32).astype(jnp.bfloat16)
    image_ids = jnp.arange(IMAGES, dtype=jnp.int32)[:, None, None]
    requester = image_ids // IMG_DEV
    requester = jnp.broadcast_to(requester, token_pick.shape).astype(jnp.int32)
    owner = (token_pick // CAP).astype(jnp.int32)
    count = wanted_count[requester, owner]
    entry = (token_pick % CAP % count).astype(jnp.int32)
    code_id = (owner * ROWS_DEV + wanted[requester, owner, entry]).astype(jnp.int32)
    quant = codes[code_id]
    quant_f = quant.astype(jnp.float32)
    latent_f = latents.astype(jnp.float32)
    hidden_f, pullback = jax.vjp(conv_same, quant_f, kernel.astype(jnp.float32))
    hidden = (hidden_f + bias.astype(jnp.float32)).astype(jnp.bfloat16)
    grad_input, grad_kernel = pullback(cotangent.astype(jnp.float32))
    grad_bias = lax.optimization_barrier(jnp.sum(cotangent.astype(jnp.float32), axis=(0, 1, 2)))
    grad_latents = (grad_input + 2.0 * commit_weight * (latent_f - quant_f)).astype(jnp.bfloat16)
    grad_quant = 2.0 * (quant_f - latent_f)
    grad_codes = jnp.zeros((VOCAB, ZCH), jnp.float32).at[code_id.reshape(-1)].add(grad_quant.reshape(-1, ZCH))
    grad_proj = jnp.dot(codebook.astype(jnp.float32).T, grad_codes, precision=lax.Precision.HIGHEST)
    return (hidden, grad_latents, unit_scale(grad_proj), unit_scale(grad_kernel), unit_scale(grad_bias))
```

```python
import functools

import jax
import jax.numpy as jnp
from jax import lax
from jax.experimental import pallas as pl
from jax.experimental.pallas import tpu as pltpu
from jax.sharding import PartitionSpec as P

commit_weight = 0.25
norm_eps = 1e-06
AXES = ("dp", "code")
PARTS = 4


class Grid:
    def __init__(self, n_dp, n_code):
        self.n_dp, self.n_code = n_dp, n_code
        self.outer = n_code // 4
        self.planes = (n_dp // 2) * self.outer
        self.total = n_dp * n_code

    def linear(self, r, i):
        dh, ch = r // self.outer, r % self.outer
        return (dh * 2 + i // 4) * self.n_code + ch * 4 + i % 4

    def perm(self, move):
        return [
            (self.linear(r, i), self.linear(*move(r, i)))
            for r in range(self.planes)
            for i in range(8)
        ]

    def flip(self, bit):
        return self.perm(lambda r, i: (r, i ^ bit))

    def turn(self, k):
        return self.perm(lambda r, i: (r // PARTS * PARTS + (r + k) % PARTS, i))

    def far(self, k):
        groups = self.planes // PARTS
        return self.perm(lambda r, i: ((r // PARTS + k) % groups * PARTS + r % PARTS, i))

    def place(self):
        dp, code = lax.axis_index("dp"), lax.axis_index("code")
        return (dp // 2) * self.outer + code // 4, (dp % 2) * 4 + code % 4


def send(x, perm):
    return lax.ppermute(x, AXES, perm)


def half(x, axis, index):
    return lax.dynamic_index_in_dim(x, index, axis, keepdims=False)


def exchange(x, axis, own, perm):
    sent = half(x, axis, 1 - own).astype(jnp.bfloat16)
    return half(x, axis, own) + send(sent, perm).astype(jnp.float32)


def reduce_planes(grid, x, r):
    part = r % PARTS
    got = half(x, 0, part)
    for k in range(1, PARTS):
        sent = half(x, 0, (part + k) % PARTS).astype(jnp.bfloat16)
        got = got + send(sent, grid.turn(k)).astype(jnp.float32)
    groups = grid.planes // PARTS
    if groups > 1:
        rest = [got] + [send(got, grid.far(k)) for k in range(1, groups)]
        order = (r // PARTS - jnp.arange(groups)) % groups
        got = jnp.sum(jnp.take(jnp.stack(rest), order, axis=0), axis=0)
    return got


def reduce_scatter(grid, x, r, i):
    x = x.reshape(2, 2, 2, PARTS, *x.shape[2:])
    core, col, row = i % 2, i // 2 % 2, i // 4
    x = exchange(x, 2, core, grid.flip(1))
    cut = PARTS // 2
    first = exchange(x[:, :, :cut], 1, col, grid.flip(2))
    second = exchange(x[:, :, cut:], 0, row, grid.flip(4))
    first = exchange(first, 0, row, grid.flip(4))
    second = exchange(second, 0, col, grid.flip(2))
    return reduce_planes(grid, jnp.concatenate([first, second]), r)


def all_gather(grid, own):
    zs = jnp.stack([own] + [send(own, grid.turn(k)) for k in range(1, PARTS)])
    xs, ys = send(zs, grid.flip(2)), send(zs, grid.flip(4))
    cut = PARTS // 2
    near, far = send(xs[:cut], grid.flip(4)), send(ys[cut:], grid.flip(2))
    mine = jnp.concatenate([zs, xs, ys, near, far])
    return mine, send(mine, grid.flip(1))


def butterfly(grid, x):
    bit = 1
    while bit < grid.total:
        x = x + send(x, [(d, d ^ bit) for d in range(grid.total)])
        bit *= 2
    return x


def finish_kernel(order_ref, mine_ref, other_ref, kernel_ref, proj_ref, *, krows, prows, kcount, pcount):
    slice_rows = krows // 9
    ksum = jnp.zeros((8, 128), jnp.float32)
    psum = jnp.zeros((8, 128), jnp.float32)

    def load(e):
        src = order_ref[e]
        core = src // 16
        return src, core

    def body(e, sums):
        src, core = load(e)

        def total(ref):
            v = ref[src % 16].astype(jnp.float32)
            v = v * v
            return (
                jnp.sum(v[:krows].reshape(krows // 8, 8, 128), axis=0),
                jnp.sum(v[krows : krows + prows].reshape(prows // 8, 8, 128), axis=0),
            )

        a, b = lax.cond(core == 0, lambda: total(mine_ref), lambda: total(other_ref))
        return sums[0] + a, sums[1] + b

    ksum, psum = lax.fori_loop(0, 32, body, (ksum, psum))

    def factor(v, count):
        s = jnp.sum(jnp.sum(v, axis=0, keepdims=True), axis=1, keepdims=True)
        return 1.0 / jnp.sqrt(s / count + norm_eps)

    kf, pf = factor(ksum, kcount), factor(psum, pcount)
    for e in range(32):
        i, q = e // 4, e % 4
        src, core = load(e)
        row = (i // 2 % 2) * 2 + i // 4
        row = row * 4 * prows + q * prows
        col = (i % 2) * 128

        def put(ref):
            v = ref[src % 16].astype(jnp.float32)
            kernel_ref[:, i * slice_rows : (i + 1) * slice_rows, q * 128 : (q + 1) * 128] = (
                v[:krows] * kf
            ).reshape(9, slice_rows, 128)
            proj_ref[row : row + prows, col : col + 128] = v[krows : krows + prows] * pf

        pl.when(core == 0)(functools.partial(put, mine_ref))
        pl.when(core == 1)(functools.partial(put, other_ref))


def finish(order, mine, other, zch, channels, feat):
    krows, prows = 9 * zch // 8, feat // 16
    body = functools.partial(
        finish_kernel,
        krows=krows,
        prows=prows,
        kcount=9 * zch * channels,
        pcount=feat * zch,
    )
    return pl.pallas_call(
        body,
        out_shape=(
            jax.ShapeDtypeStruct((9, zch, channels), jnp.float32),
            jax.ShapeDtypeStruct((feat, zch), jnp.float32),
        ),
        in_specs=[
            pl.BlockSpec(memory_space=pltpu.SMEM),
            pl.BlockSpec(memory_space=pltpu.VMEM),
            pl.BlockSpec(memory_space=pltpu.VMEM),
        ],
        out_specs=(
            pl.BlockSpec(memory_space=pltpu.VMEM),
            pl.BlockSpec(memory_space=pltpu.VMEM),
        ),
        compiler_params=pltpu.CompilerParams(vmem_limit_bytes=24 << 20),
    )(order, mine, other)


def split_product(left, right):
    upper = right.astype(jnp.bfloat16)
    lower = (right - upper.astype(jnp.float32)).astype(jnp.bfloat16)
    dims = (((0,), (0,)), ((), ()))
    first = lax.dot_general(left, upper, dims, preferred_element_type=jnp.float32)
    return first + lax.dot_general(left, lower, dims, preferred_element_type=jnp.float32)


def on_device(
    grid, codebook, projector, latents, wanted, wanted_count, token_pick, kernel, bias, cotangent
):
    devices = lax.axis_size(("dp", "code"))
    images, rows, width, zch = latents.shape
    channels = kernel.shape[3]
    feat = codebook.shape[1]
    rows_dev = codebook.shape[0]
    cap = wanted.shape[2]
    slots = devices * cap
    tokens = images * rows * width
    requests = wanted.reshape(devices, cap)
    counts = wanted_count.reshape(devices)
    pick = token_pick.reshape(tokens)
    owner = pick // cap
    owner_hit = owner[:, None] == jnp.arange(devices, dtype=jnp.int32)[None, :]
    count = jnp.sum(jnp.where(owner_hit, counts[None, :], 0), axis=1)
    slot = owner * cap + pick % cap % count
    asked = lax.all_to_all(
        requests, ("dp", "code"), split_axis=0, concat_axis=0, tiled=True
    ).reshape(slots)
    select = (asked[:, None] == jnp.arange(rows_dev, dtype=jnp.int32)[None, :]).astype(jnp.bfloat16)
    local_codes = jnp.dot(codebook, projector, preferred_element_type=jnp.float32).astype(
        jnp.bfloat16
    )
    answer = jnp.dot(select, local_codes, preferred_element_type=jnp.float32).astype(jnp.bfloat16)
    slot_codes = lax.all_to_all(
        answer.reshape(devices, cap, zch), ("dp", "code"), split_axis=0, concat_axis=0, tiled=True
    ).reshape(slots, zch)
    slot_ids = jnp.arange(slots, dtype=jnp.int32)
    onehot = (slot[:, None] == slot_ids[None, :]).astype(jnp.bfloat16)
    quant = jnp.dot(onehot, slot_codes, preferred_element_type=jnp.float32).astype(jnp.bfloat16)
    quant = quant.reshape(images, rows, width, zch)
    quant_f = quant.astype(jnp.float32)
    latent_f = latents.astype(jnp.float32)
    grad_quant = 2.0 * (quant_f - latent_f)
    slot_grads = split_product(onehot, grad_quant.reshape(tokens, zch))
    returned = (
        lax.all_to_all(
            slot_grads.reshape(devices, cap, zch).astype(jnp.bfloat16),
            ("dp", "code"),
            split_axis=0,
            concat_axis=0,
            tiled=True,
        )
        .astype(jnp.float32)
        .reshape(slots, zch)
    )
    grad_rows = split_product(select, returned)
    grad_proj = split_product(codebook, grad_rows)
    padded = jnp.pad(quant, ((0, 0), (1, 1), (1, 1), (0, 0)))
    padded_grad = jnp.pad(cotangent, ((0, 0), (1, 1), (1, 1), (0, 0)))
    output = jnp.zeros((images, rows, width, channels), jnp.float32)
    grad_input = jnp.zeros((images, rows, width, zch), jnp.float32)
    taps = []
    for row_off in range(3):
        for col_off in range(3):
            window = padded[:, row_off : row_off + rows, col_off : col_off + width]
            output = output + jnp.einsum(
                "nhwc,co->nhwo",
                window,
                kernel[row_off, col_off],
                preferred_element_type=jnp.float32,
            )
            grad_window = padded_grad[
                :, 2 - row_off : 2 - row_off + rows, 2 - col_off : 2 - col_off + width
            ]
            grad_input = grad_input + jnp.einsum(
                "nhwo,co->nhwc",
                grad_window,
                kernel[row_off, col_off],
                preferred_element_type=jnp.float32,
            )
            taps.append(
                jnp.einsum("nhwc,nhwo->co", window, cotangent, preferred_element_type=jnp.float32)
            )
    hidden = (output + bias.astype(jnp.float32)).astype(jnp.bfloat16)
    grad_kernel = jnp.stack(taps)
    grad_bias = butterfly(grid, jnp.sum(cotangent.astype(jnp.float32), axis=(0, 1, 2)))
    grad_latents = (grad_input + 2.0 * commit_weight * (latent_f - quant_f)).astype(jnp.bfloat16)

    r, i = grid.place()
    krows, prows, wide = 9 * zch // 8, feat // 16, channels // PARTS
    kpart = (
        grad_kernel.reshape(9, 8, zch // 8, PARTS, wide)
        .transpose(1, 3, 0, 2, 4)
        .reshape(8, PARTS, krows, wide)
    )
    ppart = (
        grad_proj.reshape(2, 2, PARTS, prows, 2, zch // 2)
        .transpose(1, 0, 4, 2, 3, 5)
        .reshape(8, PARTS, prows, zch // 2)
    )
    total = reduce_scatter(grid, jnp.concatenate([kpart, ppart], axis=2), r, i)
    mine, other = all_gather(grid, total.astype(jnp.bfloat16))
    e = jnp.arange(32, dtype=jnp.int32)
    rel_i, rel_r = (e // 4) ^ i, (r - e % 4) % 4
    order = (rel_i % 2) * 16 + (rel_i // 2) * 4 + rel_r
    kernel_step, proj_step = finish(order, mine, other, zch, channels, feat)
    kernel_step = kernel_step.reshape(3, 3, zch, channels)
    bias_step = grad_bias / jnp.sqrt(jnp.sum(grad_bias * grad_bias) / channels + norm_eps)
    return (hidden, grad_latents, proj_step, kernel_step, bias_step)


def solution(mesh):
    grid = Grid(mesh.shape["dp"], mesh.shape["code"])
    in_specs = (
        P(("dp", "code"), None),
        P(),
        P(("dp", "code"), None, None, None),
        P(("dp", "code"), None, None),
        P(("dp", "code"), None),
        P(("dp", "code"), None, None),
        P(),
        P(),
        P(("dp", "code"), None, None, None),
    )
    out_specs = (
        P(("dp", "code"), None, None, None),
        P(("dp", "code"), None, None, None),
        P(),
        P(),
        P(),
    )
    return jax.shard_map(
        functools.partial(on_device, grid),
        mesh=mesh,
        in_specs=in_specs,
        out_specs=out_specs,
        check_vma=False,
    )
```

```python
import functools

import jax
import jax.numpy as jnp
from jax import lax
from jax.experimental import pallas as pl
from jax.experimental.pallas import tpu as pltpu
from jax.sharding import PartitionSpec as P

commit_weight = 0.25
norm_eps = 1e-06
AXES = ("dp", "code")
PARTS = 4


class Grid:
    def __init__(self, n_dp, n_code):
        self.n_dp, self.n_code = n_dp, n_code
        self.outer = n_code // 4
        self.planes = (n_dp // 2) * self.outer
        self.total = n_dp * n_code

    def linear(self, r, i):
        dh, ch = r // self.outer, r % self.outer
        return (dh * 2 + i // 4) * self.n_code + ch * 4 + i % 4

    def perm(self, move):
        return [
            (self.linear(r, i), self.linear(*move(r, i)))
            for r in range(self.planes)
            for i in range(8)
        ]

    def flip(self, bit):
        return self.perm(lambda r, i: (r, i ^ bit))

    def turn(self, k):
        return self.perm(lambda r, i: (r // PARTS * PARTS + (r + k) % PARTS, i))

    def far(self, k):
        groups = self.planes // PARTS
        return self.perm(lambda r, i: ((r // PARTS + k) % groups * PARTS + r % PARTS, i))

    def order(self, x):
        rest = x.shape[2:]
        x = x.reshape(self.n_dp // 2, self.outer, 2, 4, *rest)
        return jnp.swapaxes(x, 1, 2).reshape(self.total, *rest)

    def place(self):
        dp, code = lax.axis_index("dp"), lax.axis_index("code")
        return (dp // 2) * self.outer + code // 4, (dp % 2) * 4 + code % 4


def send(x, perm):
    return lax.ppermute(x, AXES, perm)


def all_gather(grid, own):
    zs = jnp.stack([own] + [send(own, grid.turn(k)) for k in range(1, PARTS)])
    xs, ys = send(zs, grid.flip(2)), send(zs, grid.flip(4))
    cut = PARTS // 2
    near, far = send(xs[:cut], grid.flip(4)), send(ys[cut:], grid.flip(2))
    mine = jnp.concatenate([zs, xs, ys, near, far])
    return mine, send(mine, grid.flip(1))


def vmem(count):
    return [pl.BlockSpec(memory_space=pltpu.VMEM)] * count


SMEM_SPEC = pl.BlockSpec(memory_space=pltpu.SMEM)
LIMIT = pltpu.CompilerParams(vmem_limit_bytes=40 << 20)


def cost(flops, nbytes):
    return pl.CostEstimate(flops=flops, bytes_accessed=nbytes, transcendentals=0)


def spread(x, grid):
    return lax.all_to_all(x, AXES, split_axis=0, concat_axis=0, tiled=True)


def answer_kernel(grid, cap, asked_ref, book_ref, codes_ref, out_ref):
    devices = grid.total
    slots = devices * cap
    entries = book_ref.shape[0]
    asked = jnp.broadcast_to(asked_ref[...][:, None, :], (devices, cap, cap)).reshape(slots, cap)
    place = lax.broadcasted_iota(jnp.int32, (slots, cap), 0) % cap
    lane = lax.broadcasted_iota(jnp.int32, (slots, cap), 1)
    column = jnp.sum(jnp.where(lane == place, asked, 0), axis=1, keepdims=True)
    hit = column == lax.broadcasted_iota(jnp.int32, (slots, entries), 1)
    select = hit.astype(jnp.float32).astype(jnp.bfloat16)
    codes = jnp.dot(select, codes_ref[...], preferred_element_type=jnp.float32)
    rows = jnp.dot(select, book_ref[...], preferred_element_type=jnp.float32)
    feat = rows.shape[1]
    thirds = feat // 256
    rows = rows.reshape(devices, cap, feat)
    block = lax.broadcasted_iota(jnp.int32, (cap, 128), 1) // 32
    turned = {}
    for v in range(2):
        part = codes[:, v * 128 : (v + 1) * 128]
        for s in range(4):
            moved = part if s == 0 else pltpu.roll(part, s * 32, 1)
            turned[v, s] = moved.reshape(devices, cap, 128)
    for r in range(grid.planes):
        for i in range(8):
            dest = grid.linear(r, i)
            v, a = i // 4, i % 4
            halves = []
            for h in range(2):
                value = turned[v, (0 - a) % 4][grid.linear(r, 4 * h)]
                for b in range(1, 4):
                    other = turned[v, (b - a) % 4][grid.linear(r, 4 * h + b)]
                    value = jnp.where(block == b, other, value)
                halves.append(value)
            own = [jnp.concatenate(halves, axis=1)]
            own += [rows[dest][:, t * 256 : (t + 1) * 256] for t in range(thirds)]
            out_ref[dest] = jnp.concatenate(own, axis=0).astype(jnp.bfloat16)


def answer(grid, asked, book, codes):
    devices, cap = asked.shape
    feat = book.shape[1]
    height = cap * (1 + feat // 256)
    return pl.pallas_call(
        functools.partial(answer_kernel, grid, cap),
        out_shape=jax.ShapeDtypeStruct((devices, height, 256), jnp.bfloat16),
        in_specs=vmem(3),
        out_specs=vmem(1)[0],
        compiler_params=LIMIT,
        cost_estimate=cost(2 * devices * cap * book.shape[0] * (feat + 256), 3 << 20),
    )(asked, book, codes)


def weights_kernel(grid, cap, place_ref, got_ref, slot_ref, *refs):
    cots, (own_ref, *send_refs), (acc_ref, xt_ref) = refs[:10], refs[10:-2], refs[-2:]
    devices = grid.total
    slots = devices * cap
    zch = got_ref.shape[2]
    wide = zch // 8
    tokens, channels = cots[0].shape
    i, part = place_ref[0], place_ref[1]
    slices = got_ref[...].astype(jnp.float32)[:, :cap].reshape(slots, zch)
    xt_ref[...] = slices.T
    token = lax.broadcasted_iota(jnp.int32, (1, tokens), 1)
    line, cell = token // 16 % 16, token % 16
    slot_id = lax.broadcasted_iota(jnp.int32, (slots, tokens), 0)
    ones = (lax.broadcasted_iota(jnp.int32, (16, tokens), 0) == 0).astype(jnp.float32)
    whole = {0: cots[0], 2: cots[1], 4: cots[2], 1: cots[5], 3: cots[6], 5: cots[7]}
    for j in range(8):
        member = i ^ j
        xt = xt_ref[pl.ds(pl.multiple_of(member * wide, wide), wide), :].astype(jnp.bfloat16)
        hit = (slot_id == slot_ref[j : j + 1, :]).astype(jnp.float32).astype(jnp.bfloat16)
        quant = jnp.dot(xt, hit, preferred_element_type=jnp.float32)
        taps = []
        for down in (-1, 0, 1):
            for right in (-1, 0, 1):
                shift = (-(down * 16 + right)) % tokens
                moved = quant if shift == 0 else pltpu.roll(quant, shift, 1)
                valid = (line + down >= 0) & (line + down < 16) & (cell + right >= 0) & (cell + right < 16)
                taps.append(moved * valid.astype(jnp.float32))
        left = jnp.concatenate(taps + [ones], axis=0).astype(jnp.bfloat16)
        if j in whole:
            value = jnp.dot(left, whole[j][...], preferred_element_type=jnp.float32)
        else:
            top, bottom = (cots[3], cots[4]) if j == 6 else (cots[8], cots[9])
            cut = tokens // 2
            value = jnp.dot(left[:, :cut], top[...], preferred_element_type=jnp.float32)
            value += jnp.dot(left[:, cut:], bottom[...], preferred_element_type=jnp.float32)
        if j == 0:
            acc_ref[...] = value
        else:
            acc_ref[...] += value
    krows = 9 * wide
    piece = channels // PARTS
    own_ref[...] = acc_ref[:, pl.ds(pl.multiple_of(part * piece, piece), piece)]
    row = lax.broadcasted_iota(jnp.int32, (16, piece), 0)
    for k, send_ref in enumerate(send_refs, 1):
        other = (part + k) % PARTS
        value = acc_ref[:, pl.ds(pl.multiple_of(other * piece, piece), piece)]
        upper = value.astype(jnp.bfloat16).astype(jnp.float32)
        lower = (value - upper)[krows : krows + 1]
        send_ref[:krows] = value[:krows].astype(jnp.bfloat16)
        last = jnp.where(row == 1, lower, value[krows:])
        send_ref[krows:] = last.astype(jnp.bfloat16)


def group_weights(grid, place, got, slot, cots, cap):
    zch, channels = got.shape[2], cots[0].shape[1]
    height = 9 * zch // 8 + 16
    piece = channels // PARTS
    slots = grid.total * cap
    return pl.pallas_call(
        functools.partial(weights_kernel, grid, cap),
        out_shape=[jax.ShapeDtypeStruct((height, piece), jnp.float32)]
        + [jax.ShapeDtypeStruct((height, piece), jnp.bfloat16)] * (PARTS - 1),
        in_specs=[SMEM_SPEC] + vmem(12),
        out_specs=vmem(PARTS),
        scratch_shapes=[
            pltpu.VMEM((height, channels), jnp.float32),
            pltpu.VMEM((zch, slots), jnp.float32),
        ],
        compiler_params=LIMIT,
        cost_estimate=cost(2 * 9 * zch * 512 * channels, 8 << 20),
    )(place, got, slot, *cots)


def own_kernel(grid, cap, got_ref, projector_ref, sums_ref, uses_ref, codes_ref, parts_ref):
    slots = grid.total * cap
    feat, zch = projector_ref.shape
    thirds = feat // 256
    got = got_ref[...].astype(jnp.float32)
    rows = []
    codes = jnp.zeros((slots, zch), jnp.float32)
    for t in range(thirds):
        rows.append(got[:, cap * (t + 1) : cap * (t + 2)].reshape(slots, 256).astype(jnp.bfloat16))
        codes += jnp.dot(
            rows[t], projector_ref[t * 256 : (t + 1) * 256], preferred_element_type=jnp.float32
        )
    codes = codes.astype(jnp.bfloat16)
    codes_ref[...] = codes
    grads = 2.0 * (uses_ref[...] * codes.astype(jnp.float32) - sums_ref[...])
    upper = grads.astype(jnp.bfloat16)
    lower = (grads - upper.astype(jnp.float32)).astype(jnp.bfloat16)
    dims = (((0,), (0,)), ((), ()))
    total = []
    for t in range(thirds):
        value = lax.dot_general(rows[t], upper, dims, preferred_element_type=jnp.float32)
        value += lax.dot_general(rows[t], lower, dims, preferred_element_type=jnp.float32)
        total.append(value.astype(jnp.bfloat16))
    total = jnp.concatenate(total, axis=0)
    prows, wide = feat // 16, zch // 2
    for r in range(grid.planes):
        for i in range(8):
            row, col = proj_place(i, r % PARTS, prows)
            parts_ref[grid.linear(r, i)] = total[row : row + prows, col * wide : (col + 1) * wide]


def proj_place(i, q, prows):
    return (((i // 2) % 2) * 2 + i // 4) * PARTS * prows + q * prows, i % 2


def own_part(grid, got, projector, sums, uses, cap):
    feat, zch = projector.shape
    slots = grid.total * cap
    return pl.pallas_call(
        functools.partial(own_kernel, grid, cap),
        out_shape=(
            jax.ShapeDtypeStruct((slots, zch), jnp.bfloat16),
            jax.ShapeDtypeStruct((grid.total, feat // 16, zch // 2), jnp.bfloat16),
        ),
        in_specs=vmem(4),
        out_specs=tuple(vmem(2)),
        compiler_params=LIMIT,
        cost_estimate=cost(6 * slots * feat * zch, 3 << 20),
    )(got, projector, sums, uses)


def combine_kernel(krows, own_ref, proj_ref, *refs):
    got_refs, out_ref = refs[:-1], refs[-1]
    total = own_ref[...]
    for ref in got_refs:
        total = total + ref[...].astype(jnp.float32)
    kernel = total[:krows]
    proj = jnp.sum(proj_ref[...].astype(jnp.float32), axis=0)
    bias = total[krows : krows + 1] + total[krows + 1 : krows + 2]
    row = lax.broadcasted_iota(jnp.int32, (16, own_ref.shape[1]), 0)
    extra = jnp.zeros(row.shape, jnp.float32)
    sums = (
        bias,
        jnp.sum(kernel * kernel, axis=0, keepdims=True),
        jnp.sum(proj * proj, axis=0, keepdims=True),
    )
    for n, value in enumerate(sums):
        upper = value.astype(jnp.bfloat16).astype(jnp.float32)
        middle = (value - upper).astype(jnp.bfloat16).astype(jnp.float32)
        for k, piece in enumerate((upper, middle, value - upper - middle)):
            extra = jnp.where(row == 3 * n + k, piece, extra)
    out_ref[:krows] = kernel.astype(jnp.bfloat16)
    out_ref[krows : krows + 16] = extra.astype(jnp.bfloat16)
    out_ref[krows + 16 :] = proj.astype(jnp.bfloat16)


def combine(krows, own, got, proj):
    height = own.shape[0] + proj.shape[1]
    return pl.pallas_call(
        functools.partial(combine_kernel, krows),
        out_shape=jax.ShapeDtypeStruct((height, own.shape[1]), jnp.bfloat16),
        in_specs=vmem(2 + len(got)),
        out_specs=vmem(1)[0],
        compiler_params=LIMIT,
    )(own, proj, *got)


def reduce_planes(grid, own, sends, r):
    got = [send(s, grid.turn(k)) for k, s in enumerate(sends, 1)]
    groups = grid.planes // PARTS
    if groups > 1:
        own = own + sum(g.astype(jnp.float32) for g in got)
        rest = [own] + [send(own, grid.far(k)) for k in range(1, groups)]
        order = (r // PARTS - jnp.arange(groups)) % groups
        own = jnp.sum(jnp.take(jnp.stack(rest), order, axis=0), axis=0)
        got = []
    return own, got


def finish_kernel(krows, counts, place_ref, mine_ref, other_ref, kernel_ref, proj_ref, bias_ref, keep_ref):
    i, part = place_ref[0], place_ref[1]
    wide = krows // 9
    prows = mine_ref.shape[1] - krows - 16
    sources = []
    for ref, core in ((mine_ref, 0), (other_ref, 1)):
        for n in range(16):
            place = i ^ (n // 4 * 2 + core)
            q = (part + PARTS - n % 4) % PARTS
            sources.append((ref, n, place, q))
            keep_ref[place * PARTS + q] = ref[n, krows : krows + 16].astype(jnp.float32)
    kept = jnp.sum(keep_ref[...], axis=0)

    def factor(values, count):
        total = jnp.sum(jnp.sum(values, axis=0, keepdims=True), axis=1, keepdims=True)
        return 1.0 / jnp.sqrt(total / count + norm_eps)

    kfactor, pfactor = factor(kept[3:6], counts[0]), factor(kept[6:9], counts[1])
    for ref, n, place, q in sources:
        value = ref[n].astype(jnp.float32)
        lanes = pl.ds(pl.multiple_of(q * 128, 128), 128)
        kernel_ref[:, pl.ds(pl.multiple_of(place * wide, wide), wide), lanes] = (
            value[:krows] * kfactor
        ).reshape(9, wide, 128)
        row, col = proj_place(place, q, prows)
        proj_ref[pl.ds(pl.multiple_of(row, 8), prows), pl.ds(pl.multiple_of(col * 128, 128), 128)] = (
            value[krows + 16 :] * pfactor
        )
    bias = [jnp.sum(keep_ref[q, 0:3], axis=0, keepdims=True) for q in range(PARTS)]
    bias = jnp.concatenate(bias, axis=1)
    bias_ref[...] = bias * factor(bias * bias, counts[2])


def finish(place, mine, other, zch, channels, feat):
    krows = 9 * zch // 8
    counts = (9 * zch * channels, feat * zch, channels)
    return pl.pallas_call(
        functools.partial(finish_kernel, krows, counts),
        out_shape=(
            jax.ShapeDtypeStruct((9, zch, channels), jnp.float32),
            jax.ShapeDtypeStruct((feat, zch), jnp.float32),
            jax.ShapeDtypeStruct((1, channels), jnp.float32),
        ),
        in_specs=[SMEM_SPEC] + vmem(2),
        out_specs=tuple(vmem(3)),
        scratch_shapes=[pltpu.VMEM((32, 16, 128), jnp.float32)],
        compiler_params=LIMIT,
    )(place, mine, other)


def gather_group(grid, own):
    col, row = send(own, grid.flip(2)), send(own, grid.flip(4))
    cut = own.shape[0] // 2
    first, second = send(col[:cut], grid.flip(4)), send(row[cut:], grid.flip(2))
    mine = [own, col, row, first, second]
    return mine + [send(x, grid.flip(1)) for x in mine]


def on_device(
    grid, codebook, projector, latents, wanted, wanted_count, token_pick, kernel, bias, cotangent
):
    devices = grid.total
    images, rows, width, zch = latents.shape
    channels = kernel.shape[3]
    feat = codebook.shape[1]
    cap = wanted.shape[2]
    slots = devices * cap
    tokens = images * rows * width
    r, i = grid.place()
    place = jnp.stack([i, r % PARTS]).astype(jnp.int32)
    asked = spread(wanted.reshape(devices, cap), grid).reshape(devices, cap)
    cots = gather_group(grid, cotangent.reshape(tokens, channels))
    counts = wanted_count.reshape(devices)
    pick = token_pick.reshape(tokens)
    owner = pick // cap
    owner_hit = owner[:, None] == jnp.arange(devices, dtype=jnp.int32)[None, :]
    count = jnp.sum(jnp.where(owner_hit, counts[None, :], 0), axis=1)
    slot = owner * cap + pick % cap % count
    group_slot = slot.reshape(1, tokens)
    for bit in (1, 2, 4):
        group_slot = jnp.concatenate([group_slot, send(group_slot, grid.flip(bit))])
    local_codes = jnp.dot(codebook, projector, preferred_element_type=jnp.float32).astype(
        jnp.bfloat16
    )
    slot_ids = jnp.arange(slots, dtype=jnp.int32)
    onehot = (slot[:, None] == slot_ids[None, :]).astype(jnp.bfloat16)
    sums = lax.dot_general(
        onehot,
        latents.reshape(tokens, zch),
        (((0,), (0,)), ((), ())),
        preferred_element_type=jnp.float32,
    )
    uses = jnp.sum((slot_ids[:, None] == slot[None, :]).astype(jnp.float32), axis=1, keepdims=True)
    got = spread(answer(grid, asked, codebook, local_codes), grid)
    own, *sends = group_weights(grid, place, got, group_slot, cots, cap)
    codes, parts = own_part(grid, got, projector, sums, uses, cap)
    own, received = reduce_planes(grid, own, sends, r)
    parts = spread(parts, grid)
    krows = 9 * zch // 8
    mine, other = all_gather(grid, combine(krows, own, received, parts))
    kernel_step, proj_step, bias_step = finish(place, mine, other, zch, channels, feat)

    quant = jnp.dot(onehot, codes, preferred_element_type=jnp.float32).astype(jnp.bfloat16)
    quant = quant.reshape(images, rows, width, zch)
    quant_f = quant.astype(jnp.float32)
    latent_f = latents.astype(jnp.float32)
    padded = jnp.pad(quant, ((0, 0), (1, 1), (1, 1), (0, 0)))
    padded_grad = jnp.pad(cotangent, ((0, 0), (1, 1), (1, 1), (0, 0)))
    output = jnp.zeros((images, rows, width, channels), jnp.float32)
    grad_input = jnp.zeros((images, rows, width, zch), jnp.float32)
    for row_off in range(3):
        for col_off in range(3):
            window = padded[:, row_off : row_off + rows, col_off : col_off + width]
            output = output + jnp.einsum(
                "nhwc,co->nhwo",
                window,
                kernel[row_off, col_off],
                preferred_element_type=jnp.float32,
            )
            grad_window = padded_grad[
                :, 2 - row_off : 2 - row_off + rows, 2 - col_off : 2 - col_off + width
            ]
            grad_input = grad_input + jnp.einsum(
                "nhwo,co->nhwc",
                grad_window,
                kernel[row_off, col_off],
                preferred_element_type=jnp.float32,
            )
    hidden = (output + bias.astype(jnp.float32)).astype(jnp.bfloat16)
    grad_latents = (grad_input + 2.0 * commit_weight * (latent_f - quant_f)).astype(jnp.bfloat16)
    kernel_step = kernel_step.reshape(3, 3, zch, channels)
    return (hidden, grad_latents, proj_step, kernel_step, bias_step.reshape(channels))


def solution(mesh):
    grid = Grid(mesh.shape["dp"], mesh.shape["code"])
    in_specs = (
        P(("dp", "code"), None),
        P(),
        P(("dp", "code"), None, None, None),
        P(("dp", "code"), None, None),
        P(("dp", "code"), None),
        P(("dp", "code"), None, None),
        P(),
        P(),
        P(("dp", "code"), None, None, None),
    )
    out_specs = (
        P(("dp", "code"), None, None, None),
        P(("dp", "code"), None, None, None),
        P(),
        P(),
        P(),
    )
    return jax.shard_map(
        functools.partial(on_device, grid),
        mesh=mesh,
        in_specs=in_specs,
        out_specs=out_specs,
        check_vma=False,
    )
```

```python
import functools

import jax
import jax.numpy as jnp
from jax import lax
from jax.experimental import pallas as pl
from jax.experimental.pallas import tpu as pltpu
from jax.sharding import PartitionSpec as P

commit_weight = 0.25
norm_eps = 1e-06
AXES = ("dp", "code")
PARTS = 4


class Grid:
    def __init__(self, n_dp, n_code):
        self.n_dp, self.n_code = n_dp, n_code
        self.outer = n_code // 4
        self.planes = (n_dp // 2) * self.outer
        self.total = n_dp * n_code

    def linear(self, r, i):
        dh, ch = r // self.outer, r % self.outer
        return (dh * 2 + i // 4) * self.n_code + ch * 4 + i % 4

    def perm(self, move):
        return [
            (self.linear(r, i), self.linear(*move(r, i)))
            for r in range(self.planes)
            for i in range(8)
        ]

    def flip(self, bit):
        return self.perm(lambda r, i: (r, i ^ bit))

    def turn(self, k):
        return self.perm(lambda r, i: (r // PARTS * PARTS + (r + k) % PARTS, i))

    def far(self, k):
        groups = self.planes // PARTS
        return self.perm(lambda r, i: ((r // PARTS + k) % groups * PARTS + r % PARTS, i))

    def order(self, x):
        rest = x.shape[2:]
        x = x.reshape(self.n_dp // 2, self.outer, 2, 4, *rest)
        return jnp.swapaxes(x, 1, 2).reshape(self.total, *rest)

    def place(self):
        dp, code = lax.axis_index("dp"), lax.axis_index("code")
        return (dp // 2) * self.outer + code // 4, (dp % 2) * 4 + code % 4


def send(x, perm):
    return lax.ppermute(x, AXES, perm)


def gather_planes(grid, own):
    zs = [send(own, grid.turn(k)) for k in range(1, PARTS)]
    x, y = send(own, grid.flip(2)), send(own, grid.flip(4))
    early = jnp.stack([own, x, y, send(x, grid.flip(4))])
    zs = jnp.stack(zs)
    return early, zs, send(zs, grid.flip(2)), send(zs, grid.flip(4))


def gather_places(grid, early, zs, xs, ys):
    second, first = send(ys[:2], grid.flip(2)), send(xs[2:], grid.flip(4))
    mine = [early, jnp.concatenate([zs, xs, ys]), jnp.concatenate([second, first])]
    return mine + [send(x, grid.flip(1)) for x in mine]


def vmem(count):
    return [pl.BlockSpec(memory_space=pltpu.VMEM)] * count


SMEM_SPEC = pl.BlockSpec(memory_space=pltpu.SMEM)
LIMIT = pltpu.CompilerParams(vmem_limit_bytes=40 << 20)


def cost(flops, nbytes):
    return pl.CostEstimate(flops=flops, bytes_accessed=nbytes, transcendentals=0)


def spread(x, grid):
    return lax.all_to_all(x, AXES, split_axis=0, concat_axis=0, tiled=True)


def token_kernel(
    cap, place_ref, pick_hbm, counts_hbm, wanted_hbm, latents_hbm, cot_hbm, near_ref, far_ref, slot_ref, ask_ref, *rest
):
    pick_ref, counts_ref, wanted_ref, latents_ref, cot_ref, sems = rest
    sources = (pick_hbm, counts_hbm, wanted_hbm, latents_hbm, cot_hbm)
    copies = [
        pltpu.make_async_copy(source, target, sems.at[n])
        for n, (source, target) in enumerate(zip(sources, rest[:-1]))
    ]
    for copy in copies:
        copy.start()
    for copy in copies[:4]:
        copy.wait()
    lines, width = pick_ref.shape
    devices = counts_ref.shape[1]
    tokens = lines * width
    pick = pick_ref[...]
    owner = pick // cap
    first = pick - owner * cap
    token = lax.broadcasted_iota(jnp.int32, (width, tokens), 1)
    wide = (token % width == lax.broadcasted_iota(jnp.int32, (width, tokens), 0)).astype(jnp.float32)
    wide = wide.astype(jnp.bfloat16)
    token = lax.broadcasted_iota(jnp.int32, (lines, tokens), 1)
    keep = token // width == lax.broadcasted_iota(jnp.int32, (lines, tokens), 0)

    def flat(x):
        x = x.astype(jnp.float32).astype(jnp.bfloat16)
        x = jnp.dot(x, wide, preferred_element_type=jnp.float32)
        return jnp.sum(jnp.where(keep, x, 0.0), axis=0, keepdims=True)

    owner, entry = flat(owner), flat(first)
    row = lax.broadcasted_iota(jnp.int32, (devices, devices), 0)
    col = lax.broadcasted_iota(jnp.int32, (devices, devices), 1)
    counts = jnp.where(row == col, counts_ref[...].astype(jnp.float32), 0.0)
    counts = jnp.sum(counts, axis=1, keepdims=True)
    owner_id = lax.broadcasted_iota(jnp.int32, (devices, tokens), 0)
    count = jnp.sum(
        jnp.where(owner_id == owner.astype(jnp.int32), counts, 0.0), axis=0, keepdims=True
    )
    for _ in range(cap - 1):
        entry = jnp.where(entry >= count, entry - count, entry)
    slot = (owner * cap + entry).astype(jnp.int32)
    slot_ref[...] = slot
    place = lax.broadcasted_iota(jnp.int32, (16, tokens), 0)
    wide = cot_ref.shape[1] // 2
    place = place[:, :wide]
    extra = jnp.zeros((16, wide), jnp.float32)
    for n, row in enumerate((owner[:, :wide], owner[:, wide:], entry[:, :wide], entry[:, wide:])):
        extra = jnp.where(place == n, row, extra)
    copies[4].wait()
    for ref, side in ((near_ref, place_ref[0] // 4), (far_ref, 1 - place_ref[0] // 4)):
        ref[:tokens] = cot_ref[:, pl.ds(pl.multiple_of(side * wide, wide), wide)]
        ref[tokens:] = extra.astype(jnp.bfloat16)
    hit = (lax.broadcasted_iota(jnp.int32, (devices * cap, tokens), 0) == slot).astype(jnp.float32)
    slots = devices * cap
    uses = jnp.sum(hit, axis=1, keepdims=True)
    sums = jnp.dot(hit.astype(jnp.bfloat16), latents_ref[...], preferred_element_type=jnp.float32)
    zch = sums.shape[1]
    wanted = wanted_ref[...].astype(jnp.float32).T
    wanted = jnp.broadcast_to(wanted[:, None, :], (devices, cap, cap)).reshape(slots, cap)
    place = lax.broadcasted_iota(jnp.int32, (slots, cap), 0) % cap
    lane = lax.broadcasted_iota(jnp.int32, (slots, cap), 1)
    wanted = jnp.sum(jnp.where(lane == place, wanted, 0.0), axis=1, keepdims=True)
    lane = lax.broadcasted_iota(jnp.int32, (slots, 128), 1)
    last = jnp.where(lane == 0, uses, jnp.where(lane == 1, wanted, 0.0))
    ask_ref[:, :, :zch] = sums.reshape(devices, cap, zch)
    ask_ref[:, :, zch:] = last.reshape(devices, cap, 128)


def token_part(place, pick, counts, wanted, latents, cots):
    tokens, channels = cots.shape
    cap, devices = wanted.shape
    slots = devices * cap
    return pl.pallas_call(
        functools.partial(token_kernel, cap),
        out_shape=(
            jax.ShapeDtypeStruct((tokens + 16, channels // 2), jnp.bfloat16),
            jax.ShapeDtypeStruct((tokens + 16, channels // 2), jnp.bfloat16),
            jax.ShapeDtypeStruct((1, tokens), jnp.int32),
            jax.ShapeDtypeStruct((devices, cap, latents.shape[1] + 128), jnp.float32),
        ),
        in_specs=[SMEM_SPEC] + [pl.BlockSpec(memory_space=pltpu.HBM)] * 5,
        out_specs=tuple(vmem(4)),
        scratch_shapes=[
            pltpu.VMEM(x.shape, x.dtype) for x in (pick, counts, wanted, latents, cots)
        ]
        + [pltpu.SemaphoreType.DMA((5,))],
        compiler_params=pltpu.CompilerParams(vmem_limit_bytes=62 << 20),
        cost_estimate=cost(2 * slots * tokens * latents.shape[1], 2 << 20),
    )(place, pick, counts, wanted, latents, cots)


def select_rows(asked, zch, entries):
    column = asked[:, zch + 1 : zch + 2].astype(jnp.int32)
    hit = column == lax.broadcasted_iota(jnp.int32, (asked.shape[0], entries), 1)
    return hit.astype(jnp.float32).astype(jnp.bfloat16)


def answer_kernel(grid, cap, asked_ref, codes_ref, out_ref):
    devices = grid.total
    entries, zch = codes_ref.shape
    select = select_rows(asked_ref[...].reshape(devices * cap, zch + 128), zch, entries)
    codes = jnp.dot(select, codes_ref[...], preferred_element_type=jnp.float32)
    whole = codes.reshape(devices, cap, zch)
    second = lax.broadcasted_iota(jnp.int32, (cap, 128), 1) >= 64
    turned = {}
    for v in range(2):
        part = codes[:, v * 128 : (v + 1) * 128]
        turned[v, 0] = part.reshape(devices, cap, 128)
        turned[v, 1] = pltpu.roll(part, 64, 1).reshape(devices, cap, 128)
    for r in range(grid.planes):
        for u in range(4):
            v, a = u // 2, u % 2
            slices = [
                jnp.where(
                    second,
                    turned[v, 1 - a][grid.linear(r, 2 * h + 1)],
                    turned[v, a][grid.linear(r, 2 * h)],
                )
                for h in range(4)
            ]
            for dest in (grid.linear(r, u), grid.linear(r, u + 4)):
                top = jnp.concatenate(slices[:3], axis=1)
                bottom = jnp.concatenate([slices[3], whole[dest]], axis=1)
                out_ref[dest] = jnp.concatenate([top, bottom], axis=0).astype(jnp.bfloat16)


def answer(grid, asked, codes):
    devices, cap, _ = asked.shape
    zch = codes.shape[1]
    return pl.pallas_call(
        functools.partial(answer_kernel, grid, cap),
        out_shape=jax.ShapeDtypeStruct((devices, 2 * cap, 384), jnp.bfloat16),
        in_specs=vmem(2),
        out_specs=vmem(1)[0],
        compiler_params=LIMIT,
        cost_estimate=cost(2 * devices * cap * codes.shape[0] * zch, 2 << 20),
    )(asked, codes)


def proj_kernel(place_ref, asked_ref, book_ref, codes_ref, keep_ref, send_ref, all_ref):
    entries, feat = book_ref.shape
    zch = codes_ref.shape[1]
    devices, cap, _ = asked_ref.shape
    asked = asked_ref[...].reshape(devices * cap, zch + 128)
    select = select_rows(asked, zch, entries)
    codes = jnp.dot(select, codes_ref[...], preferred_element_type=jnp.float32)
    rows = jnp.dot(select, book_ref[...], preferred_element_type=jnp.float32).astype(jnp.bfloat16)
    grads = 2.0 * (asked[:, zch : zch + 1] * codes - asked[:, :zch])
    upper = grads.astype(jnp.bfloat16)
    lower = (grads - upper.astype(jnp.float32)).astype(jnp.bfloat16)
    dims = (((0,), (0,)), ((), ()))
    total = lax.dot_general(rows, upper, dims, preferred_element_type=jnp.float32)
    all_ref[...] = total + lax.dot_general(rows, lower, dims, preferred_element_type=jnp.float32)
    core = place_ref[0] % 2
    keep_ref[...] = all_ref[:, pl.ds(pl.multiple_of(core * 128, 128), 128)]
    send_ref[...] = all_ref[:, pl.ds(pl.multiple_of((1 - core) * 128, 128), 128)]


def proj_part(place, asked, book, codes):
    feat, zch = book.shape[1], codes.shape[1]
    slots = asked.shape[0] * asked.shape[1]
    return pl.pallas_call(
        proj_kernel,
        out_shape=(jax.ShapeDtypeStruct((feat, 128), jnp.float32),) * 2,
        in_specs=[SMEM_SPEC] + vmem(3),
        out_specs=tuple(vmem(2)),
        scratch_shapes=[pltpu.VMEM((feat, zch), jnp.float32)],
        compiler_params=LIMIT,
        cost_estimate=cost(2 * slots * (book.shape[0] + 2 * zch) * feat, 4 << 20),
    )(place, asked, book, codes)


def half(x, axis, index):
    return lax.dynamic_index_in_dim(x, index, axis, keepdims=False)


def exchange(x, own, perm):
    sent = half(x, 0, 1 - own).astype(jnp.bfloat16)
    return half(x, 0, own) + send(sent, perm).astype(jnp.float32)


def proj_place(i, q, prows):
    return (((i // 2) % 2) * 2 + i // 4) * PARTS * prows + q * prows, i % 2


def weights_kernel(grid, cap, place_ref, got_ref, *refs):
    cots, (acc_ref, xt_ref) = refs[:8], refs[8:]
    devices = grid.total
    slots = devices * cap
    tokens, channels = cots[0].shape
    tokens -= 16
    cut = tokens // 2
    i, part = place_ref[0], place_ref[1]
    got = got_ref[...].astype(jnp.float32)
    xt_ref[:384] = got[:, :cap].reshape(slots, 384).T
    xt_ref[384:] = got[:, cap:, :128].reshape(slots, 128).T
    wide = 64
    krows = 9 * wide // 2
    token = lax.broadcasted_iota(jnp.int32, (1, tokens), 1)
    line, cell = token // 16 % 16, token % 16
    slot_id = lax.broadcasted_iota(jnp.int32, (slots, tokens), 0)
    ones = (lax.broadcasted_iota(jnp.int32, (16, tokens), 0) == 0).astype(jnp.float32)
    cots = {j: cots[j % 2 * 4 + j // 2] for j in range(8)}
    for j in range(8):
        member = i ^ j
        xt = xt_ref[pl.ds(pl.multiple_of(member * wide, wide), wide), :].astype(jnp.bfloat16)
        last = cots[j][tokens:].astype(jnp.float32)
        last = last[0:2] * cap + last[2:4]
        slot = jnp.concatenate([last[0:1], last[1:2]], axis=1).astype(jnp.int32)
        hit = (slot_id == slot).astype(jnp.float32).astype(jnp.bfloat16)
        quant = jnp.dot(xt, hit, preferred_element_type=jnp.float32)
        taps = []
        for down in (-1, 0, 1):
            for right in (-1, 0, 1):
                shift = (-(down * 16 + right)) % tokens
                moved = quant if shift == 0 else pltpu.roll(quant, shift, 1)
                valid = (line + down >= 0) & (line + down < 16) & (cell + right >= 0) & (cell + right < 16)
                taps.append(moved * valid.astype(jnp.float32))
        taps = [x[: wide // 2] for x in taps] + [x[wide // 2 :] for x in taps]
        left = jnp.concatenate(taps + [ones], axis=0).astype(jnp.bfloat16)
        value = jnp.dot(left, cots[j][:tokens], preferred_element_type=jnp.float32)
        if j == 0:
            acc_ref[...] = value
        else:
            acc_ref[...] += value


def pack_kernel(krows, place_ref, acc_ref, proj_ref, own_ref, *send_refs):
    part = place_ref[1]

    def piece(q):
        lanes = pl.ds(pl.multiple_of(q % 2 * 128, 128), 128)
        rows = pl.ds(pl.multiple_of(q // 2 * krows, 8), krows)
        return acc_ref[rows, lanes], acc_ref[2 * krows :, lanes]

    own_ref[:krows], own_ref[krows : krows + 16] = piece(part)
    own_ref[krows + 16 :] = proj_ref[part]
    row = lax.broadcasted_iota(jnp.int32, (16, 128), 0)
    for k, send_ref in enumerate(send_refs, 1):
        value, last = piece((part + k) % PARTS)
        upper = last.astype(jnp.bfloat16).astype(jnp.float32)
        lower = (last - upper)[0:1]
        send_ref[:krows] = value.astype(jnp.bfloat16)
        send_ref[krows : krows + 16] = jnp.where(row == 1, lower, last).astype(jnp.bfloat16)
        send_ref[krows + 16 :] = proj_ref[(part + k) % PARTS].astype(jnp.bfloat16)


def group_weights(grid, place, got, cots, cap):
    channels = cots[0].shape[1]
    slots = grid.total * cap
    return pl.pallas_call(
        functools.partial(weights_kernel, grid, cap),
        out_shape=jax.ShapeDtypeStruct((9 * 64 + 16, channels), jnp.float32),
        in_specs=[SMEM_SPEC] + vmem(9),
        out_specs=vmem(1)[0],
        scratch_shapes=[pltpu.VMEM((512, slots), jnp.float32)],
        compiler_params=LIMIT,
        cost_estimate=cost(2 * 9 * 512 * 512 * channels, 8 << 20),
    )(place, got, *cots)


def pack(place, acc, proj):
    krows = (acc.shape[0] - 16) // 2
    height = krows + 16 + proj.shape[1]
    return pl.pallas_call(
        functools.partial(pack_kernel, krows),
        out_shape=[jax.ShapeDtypeStruct((height, 128), jnp.float32)]
        + [jax.ShapeDtypeStruct((height, 128), jnp.bfloat16)] * (PARTS - 1),
        in_specs=[SMEM_SPEC] + vmem(2),
        out_specs=vmem(PARTS),
        compiler_params=LIMIT,
    )(place, acc, proj)


def combine_kernel(krows, own_ref, *refs):
    got_refs, out_ref = refs[:-1], refs[-1]
    total = own_ref[...]
    for ref in got_refs:
        total = total + ref[...].astype(jnp.float32)
    kernel = total[:krows]
    proj = total[krows + 16 :]
    bias = total[krows : krows + 1] + total[krows + 1 : krows + 2]
    row = lax.broadcasted_iota(jnp.int32, (16, own_ref.shape[1]), 0)
    extra = jnp.zeros(row.shape, jnp.float32)
    sums = (
        bias,
        jnp.sum(kernel * kernel, axis=0, keepdims=True),
        jnp.sum(proj * proj, axis=0, keepdims=True),
    )
    for n, value in enumerate(sums):
        upper = value.astype(jnp.bfloat16).astype(jnp.float32)
        middle = (value - upper).astype(jnp.bfloat16).astype(jnp.float32)
        for k, piece in enumerate((upper, middle, value - upper - middle)):
            extra = jnp.where(row == 3 * n + k, piece, extra)
    out_ref[:krows] = kernel.astype(jnp.bfloat16)
    out_ref[krows : krows + 16] = extra.astype(jnp.bfloat16)
    out_ref[krows + 16 :] = proj.astype(jnp.bfloat16)


def combine(krows, own, got):
    return pl.pallas_call(
        functools.partial(combine_kernel, krows),
        out_shape=jax.ShapeDtypeStruct(own.shape, jnp.bfloat16),
        in_specs=vmem(1 + len(got)),
        out_specs=vmem(1)[0],
        compiler_params=LIMIT,
    )(own, *got)


def reduce_planes(grid, own, sends, r):
    got = [send(s, grid.turn(k)) for k, s in enumerate(sends, 1)]
    groups = grid.planes // PARTS
    if groups > 1:
        own = own + sum(g.astype(jnp.float32) for g in got)
        rest = [own] + [send(own, grid.far(k)) for k in range(1, groups)]
        order = (r // PARTS - jnp.arange(groups)) % groups
        own = jnp.sum(jnp.take(jnp.stack(rest), order, axis=0), axis=0)
        got = []
    return own, got


def finish_kernel(krows, counts, place_ref, *refs):
    (kernel_ref, proj_ref, bias_ref, keep_ref), refs = refs[6:], refs[:6]
    i, part = place_ref[0], place_ref[1]
    wide = krows // 9
    prows = refs[0].shape[1] - krows - 16
    sources = []
    near = [(n, 2 * n, 0) for n in range(4)]
    middle = [(n, n // 3 * 2, n % 3 + 1) for n in range(9)]
    last = [(n, 6, n + 1) for n in range(3)]
    for m, ref in enumerate(refs):
        for n, bits, turn in (near, middle, last)[m % 3]:
            place = i ^ (bits + m // 3)
            q = (part + PARTS - turn) % PARTS
            sources.append((ref, n, place, q))
            keep_ref[place * PARTS + q] = ref[n, krows : krows + 16].astype(jnp.float32)
    kept = jnp.sum(keep_ref[...], axis=0)

    def factor(values, count):
        total = jnp.sum(jnp.sum(values, axis=0, keepdims=True), axis=1, keepdims=True)
        return 1.0 / jnp.sqrt(total / count + norm_eps)

    kfactor, pfactor = factor(kept[3:6], counts[0]), factor(kept[6:9], counts[1])
    for ref, n, place, q in sources:
        value = ref[n].astype(jnp.float32)
        lanes = pl.ds(pl.multiple_of(place // 4 * 256 + q % 2 * 128, 128), 128)
        start = place % 4 * 64 + q // 2 * 32
        kernel_ref[:, pl.ds(pl.multiple_of(start, 32), wide), lanes] = (
            value[:krows] * kfactor
        ).reshape(9, wide, 128)
        row, col = proj_place(place, q, prows)
        proj_ref[pl.ds(pl.multiple_of(row, 8), prows), pl.ds(pl.multiple_of(col * 128, 128), 128)] = (
            value[krows + 16 :] * pfactor
        )
    bias = [jnp.sum(keep_ref[n, 0:3], axis=0, keepdims=True) for n in (0, 1, 16, 17)]
    bias = jnp.concatenate(bias, axis=1)
    bias_ref[...] = bias * factor(bias * bias, counts[2])


def finish(place, blocks, zch, channels, feat):
    krows = 9 * zch // 8
    counts = (9 * zch * channels, feat * zch, channels)
    return pl.pallas_call(
        functools.partial(finish_kernel, krows, counts),
        out_shape=(
            jax.ShapeDtypeStruct((9, zch, channels), jnp.float32),
            jax.ShapeDtypeStruct((feat, zch), jnp.float32),
            jax.ShapeDtypeStruct((1, channels), jnp.float32),
        ),
        in_specs=[SMEM_SPEC] + vmem(6),
        out_specs=tuple(vmem(3)),
        scratch_shapes=[pltpu.VMEM((32, 16, 128), jnp.float32)],
        compiler_params=LIMIT,
    )(place, *blocks)


def gather_near(grid, near, far):
    return send(near, grid.flip(2)), send(far, grid.flip(4))


def gather_rest(grid, near, col, row):
    mine = [near, col, row, send(row, grid.flip(2))]
    return mine + [send(x, grid.flip(1)) for x in mine]


def on_device(
    grid, codebook, projector, latents, wanted, wanted_count, token_pick, kernel, bias, cotangent
):
    devices = grid.total
    images, rows, width, zch = latents.shape
    channels = kernel.shape[3]
    feat = codebook.shape[1]
    cap = wanted.shape[2]
    slots = devices * cap
    tokens = images * rows * width
    r, i = grid.place()
    place = jnp.stack([i, r % PARTS]).astype(jnp.int32)
    near, far, slot, ask = token_part(
        place,
        token_pick.reshape(images * rows, width),
        wanted_count,
        jnp.swapaxes(wanted.reshape(devices, cap), 0, 1),
        latents.reshape(tokens, zch),
        cotangent.reshape(tokens, channels),
    )
    asked = spread(ask, grid)
    col, row = gather_near(grid, near, far)
    local_codes = jnp.dot(codebook, projector, preferred_element_type=jnp.float32).astype(
        jnp.bfloat16
    )
    slot_ids = jnp.arange(slots, dtype=jnp.int32)
    onehot = (slot.reshape(tokens, 1) == slot_ids[None, :]).astype(jnp.bfloat16)
    replies = answer(grid, asked, local_codes)
    got = spread(replies, grid)
    asked, col, row, _ = lax.optimization_barrier((asked, col, row, replies))
    cots = gather_rest(grid, near, col, row)
    kept, sent = proj_part(place, asked, codebook, local_codes)
    proj = (kept + send(sent, grid.flip(1))).reshape(2, 2, PARTS, feat // 16, 128)
    cotangent, _ = lax.optimization_barrier((cotangent, replies))
    proj = exchange(proj, i // 2 % 2, grid.flip(2))
    got_half = send(half(proj, 0, 1 - i // 4).astype(jnp.bfloat16), grid.flip(4))
    acc = group_weights(grid, place, got, cots, cap)
    kept, acc = lax.optimization_barrier((half(proj, 0, i // 4), acc))
    own, *sends = pack(place, acc, kept + got_half.astype(jnp.float32))
    codes = got[:, cap:, 128:].reshape(slots, zch)
    codes, own, *sends = lax.optimization_barrier((codes, own, *sends))
    own, received = reduce_planes(grid, own, sends, r)
    quant = jnp.dot(onehot, codes, preferred_element_type=jnp.float32).astype(jnp.bfloat16)
    quant = quant.reshape(images, rows, width, zch)
    quant_f = quant.astype(jnp.float32)
    latent_f = latents.astype(jnp.float32)
    padded = jnp.pad(quant, ((0, 0), (1, 1), (1, 1), (0, 0)))
    padded_grad = jnp.pad(cotangent, ((0, 0), (1, 1), (1, 1), (0, 0)))
    output = jnp.zeros((images, rows, width, channels), jnp.float32)
    grad_input = jnp.zeros((images, rows, width, zch), jnp.float32)
    for row_off in range(3):
        for col_off in range(3):
            window = padded[:, row_off : row_off + rows, col_off : col_off + width]
            output = output + jnp.einsum(
                "nhwc,co->nhwo",
                window,
                kernel[row_off, col_off],
                preferred_element_type=jnp.float32,
            )
            grad_window = padded_grad[
                :, 2 - row_off : 2 - row_off + rows, 2 - col_off : 2 - col_off + width
            ]
            grad_input = grad_input + jnp.einsum(
                "nhwo,co->nhwc",
                grad_window,
                kernel[row_off, col_off],
                preferred_element_type=jnp.float32,
            )
    hidden = (output + bias.astype(jnp.float32)).astype(jnp.bfloat16)
    grad_latents = (grad_input + 2.0 * commit_weight * (latent_f - quant_f)).astype(jnp.bfloat16)
    krows = 9 * zch // 8
    planes = gather_planes(grid, combine(krows, own, received))
    *planes, hidden, grad_latents = lax.optimization_barrier((*planes, hidden, grad_latents))
    blocks = gather_places(grid, *planes)
    kernel_step, proj_step, bias_step = finish(place, blocks, zch, channels, feat)
    kernel_step = kernel_step.reshape(3, 3, zch, channels)
    return (hidden, grad_latents, proj_step, kernel_step, bias_step.reshape(channels))


def solution(mesh):
    grid = Grid(mesh.shape["dp"], mesh.shape["code"])
    in_specs = (
        P(("dp", "code"), None),
        P(),
        P(("dp", "code"), None, None, None),
        P(("dp", "code"), None, None),
        P(("dp", "code"), None),
        P(("dp", "code"), None, None),
        P(),
        P(),
        P(("dp", "code"), None, None, None),
    )
    out_specs = (
        P(("dp", "code"), None, None, None),
        P(("dp", "code"), None, None, None),
        P(),
        P(),
        P(),
    )
    return jax.shard_map(
        functools.partial(on_device, grid),
        mesh=mesh,
        in_specs=in_specs,
        out_specs=out_specs,
        check_vma=False,
    )
```

```python
import functools

import jax
import jax.numpy as jnp
from jax import lax
from jax.experimental import pallas as pl
from jax.experimental.pallas import tpu as pltpu
from jax.sharding import PartitionSpec as P

commit_weight = 0.25
norm_eps = 1e-06
AXES = ("dp", "code")
PARTS = 4


class Grid:
    def __init__(self, n_dp, n_code):
        self.n_dp, self.n_code = n_dp, n_code
        self.outer = n_code // 4
        self.planes = (n_dp // 2) * self.outer
        self.total = n_dp * n_code

    def linear(self, r, i):
        dh, ch = r // self.outer, r % self.outer
        return (dh * 2 + i // 4) * self.n_code + ch * 4 + i % 4

    def perm(self, move):
        return [
            (self.linear(r, i), self.linear(*move(r, i)))
            for r in range(self.planes)
            for i in range(8)
        ]

    def flip(self, bit):
        return self.perm(lambda r, i: (r, i ^ bit))

    def turn(self, k):
        return self.perm(lambda r, i: (r // PARTS * PARTS + (r + k) % PARTS, i))

    def far(self, k):
        groups = self.planes // PARTS
        return self.perm(lambda r, i: ((r // PARTS + k) % groups * PARTS + r % PARTS, i))

    def order(self, x):
        rest = x.shape[2:]
        x = x.reshape(self.n_dp // 2, self.outer, 2, 4, *rest)
        return jnp.swapaxes(x, 1, 2).reshape(self.total, *rest)

    def place(self):
        dp, code = lax.axis_index("dp"), lax.axis_index("code")
        return (dp // 2) * self.outer + code // 4, (dp % 2) * 4 + code % 4


def send(x, perm):
    return lax.ppermute(x, AXES, perm)


def gather_planes(grid, own):
    zs = [send(own, grid.turn(k)) for k in range(1, PARTS)]
    x, y = send(own, grid.flip(2)), send(own, grid.flip(4))
    early = jnp.stack([own, x, y, send(x, grid.flip(4))])
    zs = jnp.stack(zs)
    return early, zs, send(zs, grid.flip(2)), send(zs, grid.flip(4))


def gather_places(grid, early, zs, xs, ys):
    second, first = send(ys[:2], grid.flip(2)), send(xs[2:], grid.flip(4))
    mine = [early, jnp.concatenate([zs, xs, ys]), jnp.concatenate([second, first])]
    return mine + [send(x, grid.flip(1)) for x in mine]


def vmem(count):
    return [pl.BlockSpec(memory_space=pltpu.VMEM)] * count


SMEM_SPEC = pl.BlockSpec(memory_space=pltpu.SMEM)
LIMIT = pltpu.CompilerParams(vmem_limit_bytes=40 << 20)


def cost(flops, nbytes):
    return pl.CostEstimate(flops=flops, bytes_accessed=nbytes, transcendentals=0)


def spread(x, grid):
    return lax.all_to_all(x, AXES, split_axis=0, concat_axis=0, tiled=True)


def token_kernel(
    cap, place_ref, pick_hbm, counts_hbm, wanted_hbm, latents_hbm, cot_hbm, near_ref, far_ref, slot_ref, ask_ref, *rest
):
    pick_ref, counts_ref, wanted_ref, latents_ref, cot_ref, sems = rest
    sources = (pick_hbm, counts_hbm, wanted_hbm, latents_hbm, cot_hbm)
    copies = [
        pltpu.make_async_copy(source, target, sems.at[n])
        for n, (source, target) in enumerate(zip(sources, rest[:-1]))
    ]
    for copy in copies:
        copy.start()
    for copy in copies[:4]:
        copy.wait()
    lines, width = pick_ref.shape
    devices = counts_ref.shape[1]
    tokens = lines * width
    pick = pick_ref[...]
    owner = pick // cap
    first = pick - owner * cap
    token = lax.broadcasted_iota(jnp.int32, (width, tokens), 1)
    wide = (token % width == lax.broadcasted_iota(jnp.int32, (width, tokens), 0)).astype(jnp.float32)
    wide = wide.astype(jnp.bfloat16)
    token = lax.broadcasted_iota(jnp.int32, (lines, tokens), 1)
    keep = token // width == lax.broadcasted_iota(jnp.int32, (lines, tokens), 0)

    def flat(x):
        x = x.astype(jnp.float32).astype(jnp.bfloat16)
        x = jnp.dot(x, wide, preferred_element_type=jnp.float32)
        return jnp.sum(jnp.where(keep, x, 0.0), axis=0, keepdims=True)

    owner, entry = flat(owner), flat(first)
    row = lax.broadcasted_iota(jnp.int32, (devices, devices), 0)
    col = lax.broadcasted_iota(jnp.int32, (devices, devices), 1)
    counts = jnp.where(row == col, counts_ref[...].astype(jnp.float32), 0.0)
    counts = jnp.sum(counts, axis=1, keepdims=True)
    owner_id = lax.broadcasted_iota(jnp.int32, (devices, tokens), 0)
    count = jnp.sum(
        jnp.where(owner_id == owner.astype(jnp.int32), counts, 0.0), axis=0, keepdims=True
    )
    for _ in range(cap - 1):
        entry = jnp.where(entry >= count, entry - count, entry)
    slot = (owner * cap + entry).astype(jnp.int32)
    slot_ref[...] = slot
    place = lax.broadcasted_iota(jnp.int32, (16, tokens), 0)
    wide = cot_ref.shape[1] // 2
    place = place[:, :wide]
    extra = jnp.zeros((16, wide), jnp.float32)
    for n, row in enumerate((owner[:, :wide], owner[:, wide:], entry[:, :wide], entry[:, wide:])):
        extra = jnp.where(place == n, row, extra)
    copies[4].wait()
    for ref, side in ((near_ref, place_ref[0] // 4), (far_ref, 1 - place_ref[0] // 4)):
        ref[:tokens] = cot_ref[:, pl.ds(pl.multiple_of(side * wide, wide), wide)]
        ref[tokens:] = extra.astype(jnp.bfloat16)
    hit = (lax.broadcasted_iota(jnp.int32, (devices * cap, tokens), 0) == slot).astype(jnp.float32)
    slots = devices * cap
    uses = jnp.sum(hit, axis=1, keepdims=True)
    sums = jnp.dot(hit.astype(jnp.bfloat16), latents_ref[...], preferred_element_type=jnp.float32)
    zch = sums.shape[1]
    wanted = wanted_ref[...].astype(jnp.float32).T
    wanted = jnp.broadcast_to(wanted[:, None, :], (devices, cap, cap)).reshape(slots, cap)
    place = lax.broadcasted_iota(jnp.int32, (slots, cap), 0) % cap
    lane = lax.broadcasted_iota(jnp.int32, (slots, cap), 1)
    wanted = jnp.sum(jnp.where(lane == place, wanted, 0.0), axis=1, keepdims=True)
    lane = lax.broadcasted_iota(jnp.int32, (slots, 128), 1)
    last = jnp.where(lane == 0, uses, jnp.where(lane == 1, wanted, 0.0))
    ask_ref[:, :, :zch] = sums.reshape(devices, cap, zch)
    ask_ref[:, :, zch:] = last.reshape(devices, cap, 128)


def token_part(place, pick, counts, wanted, latents, cots):
    tokens, channels = cots.shape
    cap, devices = wanted.shape
    slots = devices * cap
    return pl.pallas_call(
        functools.partial(token_kernel, cap),
        out_shape=(
            jax.ShapeDtypeStruct((tokens + 16, channels // 2), jnp.bfloat16),
            jax.ShapeDtypeStruct((tokens + 16, channels // 2), jnp.bfloat16),
            jax.ShapeDtypeStruct((1, tokens), jnp.int32),
            jax.ShapeDtypeStruct((devices, cap, latents.shape[1] + 128), jnp.float32),
        ),
        in_specs=[SMEM_SPEC] + [pl.BlockSpec(memory_space=pltpu.HBM)] * 5,
        out_specs=tuple(vmem(4)),
        scratch_shapes=[
            pltpu.VMEM(x.shape, x.dtype) for x in (pick, counts, wanted, latents, cots)
        ]
        + [pltpu.SemaphoreType.DMA((5,))],
        compiler_params=pltpu.CompilerParams(vmem_limit_bytes=62 << 20),
        cost_estimate=cost(2 * slots * tokens * latents.shape[1], 2 << 20),
    )(place, pick, counts, wanted, latents, cots)


def select_rows(asked, zch, entries):
    column = asked[:, zch + 1 : zch + 2].astype(jnp.int32)
    hit = column == lax.broadcasted_iota(jnp.int32, (asked.shape[0], entries), 1)
    return hit.astype(jnp.float32).astype(jnp.bfloat16)


def answer_kernel(grid, cap, asked_ref, codes_ref, out_ref):
    devices = grid.total
    entries, zch = codes_ref.shape
    select = select_rows(asked_ref[...].reshape(devices * cap, zch + 128), zch, entries)
    codes = jnp.dot(select, codes_ref[...], preferred_element_type=jnp.float32)
    whole = codes.reshape(devices, cap, zch)
    second = lax.broadcasted_iota(jnp.int32, (cap, 128), 1) >= 64
    turned = {}
    for v in range(2):
        part = codes[:, v * 128 : (v + 1) * 128]
        turned[v, 0] = part.reshape(devices, cap, 128)
        turned[v, 1] = pltpu.roll(part, 64, 1).reshape(devices, cap, 128)
    for r in range(grid.planes):
        for u in range(4):
            v, a = u // 2, u % 2
            slices = [
                jnp.where(
                    second,
                    turned[v, 1 - a][grid.linear(r, 2 * h + 1)],
                    turned[v, a][grid.linear(r, 2 * h)],
                )
                for h in range(4)
            ]
            for dest in (grid.linear(r, u), grid.linear(r, u + 4)):
                top = jnp.concatenate(slices[:3], axis=1)
                bottom = jnp.concatenate([slices[3], whole[dest]], axis=1)
                out_ref[dest] = jnp.concatenate([top, bottom], axis=0).astype(jnp.bfloat16)


def answer(grid, asked, codes):
    devices, cap, _ = asked.shape
    zch = codes.shape[1]
    return pl.pallas_call(
        functools.partial(answer_kernel, grid, cap),
        out_shape=jax.ShapeDtypeStruct((devices, 2 * cap, 384), jnp.bfloat16),
        in_specs=vmem(2),
        out_specs=vmem(1)[0],
        compiler_params=LIMIT,
        cost_estimate=cost(2 * devices * cap * codes.shape[0] * zch, 2 << 20),
    )(asked, codes)


def proj_kernel(place_ref, asked_ref, book_ref, codes_ref, keep_ref, send_ref, all_ref):
    entries, feat = book_ref.shape
    zch = codes_ref.shape[1]
    devices, cap, _ = asked_ref.shape
    asked = asked_ref[...].reshape(devices * cap, zch + 128)
    select = select_rows(asked, zch, entries)
    codes = jnp.dot(select, codes_ref[...], preferred_element_type=jnp.float32)
    rows = jnp.dot(select, book_ref[...], preferred_element_type=jnp.float32).astype(jnp.bfloat16)
    grads = 2.0 * (asked[:, zch : zch + 1] * codes - asked[:, :zch])
    upper = grads.astype(jnp.bfloat16)
    lower = (grads - upper.astype(jnp.float32)).astype(jnp.bfloat16)
    dims = (((0,), (0,)), ((), ()))
    total = lax.dot_general(rows, upper, dims, preferred_element_type=jnp.float32)
    all_ref[...] = total + lax.dot_general(rows, lower, dims, preferred_element_type=jnp.float32)
    core = place_ref[0] % 2
    keep_ref[...] = all_ref[:, pl.ds(pl.multiple_of(core * 128, 128), 128)]
    send_ref[...] = all_ref[:, pl.ds(pl.multiple_of((1 - core) * 128, 128), 128)]


def proj_part(place, asked, book, codes):
    feat, zch = book.shape[1], codes.shape[1]
    slots = asked.shape[0] * asked.shape[1]
    return pl.pallas_call(
        proj_kernel,
        out_shape=(jax.ShapeDtypeStruct((feat, 128), jnp.float32),) * 2,
        in_specs=[SMEM_SPEC] + vmem(3),
        out_specs=tuple(vmem(2)),
        scratch_shapes=[pltpu.VMEM((feat, zch), jnp.float32)],
        compiler_params=LIMIT,
        cost_estimate=cost(2 * slots * (book.shape[0] + 2 * zch) * feat, 4 << 20),
    )(place, asked, book, codes)


def half(x, axis, index):
    return lax.dynamic_index_in_dim(x, index, axis, keepdims=False)


def exchange(x, own, perm):
    sent = half(x, 0, 1 - own).astype(jnp.bfloat16)
    return half(x, 0, own) + send(sent, perm).astype(jnp.float32)


def proj_place(i, q, prows):
    return (((i // 2) % 2) * 2 + i // 4) * PARTS * prows + q * prows, i % 2


def weights_kernel(grid, cap, place_ref, got_ref, *refs):
    cots, (acc_ref, xt_ref) = refs[:8], refs[8:]
    devices = grid.total
    slots = devices * cap
    tokens, channels = cots[0].shape
    tokens -= 16
    cut = tokens // 2
    i, part = place_ref[0], place_ref[1]
    got = got_ref[...].astype(jnp.float32)
    xt_ref[:384] = got[:, :cap].reshape(slots, 384).T
    xt_ref[384:] = got[:, cap:, :128].reshape(slots, 128).T
    wide = 64
    krows = 9 * wide // 2
    token = lax.broadcasted_iota(jnp.int32, (1, tokens), 1)
    line, cell = token // 16 % 16, token % 16
    slot_id = lax.broadcasted_iota(jnp.int32, (slots, tokens), 0)
    ones = (lax.broadcasted_iota(jnp.int32, (16, tokens), 0) == 0).astype(jnp.float32)
    cots = {j: cots[j % 2 * 4 + j // 2] for j in range(8)}
    for j in range(8):
        member = i ^ j
        xt = xt_ref[pl.ds(pl.multiple_of(member * wide, wide), wide), :].astype(jnp.bfloat16)
        last = cots[j][tokens:].astype(jnp.float32)
        last = last[0:2] * cap + last[2:4]
        slot = jnp.concatenate([last[0:1], last[1:2]], axis=1).astype(jnp.int32)
        hit = (slot_id == slot).astype(jnp.float32).astype(jnp.bfloat16)
        quant = jnp.dot(xt, hit, preferred_element_type=jnp.float32)
        taps = []
        for down in (-1, 0, 1):
            for right in (-1, 0, 1):
                shift = (-(down * 16 + right)) % tokens
                moved = quant if shift == 0 else pltpu.roll(quant, shift, 1)
                valid = (line + down >= 0) & (line + down < 16) & (cell + right >= 0) & (cell + right < 16)
                taps.append(moved * valid.astype(jnp.float32))
        taps = [x[: wide // 2] for x in taps] + [x[wide // 2 :] for x in taps]
        left = jnp.concatenate(taps + [ones], axis=0).astype(jnp.bfloat16)
        value = jnp.dot(left, cots[j][:tokens], preferred_element_type=jnp.float32)
        if j == 0:
            acc_ref[...] = value
        else:
            acc_ref[...] += value


def pack_kernel(krows, place_ref, acc_ref, proj_ref, own_ref, *send_refs):
    part = place_ref[1]

    def piece(q):
        lanes = pl.ds(pl.multiple_of(q % 2 * 128, 128), 128)
        rows = pl.ds(pl.multiple_of(q // 2 * krows, 8), krows)
        return acc_ref[rows, lanes], acc_ref[2 * krows :, lanes]

    own_ref[:krows], own_ref[krows : krows + 16] = piece(part)
    own_ref[krows + 16 :] = proj_ref[part]
    row = lax.broadcasted_iota(jnp.int32, (16, 128), 0)
    for k, send_ref in enumerate(send_refs, 1):
        value, last = piece((part + k) % PARTS)
        upper = last.astype(jnp.bfloat16).astype(jnp.float32)
        lower = (last - upper)[0:1]
        send_ref[:krows] = value.astype(jnp.bfloat16)
        send_ref[krows : krows + 16] = jnp.where(row == 1, lower, last).astype(jnp.bfloat16)
        send_ref[krows + 16 :] = proj_ref[(part + k) % PARTS].astype(jnp.bfloat16)


def group_weights(grid, place, got, cots, cap):
    channels = cots[0].shape[1]
    slots = grid.total * cap
    return pl.pallas_call(
        functools.partial(weights_kernel, grid, cap),
        out_shape=jax.ShapeDtypeStruct((9 * 64 + 16, channels), jnp.float32),
        in_specs=[SMEM_SPEC] + vmem(9),
        out_specs=vmem(1)[0],
        scratch_shapes=[pltpu.VMEM((512, slots), jnp.float32)],
        compiler_params=LIMIT,
        cost_estimate=cost(2 * 9 * 512 * 512 * channels, 8 << 20),
    )(place, got, *cots)


def pack(place, acc, proj):
    krows = (acc.shape[0] - 16) // 2
    height = krows + 16 + proj.shape[1]
    return pl.pallas_call(
        functools.partial(pack_kernel, krows),
        out_shape=[jax.ShapeDtypeStruct((height, 128), jnp.float32)]
        + [jax.ShapeDtypeStruct((height, 128), jnp.bfloat16)] * (PARTS - 1),
        in_specs=[SMEM_SPEC] + vmem(2),
        out_specs=vmem(PARTS),
        compiler_params=LIMIT,
    )(place, acc, proj)


def combine_kernel(krows, own_ref, *refs):
    got_refs, out_ref = refs[:-1], refs[-1]
    total = own_ref[...]
    for ref in got_refs:
        total = total + ref[...].astype(jnp.float32)
    kernel = total[:krows]
    proj = total[krows + 16 :]
    bias = total[krows : krows + 1] + total[krows + 1 : krows + 2]
    row = lax.broadcasted_iota(jnp.int32, (16, own_ref.shape[1]), 0)
    extra = jnp.zeros(row.shape, jnp.float32)
    sums = (
        bias,
        jnp.sum(kernel * kernel, axis=0, keepdims=True),
        jnp.sum(proj * proj, axis=0, keepdims=True),
    )
    for n, value in enumerate(sums):
        upper = value.astype(jnp.bfloat16).astype(jnp.float32)
        middle = (value - upper).astype(jnp.bfloat16).astype(jnp.float32)
        for k, piece in enumerate((upper, middle, value - upper - middle)):
            extra = jnp.where(row == 3 * n + k, piece, extra)
    out_ref[:krows] = kernel.astype(jnp.bfloat16)
    out_ref[krows : krows + 16] = extra.astype(jnp.bfloat16)
    out_ref[krows + 16 :] = proj.astype(jnp.bfloat16)


def combine(krows, own, got):
    return pl.pallas_call(
        functools.partial(combine_kernel, krows),
        out_shape=jax.ShapeDtypeStruct(own.shape, jnp.bfloat16),
        in_specs=vmem(1 + len(got)),
        out_specs=vmem(1)[0],
        compiler_params=LIMIT,
    )(own, *got)


def reduce_planes(grid, own, sends, r):
    got = [send(s, grid.turn(k)) for k, s in enumerate(sends, 1)]
    groups = grid.planes // PARTS
    if groups > 1:
        own = own + sum(g.astype(jnp.float32) for g in got)
        rest = [own] + [send(own, grid.far(k)) for k in range(1, groups)]
        order = (r // PARTS - jnp.arange(groups)) % groups
        own = jnp.sum(jnp.take(jnp.stack(rest), order, axis=0), axis=0)
        got = []
    return own, got


def finish_kernel(krows, counts, place_ref, *refs):
    (kernel_ref, proj_ref, bias_ref, keep_ref), refs = refs[6:], refs[:6]
    i, part = place_ref[0], place_ref[1]
    wide = krows // 9
    prows = refs[0].shape[1] - krows - 16
    sources = []
    near = [(n, 2 * n, 0) for n in range(4)]
    middle = [(n, n // 3 * 2, n % 3 + 1) for n in range(9)]
    last = [(n, 6, n + 1) for n in range(3)]
    for m, ref in enumerate(refs):
        for n, bits, turn in (near, middle, last)[m % 3]:
            place = i ^ (bits + m // 3)
            q = (part + PARTS - turn) % PARTS
            sources.append((ref, n, place, q))
            keep_ref[place * PARTS + q] = ref[n, krows : krows + 16].astype(jnp.float32)
    kept = jnp.sum(keep_ref[...], axis=0)

    def factor(values, count):
        total = jnp.sum(jnp.sum(values, axis=0, keepdims=True), axis=1, keepdims=True)
        return 1.0 / jnp.sqrt(total / count + norm_eps)

    kfactor, pfactor = factor(kept[3:6], counts[0]), factor(kept[6:9], counts[1])
    for ref, n, place, q in sources:
        value = ref[n].astype(jnp.float32)
        lanes = pl.ds(pl.multiple_of(place // 4 * 256 + q % 2 * 128, 128), 128)
        start = place % 4 * 64 + q // 2 * 32
        kernel_ref[:, pl.ds(pl.multiple_of(start, 32), wide), lanes] = (
            value[:krows] * kfactor
        ).reshape(9, wide, 128)
        row, col = proj_place(place, q, prows)
        proj_ref[pl.ds(pl.multiple_of(row, 8), prows), pl.ds(pl.multiple_of(col * 128, 128), 128)] = (
            value[krows + 16 :] * pfactor
        )
    bias = [jnp.sum(keep_ref[n, 0:3], axis=0, keepdims=True) for n in (0, 1, 16, 17)]
    bias = jnp.concatenate(bias, axis=1)
    bias_ref[...] = bias * factor(bias * bias, counts[2])


def finish(place, blocks, zch, channels, feat):
    krows = 9 * zch // 8
    counts = (9 * zch * channels, feat * zch, channels)
    return pl.pallas_call(
        functools.partial(finish_kernel, krows, counts),
        out_shape=(
            jax.ShapeDtypeStruct((9, zch, channels), jnp.float32),
            jax.ShapeDtypeStruct((feat, zch), jnp.float32),
            jax.ShapeDtypeStruct((1, channels), jnp.float32),
        ),
        in_specs=[SMEM_SPEC] + vmem(6),
        out_specs=tuple(vmem(3)),
        scratch_shapes=[pltpu.VMEM((32, 16, 128), jnp.float32)],
        compiler_params=LIMIT,
    )(place, *blocks)


def gather_near(grid, near, far):
    return [near, send(near, grid.flip(2)), send(far, grid.flip(4)), send(far, grid.flip(6))]


def on_device(
    grid, codebook, projector, latents, wanted, wanted_count, token_pick, kernel, bias, cotangent
):
    devices = grid.total
    images, rows, width, zch = latents.shape
    channels = kernel.shape[3]
    feat = codebook.shape[1]
    cap = wanted.shape[2]
    slots = devices * cap
    tokens = images * rows * width
    r, i = grid.place()
    place = jnp.stack([i, r % PARTS]).astype(jnp.int32)
    near, far, slot, ask = token_part(
        place,
        token_pick.reshape(images * rows, width),
        wanted_count,
        jnp.swapaxes(wanted.reshape(devices, cap), 0, 1),
        latents.reshape(tokens, zch),
        cotangent.reshape(tokens, channels),
    )
    asked = spread(ask, grid)
    cots = gather_near(grid, near, far)
    local_codes = jnp.dot(codebook, projector, preferred_element_type=jnp.float32).astype(
        jnp.bfloat16
    )
    slot_ids = jnp.arange(slots, dtype=jnp.int32)
    onehot = (slot.reshape(tokens, 1) == slot_ids[None, :]).astype(jnp.bfloat16)
    replies = answer(grid, asked, local_codes)
    got = spread(replies, grid)
    asked, _, *cots = lax.optimization_barrier((asked, replies, *cots))
    cots = cots + [send(x, grid.flip(1)) for x in cots]
    kept, sent = proj_part(place, asked, codebook, local_codes)
    proj = (kept + send(sent, grid.flip(1))).reshape(2, 2, PARTS, feat // 16, 128)
    cotangent, _ = lax.optimization_barrier((cotangent, replies))
    proj = exchange(proj, i // 2 % 2, grid.flip(2))
    got_half = send(half(proj, 0, 1 - i // 4).astype(jnp.bfloat16), grid.flip(4))
    acc = group_weights(grid, place, got, cots, cap)
    kept, acc = lax.optimization_barrier((half(proj, 0, i // 4), acc))
    own, *sends = pack(place, acc, kept + got_half.astype(jnp.float32))
    codes = got[:, cap:, 128:].reshape(slots, zch)
    codes, own, *sends = lax.optimization_barrier((codes, own, *sends))
    own, received = reduce_planes(grid, own, sends, r)
    quant = jnp.dot(onehot, codes, preferred_element_type=jnp.float32).astype(jnp.bfloat16)
    quant = quant.reshape(images, rows, width, zch)
    quant_f = quant.astype(jnp.float32)
    latent_f = latents.astype(jnp.float32)
    padded = jnp.pad(quant, ((0, 0), (1, 1), (1, 1), (0, 0)))
    padded_grad = jnp.pad(cotangent, ((0, 0), (1, 1), (1, 1), (0, 0)))
    output = jnp.zeros((images, rows, width, channels), jnp.float32)
    grad_input = jnp.zeros((images, rows, width, zch), jnp.float32)
    for row_off in range(3):
        for col_off in range(3):
            window = padded[:, row_off : row_off + rows, col_off : col_off + width]
            output = output + jnp.einsum(
                "nhwc,co->nhwo",
                window,
                kernel[row_off, col_off],
                preferred_element_type=jnp.float32,
            )
            grad_window = padded_grad[
                :, 2 - row_off : 2 - row_off + rows, 2 - col_off : 2 - col_off + width
            ]
            grad_input = grad_input + jnp.einsum(
                "nhwo,co->nhwc",
                grad_window,
                kernel[row_off, col_off],
                preferred_element_type=jnp.float32,
            )
    hidden = (output + bias.astype(jnp.float32)).astype(jnp.bfloat16)
    grad_latents = (grad_input + 2.0 * commit_weight * (latent_f - quant_f)).astype(jnp.bfloat16)
    krows = 9 * zch // 8
    planes = gather_planes(grid, combine(krows, own, received))
    *planes, hidden, grad_latents = lax.optimization_barrier((*planes, hidden, grad_latents))
    blocks = gather_places(grid, *planes)
    kernel_step, proj_step, bias_step = finish(place, blocks, zch, channels, feat)
    kernel_step = kernel_step.reshape(3, 3, zch, channels)
    return (hidden, grad_latents, proj_step, kernel_step, bias_step.reshape(channels))


def solution(mesh):
    grid = Grid(mesh.shape["dp"], mesh.shape["code"])
    in_specs = (
        P(("dp", "code"), None),
        P(),
        P(("dp", "code"), None, None, None),
        P(("dp", "code"), None, None),
        P(("dp", "code"), None),
        P(("dp", "code"), None, None),
        P(),
        P(),
        P(("dp", "code"), None, None, None),
    )
    out_specs = (
        P(("dp", "code"), None, None, None),
        P(("dp", "code"), None, None, None),
        P(),
        P(),
        P(),
    )
    return jax.shard_map(
        functools.partial(on_device, grid),
        mesh=mesh,
        in_specs=in_specs,
        out_specs=out_specs,
        check_vma=False,
    )
```

```python
import functools

import jax
import jax.numpy as jnp
from jax import lax
from jax.experimental import pallas as pl
from jax.experimental.pallas import tpu as pltpu
from jax.sharding import PartitionSpec as P

commit_weight = 0.25
norm_eps = 1e-06
AXES = ("dp", "code")
PARTS = 4


class Grid:
    def __init__(self, n_dp, n_code):
        self.n_dp, self.n_code = n_dp, n_code
        self.outer = n_code // 4
        self.planes = (n_dp // 2) * self.outer
        self.total = n_dp * n_code

    def linear(self, r, i):
        dh, ch = r // self.outer, r % self.outer
        return (dh * 2 + i // 4) * self.n_code + ch * 4 + i % 4

    def perm(self, move):
        return [
            (self.linear(r, i), self.linear(*move(r, i)))
            for r in range(self.planes)
            for i in range(8)
        ]

    def flip(self, bit):
        return self.perm(lambda r, i: (r, i ^ bit))

    def turn(self, k):
        return self.perm(lambda r, i: (r // PARTS * PARTS + (r + k) % PARTS, i))

    def far(self, k):
        groups = self.planes // PARTS
        return self.perm(lambda r, i: ((r // PARTS + k) % groups * PARTS + r % PARTS, i))

    def order(self, x):
        rest = x.shape[2:]
        x = x.reshape(self.n_dp // 2, self.outer, 2, 4, *rest)
        return jnp.swapaxes(x, 1, 2).reshape(self.total, *rest)

    def place(self):
        dp, code = lax.axis_index("dp"), lax.axis_index("code")
        return (dp // 2) * self.outer + code // 4, (dp % 2) * 4 + code % 4


def send(x, perm):
    return lax.ppermute(x, AXES, perm)


def gather_planes(grid, own):
    zs = [send(own, grid.turn(k)) for k in range(1, PARTS)]
    x, y = send(own, grid.flip(2)), send(own, grid.flip(4))
    early = jnp.stack([own, x, y, send(x, grid.flip(4))])
    zs = jnp.stack(zs)
    return early, zs, send(zs, grid.flip(2)), send(zs, grid.flip(4))


def gather_places(grid, early, zs, xs, ys):
    second, first = send(ys[:2], grid.flip(2)), send(xs[2:], grid.flip(4))
    mine = [early, jnp.concatenate([zs, xs, ys]), jnp.concatenate([second, first])]
    return mine + [send(x, grid.flip(1)) for x in mine]


def vmem(count):
    return [pl.BlockSpec(memory_space=pltpu.VMEM)] * count


SMEM_SPEC = pl.BlockSpec(memory_space=pltpu.SMEM)
LIMIT = pltpu.CompilerParams(vmem_limit_bytes=40 << 20)


def cost(flops, nbytes):
    return pl.CostEstimate(flops=flops, bytes_accessed=nbytes, transcendentals=0)


def spread(x, grid):
    return lax.all_to_all(x, AXES, split_axis=0, concat_axis=0, tiled=True)


def token_kernel(
    cap, place_ref, pick_hbm, counts_hbm, wanted_hbm, latents_hbm, cot_hbm, near_ref, far_ref, slot_ref, ask_ref, *rest
):
    pick_ref, counts_ref, wanted_ref, latents_ref, cot_ref, sems = rest
    sources = (pick_hbm, counts_hbm, wanted_hbm, latents_hbm, cot_hbm)
    copies = [
        pltpu.make_async_copy(source, target, sems.at[n])
        for n, (source, target) in enumerate(zip(sources, rest[:-1]))
    ]
    for copy in copies:
        copy.start()
    for copy in copies[:4]:
        copy.wait()
    lines, width = pick_ref.shape
    devices = counts_ref.shape[1]
    tokens = lines * width
    pick = pick_ref[...]
    owner = pick // cap
    first = pick - owner * cap
    token = lax.broadcasted_iota(jnp.int32, (width, tokens), 1)
    wide = (token % width == lax.broadcasted_iota(jnp.int32, (width, tokens), 0)).astype(jnp.float32)
    wide = wide.astype(jnp.bfloat16)
    token = lax.broadcasted_iota(jnp.int32, (lines, tokens), 1)
    keep = token // width == lax.broadcasted_iota(jnp.int32, (lines, tokens), 0)

    def flat(x):
        x = x.astype(jnp.float32).astype(jnp.bfloat16)
        x = jnp.dot(x, wide, preferred_element_type=jnp.float32)
        return jnp.sum(jnp.where(keep, x, 0.0), axis=0, keepdims=True)

    owner, entry = flat(owner), flat(first)
    row = lax.broadcasted_iota(jnp.int32, (devices, devices), 0)
    col = lax.broadcasted_iota(jnp.int32, (devices, devices), 1)
    counts = jnp.where(row == col, counts_ref[...].astype(jnp.float32), 0.0)
    counts = jnp.sum(counts, axis=1, keepdims=True)
    owner_id = lax.broadcasted_iota(jnp.int32, (devices, tokens), 0)
    count = jnp.sum(
        jnp.where(owner_id == owner.astype(jnp.int32), counts, 0.0), axis=0, keepdims=True
    )
    for _ in range(cap - 1):
        entry = jnp.where(entry >= count, entry - count, entry)
    slot = (owner * cap + entry).astype(jnp.int32)
    slot_ref[...] = slot
    place = lax.broadcasted_iota(jnp.int32, (16, tokens), 0)
    wide = cot_ref.shape[1] // 2
    place = place[:, :wide]
    extra = jnp.zeros((16, wide), jnp.float32)
    for n, row in enumerate((owner[:, :wide], owner[:, wide:], entry[:, :wide], entry[:, wide:])):
        extra = jnp.where(place == n, row, extra)
    copies[4].wait()
    for ref, side in ((near_ref, place_ref[0] // 4), (far_ref, 1 - place_ref[0] // 4)):
        ref[:tokens] = cot_ref[:, pl.ds(pl.multiple_of(side * wide, wide), wide)]
        ref[tokens:] = extra.astype(jnp.bfloat16)
    hit = (lax.broadcasted_iota(jnp.int32, (devices * cap, tokens), 0) == slot).astype(jnp.float32)
    slots = devices * cap
    uses = jnp.sum(hit, axis=1, keepdims=True)
    sums = jnp.dot(hit.astype(jnp.bfloat16), latents_ref[...], preferred_element_type=jnp.float32)
    zch = sums.shape[1]
    wanted = wanted_ref[...].astype(jnp.float32).T
    wanted = jnp.broadcast_to(wanted[:, None, :], (devices, cap, cap)).reshape(slots, cap)
    place = lax.broadcasted_iota(jnp.int32, (slots, cap), 0) % cap
    lane = lax.broadcasted_iota(jnp.int32, (slots, cap), 1)
    wanted = jnp.sum(jnp.where(lane == place, wanted, 0.0), axis=1, keepdims=True)
    lane = lax.broadcasted_iota(jnp.int32, (slots, 128), 1)
    last = jnp.where(lane == 0, uses, jnp.where(lane == 1, wanted, 0.0))
    ask_ref[:, :, :zch] = sums.reshape(devices, cap, zch)
    ask_ref[:, :, zch:] = last.reshape(devices, cap, 128)


def token_part(place, pick, counts, wanted, latents, cots):
    tokens, channels = cots.shape
    cap, devices = wanted.shape
    slots = devices * cap
    return pl.pallas_call(
        functools.partial(token_kernel, cap),
        out_shape=(
            jax.ShapeDtypeStruct((tokens + 16, channels // 2), jnp.bfloat16),
            jax.ShapeDtypeStruct((tokens + 16, channels // 2), jnp.bfloat16),
            jax.ShapeDtypeStruct((1, tokens), jnp.int32),
            jax.ShapeDtypeStruct((devices, cap, latents.shape[1] + 128), jnp.float32),
        ),
        in_specs=[SMEM_SPEC] + [pl.BlockSpec(memory_space=pltpu.HBM)] * 5,
        out_specs=tuple(vmem(4)),
        scratch_shapes=[
            pltpu.VMEM(x.shape, x.dtype) for x in (pick, counts, wanted, latents, cots)
        ]
        + [pltpu.SemaphoreType.DMA((5,))],
        compiler_params=pltpu.CompilerParams(vmem_limit_bytes=62 << 20),
        cost_estimate=cost(2 * slots * tokens * latents.shape[1], 2 << 20),
    )(place, pick, counts, wanted, latents, cots)


def select_rows(asked, zch, entries):
    column = asked[:, zch + 1 : zch + 2].astype(jnp.int32)
    hit = column == lax.broadcasted_iota(jnp.int32, (asked.shape[0], entries), 1)
    return hit.astype(jnp.float32).astype(jnp.bfloat16)


def answer_kernel(grid, cap, asked_ref, codes_ref, out_ref):
    devices = grid.total
    entries, zch = codes_ref.shape
    select = select_rows(asked_ref[...].reshape(devices * cap, zch + 128), zch, entries)
    codes = jnp.dot(select, codes_ref[...], preferred_element_type=jnp.float32)
    whole = codes.reshape(devices, cap, zch)
    second = lax.broadcasted_iota(jnp.int32, (cap, 128), 1) >= 64
    turned = {}
    for v in range(2):
        part = codes[:, v * 128 : (v + 1) * 128]
        turned[v, 0] = part.reshape(devices, cap, 128)
        turned[v, 1] = pltpu.roll(part, 64, 1).reshape(devices, cap, 128)
    for r in range(grid.planes):
        for u in range(4):
            v, a = u // 2, u % 2
            slices = [
                jnp.where(
                    second,
                    turned[v, 1 - a][grid.linear(r, 2 * h + 1)],
                    turned[v, a][grid.linear(r, 2 * h)],
                )
                for h in range(4)
            ]
            for dest in (grid.linear(r, u), grid.linear(r, u + 4)):
                top = jnp.concatenate(slices[:3], axis=1)
                bottom = jnp.concatenate([slices[3], whole[dest]], axis=1)
                out_ref[dest] = jnp.concatenate([top, bottom], axis=0).astype(jnp.bfloat16)


def answer(grid, asked, codes):
    devices, cap, _ = asked.shape
    zch = codes.shape[1]
    return pl.pallas_call(
        functools.partial(answer_kernel, grid, cap),
        out_shape=jax.ShapeDtypeStruct((devices, 2 * cap, 384), jnp.bfloat16),
        in_specs=vmem(2),
        out_specs=vmem(1)[0],
        compiler_params=LIMIT,
        cost_estimate=cost(2 * devices * cap * codes.shape[0] * zch, 2 << 20),
    )(asked, codes)


def proj_kernel(place_ref, asked_ref, book_ref, codes_ref, keep_ref, send_ref, all_ref):
    entries, feat = book_ref.shape
    zch = codes_ref.shape[1]
    devices, cap, _ = asked_ref.shape
    asked = asked_ref[...].reshape(devices * cap, zch + 128)
    select = select_rows(asked, zch, entries)
    codes = jnp.dot(select, codes_ref[...], preferred_element_type=jnp.float32)
    rows = jnp.dot(select, book_ref[...], preferred_element_type=jnp.float32).astype(jnp.bfloat16)
    grads = 2.0 * (asked[:, zch : zch + 1] * codes - asked[:, :zch])
    upper = grads.astype(jnp.bfloat16)
    lower = (grads - upper.astype(jnp.float32)).astype(jnp.bfloat16)
    dims = (((0,), (0,)), ((), ()))
    total = lax.dot_general(rows, upper, dims, preferred_element_type=jnp.float32)
    all_ref[...] = total + lax.dot_general(rows, lower, dims, preferred_element_type=jnp.float32)
    core = place_ref[0] % 2
    keep_ref[...] = all_ref[:, pl.ds(pl.multiple_of(core * 128, 128), 128)]
    send_ref[...] = all_ref[:, pl.ds(pl.multiple_of((1 - core) * 128, 128), 128)]


def proj_part(place, asked, book, codes):
    feat, zch = book.shape[1], codes.shape[1]
    slots = asked.shape[0] * asked.shape[1]
    return pl.pallas_call(
        proj_kernel,
        out_shape=(jax.ShapeDtypeStruct((feat, 128), jnp.float32),) * 2,
        in_specs=[SMEM_SPEC] + vmem(3),
        out_specs=tuple(vmem(2)),
        scratch_shapes=[pltpu.VMEM((feat, zch), jnp.float32)],
        compiler_params=LIMIT,
        cost_estimate=cost(2 * slots * (book.shape[0] + 2 * zch) * feat, 4 << 20),
    )(place, asked, book, codes)


def proj_split_kernel(place_ref, kept_ref, got_ref, own_ref, *rest):
    send_refs, all_ref = rest[:-1], rest[-1]
    all_ref[...] = kept_ref[...] + got_ref[...]
    i = place_ref[0]
    size = all_ref.shape[0] // 4

    def quarter(place):
        start = (place // 2 % 2 * 2 + place // 4) * size
        return all_ref[pl.ds(pl.multiple_of(start, 8), size), :].reshape(own_ref.shape)

    own_ref[...] = quarter(i)
    for bits, send_ref in zip((2, 4, 6), send_refs):
        send_ref[...] = quarter(i ^ bits).astype(jnp.bfloat16)


def proj_split(place, kept, got):
    shape = (PARTS, kept.shape[0] // 16, 128)
    return pl.pallas_call(
        proj_split_kernel,
        out_shape=[jax.ShapeDtypeStruct(shape, jnp.float32)]
        + [jax.ShapeDtypeStruct(shape, jnp.bfloat16)] * 3,
        in_specs=[SMEM_SPEC] + vmem(2),
        out_specs=vmem(4),
        scratch_shapes=[pltpu.VMEM(kept.shape, jnp.float32)],
        compiler_params=LIMIT,
    )(place, kept, got)


def proj_place(i, q, prows):
    return (((i // 2) % 2) * 2 + i // 4) * PARTS * prows + q * prows, i % 2


def weights_kernel(grid, cap, place_ref, got_ref, *refs):
    cots, (acc_ref, xt_ref) = refs[:8], refs[8:]
    devices = grid.total
    slots = devices * cap
    tokens, channels = cots[0].shape
    tokens -= 16
    cut = tokens // 2
    i, part = place_ref[0], place_ref[1]
    got = got_ref[...].astype(jnp.float32)
    xt_ref[:384] = got[:, :cap].reshape(slots, 384).T
    xt_ref[384:] = got[:, cap:, :128].reshape(slots, 128).T
    wide = 64
    krows = 9 * wide // 2
    token = lax.broadcasted_iota(jnp.int32, (1, tokens), 1)
    line, cell = token // 16 % 16, token % 16
    slot_id = lax.broadcasted_iota(jnp.int32, (slots, tokens), 0)
    ones = (lax.broadcasted_iota(jnp.int32, (16, tokens), 0) == 0).astype(jnp.float32)
    cots = {j: cots[j % 2 * 4 + j // 2] for j in range(8)}
    for j in range(8):
        member = i ^ j
        xt = xt_ref[pl.ds(pl.multiple_of(member * wide, wide), wide), :].astype(jnp.bfloat16)
        last = cots[j][tokens:].astype(jnp.float32)
        last = last[0:2] * cap + last[2:4]
        slot = jnp.concatenate([last[0:1], last[1:2]], axis=1).astype(jnp.int32)
        hit = (slot_id == slot).astype(jnp.float32).astype(jnp.bfloat16)
        quant = jnp.dot(xt, hit, preferred_element_type=jnp.float32)
        taps = []
        for down in (-1, 0, 1):
            for right in (-1, 0, 1):
                shift = (-(down * 16 + right)) % tokens
                moved = quant if shift == 0 else pltpu.roll(quant, shift, 1)
                valid = (line + down >= 0) & (line + down < 16) & (cell + right >= 0) & (cell + right < 16)
                taps.append(moved * valid.astype(jnp.float32))
        taps = [x[: wide // 2] for x in taps] + [x[wide // 2 :] for x in taps]
        left = jnp.concatenate(taps + [ones], axis=0).astype(jnp.bfloat16)
        value = jnp.dot(left, cots[j][:tokens], preferred_element_type=jnp.float32)
        if j == 0:
            acc_ref[...] = value
        else:
            acc_ref[...] += value


def pack_kernel(krows, place_ref, acc_ref, *refs):
    proj_refs, (own_ref, *send_refs) = refs[:4], refs[4:]
    part = place_ref[1]

    def proj(q):
        return sum(ref[q].astype(jnp.float32) for ref in proj_refs)

    def piece(q):
        lanes = pl.ds(pl.multiple_of(q % 2 * 128, 128), 128)
        rows = pl.ds(pl.multiple_of(q // 2 * krows, 8), krows)
        return acc_ref[rows, lanes], acc_ref[2 * krows :, lanes]

    own_ref[:krows], own_ref[krows : krows + 16] = piece(part)
    own_ref[krows + 16 :] = proj(part)
    row = lax.broadcasted_iota(jnp.int32, (16, 128), 0)
    for k, send_ref in enumerate(send_refs, 1):
        value, last = piece((part + k) % PARTS)
        upper = last.astype(jnp.bfloat16).astype(jnp.float32)
        lower = (last - upper)[0:1]
        send_ref[:krows] = value.astype(jnp.bfloat16)
        send_ref[krows : krows + 16] = jnp.where(row == 1, lower, last).astype(jnp.bfloat16)
        send_ref[krows + 16 :] = proj((part + k) % PARTS).astype(jnp.bfloat16)


def group_weights(grid, place, got, cots, cap):
    channels = cots[0].shape[1]
    slots = grid.total * cap
    return pl.pallas_call(
        functools.partial(weights_kernel, grid, cap),
        out_shape=jax.ShapeDtypeStruct((9 * 64 + 16, channels), jnp.float32),
        in_specs=[SMEM_SPEC] + vmem(9),
        out_specs=vmem(1)[0],
        scratch_shapes=[pltpu.VMEM((512, slots), jnp.float32)],
        compiler_params=LIMIT,
        cost_estimate=cost(2 * 9 * 512 * 512 * channels, 8 << 20),
    )(place, got, *cots)


def pack(place, acc, proj):
    krows = (acc.shape[0] - 16) // 2
    height = krows + 16 + proj[0].shape[1]
    return pl.pallas_call(
        functools.partial(pack_kernel, krows),
        out_shape=[jax.ShapeDtypeStruct((height, 128), jnp.float32)]
        + [jax.ShapeDtypeStruct((height, 128), jnp.bfloat16)] * (PARTS - 1),
        in_specs=[SMEM_SPEC] + vmem(5),
        out_specs=vmem(PARTS),
        compiler_params=LIMIT,
    )(place, acc, *proj)


def combine_kernel(krows, own_ref, *refs):
    got_refs, out_ref = refs[:-1], refs[-1]
    total = own_ref[...]
    for ref in got_refs:
        total = total + ref[...].astype(jnp.float32)
    kernel = total[:krows]
    proj = total[krows + 16 :]
    bias = total[krows : krows + 1] + total[krows + 1 : krows + 2]
    row = lax.broadcasted_iota(jnp.int32, (16, own_ref.shape[1]), 0)
    extra = jnp.zeros(row.shape, jnp.float32)
    sums = (
        bias,
        jnp.sum(kernel * kernel, axis=0, keepdims=True),
        jnp.sum(proj * proj, axis=0, keepdims=True),
    )
    for n, value in enumerate(sums):
        upper = value.astype(jnp.bfloat16).astype(jnp.float32)
        middle = (value - upper).astype(jnp.bfloat16).astype(jnp.float32)
        for k, piece in enumerate((upper, middle, value - upper - middle)):
            extra = jnp.where(row == 3 * n + k, piece, extra)
    out_ref[:krows] = kernel.astype(jnp.bfloat16)
    out_ref[krows : krows + 16] = extra.astype(jnp.bfloat16)
    out_ref[krows + 16 :] = proj.astype(jnp.bfloat16)


def combine(krows, own, got):
    return pl.pallas_call(
        functools.partial(combine_kernel, krows),
        out_shape=jax.ShapeDtypeStruct(own.shape, jnp.bfloat16),
        in_specs=vmem(1 + len(got)),
        out_specs=vmem(1)[0],
        compiler_params=LIMIT,
    )(own, *got)


def reduce_planes(grid, own, sends, r):
    got = [send(s, grid.turn(k)) for k, s in enumerate(sends, 1)]
    groups = grid.planes // PARTS
    if groups > 1:
        own = own + sum(g.astype(jnp.float32) for g in got)
        rest = [own] + [send(own, grid.far(k)) for k in range(1, groups)]
        order = (r // PARTS - jnp.arange(groups)) % groups
        own = jnp.sum(jnp.take(jnp.stack(rest), order, axis=0), axis=0)
        got = []
    return own, got


def finish_kernel(krows, counts, place_ref, *refs):
    (kernel_ref, proj_ref, bias_ref, keep_ref), refs = refs[6:], refs[:6]
    i, part = place_ref[0], place_ref[1]
    wide = krows // 9
    prows = refs[0].shape[1] - krows - 16
    sources = []
    near = [(n, 2 * n, 0) for n in range(4)]
    middle = [(n, n // 3 * 2, n % 3 + 1) for n in range(9)]
    last = [(n, 6, n + 1) for n in range(3)]
    for m, ref in enumerate(refs):
        for n, bits, turn in (near, middle, last)[m % 3]:
            place = i ^ (bits + m // 3)
            q = (part + PARTS - turn) % PARTS
            sources.append((ref, n, place, q))
            keep_ref[place * PARTS + q] = ref[n, krows : krows + 16].astype(jnp.float32)
    kept = jnp.sum(keep_ref[...], axis=0)

    def factor(values, count):
        total = jnp.sum(jnp.sum(values, axis=0, keepdims=True), axis=1, keepdims=True)
        return 1.0 / jnp.sqrt(total / count + norm_eps)

    kfactor, pfactor = factor(kept[3:6], counts[0]), factor(kept[6:9], counts[1])
    for ref, n, place, q in sources:
        value = ref[n].astype(jnp.float32)
        lanes = pl.ds(pl.multiple_of(place // 4 * 256 + q % 2 * 128, 128), 128)
        start = place % 4 * 64 + q // 2 * 32
        kernel_ref[:, pl.ds(pl.multiple_of(start, 32), wide), lanes] = (
            value[:krows] * kfactor
        ).reshape(9, wide, 128)
        row, col = proj_place(place, q, prows)
        proj_ref[pl.ds(pl.multiple_of(row, 8), prows), pl.ds(pl.multiple_of(col * 128, 128), 128)] = (
            value[krows + 16 :] * pfactor
        )
    bias = [jnp.sum(keep_ref[n, 0:3], axis=0, keepdims=True) for n in (0, 1, 16, 17)]
    bias = jnp.concatenate(bias, axis=1)
    bias_ref[...] = bias * factor(bias * bias, counts[2])


def finish(place, blocks, zch, channels, feat):
    krows = 9 * zch // 8
    counts = (9 * zch * channels, feat * zch, channels)
    return pl.pallas_call(
        functools.partial(finish_kernel, krows, counts),
        out_shape=(
            jax.ShapeDtypeStruct((9, zch, channels), jnp.float32),
            jax.ShapeDtypeStruct((feat, zch), jnp.float32),
            jax.ShapeDtypeStruct((1, channels), jnp.float32),
        ),
        in_specs=[SMEM_SPEC] + vmem(6),
        out_specs=tuple(vmem(3)),
        scratch_shapes=[pltpu.VMEM((32, 16, 128), jnp.float32)],
        compiler_params=LIMIT,
    )(place, *blocks)


def gather_near(grid, near, far):
    return [near, send(near, grid.flip(2)), send(far, grid.flip(4)), send(far, grid.flip(6))]


def on_device(
    grid, codebook, projector, latents, wanted, wanted_count, token_pick, kernel, bias, cotangent
):
    devices = grid.total
    images, rows, width, zch = latents.shape
    channels = kernel.shape[3]
    feat = codebook.shape[1]
    cap = wanted.shape[2]
    slots = devices * cap
    tokens = images * rows * width
    r, i = grid.place()
    place = jnp.stack([i, r % PARTS]).astype(jnp.int32)
    near, far, slot, ask = token_part(
        place,
        token_pick.reshape(images * rows, width),
        wanted_count,
        jnp.swapaxes(wanted.reshape(devices, cap), 0, 1),
        latents.reshape(tokens, zch),
        cotangent.reshape(tokens, channels),
    )
    asked = spread(ask, grid)
    cots = gather_near(grid, near, far)
    local_codes = jnp.dot(codebook, projector, preferred_element_type=jnp.float32).astype(
        jnp.bfloat16
    )
    slot_ids = jnp.arange(slots, dtype=jnp.int32)
    onehot = (slot.reshape(tokens, 1) == slot_ids[None, :]).astype(jnp.bfloat16)
    replies = answer(grid, asked, local_codes)
    got = spread(replies, grid)
    asked, _, *cots = lax.optimization_barrier((asked, replies, *cots))
    cots = cots + [send(x, grid.flip(1)) for x in cots]
    kept, sent = proj_part(place, asked, codebook, local_codes)
    proj = proj_split(place, kept, send(sent, grid.flip(1)))
    cotangent, _ = lax.optimization_barrier((cotangent, replies))
    gains = [send(x, grid.flip(bits)) for x, bits in zip(proj[1:], (2, 4, 6))]
    acc = group_weights(grid, place, got, cots, cap)
    own, *sends = pack(place, acc, [proj[0]] + gains)
    codes = got[:, cap:, 128:].reshape(slots, zch)
    codes, own, *sends = lax.optimization_barrier((codes, own, *sends))
    own, received = reduce_planes(grid, own, sends, r)
    quant = jnp.dot(onehot, codes, preferred_element_type=jnp.float32).astype(jnp.bfloat16)
    quant = quant.reshape(images, rows, width, zch)
    quant_f = quant.astype(jnp.float32)
    latent_f = latents.astype(jnp.float32)
    padded = jnp.pad(quant, ((0, 0), (1, 1), (1, 1), (0, 0)))
    padded_grad = jnp.pad(cotangent, ((0, 0), (1, 1), (1, 1), (0, 0)))
    output = jnp.zeros((images, rows, width, channels), jnp.float32)
    grad_input = jnp.zeros((images, rows, width, zch), jnp.float32)
    for row_off in range(3):
        for col_off in range(3):
            window = padded[:, row_off : row_off + rows, col_off : col_off + width]
            output = output + jnp.einsum(
                "nhwc,co->nhwo",
                window,
                kernel[row_off, col_off],
                preferred_element_type=jnp.float32,
            )
            grad_window = padded_grad[
                :, 2 - row_off : 2 - row_off + rows, 2 - col_off : 2 - col_off + width
            ]
            grad_input = grad_input + jnp.einsum(
                "nhwo,co->nhwc",
                grad_window,
                kernel[row_off, col_off],
                preferred_element_type=jnp.float32,
            )
    hidden = (output + bias.astype(jnp.float32)).astype(jnp.bfloat16)
    grad_latents = (grad_input + 2.0 * commit_weight * (latent_f - quant_f)).astype(jnp.bfloat16)
    krows = 9 * zch // 8
    planes = gather_planes(grid, combine(krows, own, received))
    *planes, hidden, grad_latents = lax.optimization_barrier((*planes, hidden, grad_latents))
    blocks = gather_places(grid, *planes)
    kernel_step, proj_step, bias_step = finish(place, blocks, zch, channels, feat)
    kernel_step = kernel_step.reshape(3, 3, zch, channels)
    return (hidden, grad_latents, proj_step, kernel_step, bias_step.reshape(channels))


def solution(mesh):
    grid = Grid(mesh.shape["dp"], mesh.shape["code"])
    in_specs = (
        P(("dp", "code"), None),
        P(),
        P(("dp", "code"), None, None, None),
        P(("dp", "code"), None, None),
        P(("dp", "code"), None),
        P(("dp", "code"), None, None),
        P(),
        P(),
        P(("dp", "code"), None, None, None),
    )
    out_specs = (
        P(("dp", "code"), None, None, None),
        P(("dp", "code"), None, None, None),
        P(),
        P(),
        P(),
    )
    return jax.shard_map(
        functools.partial(on_device, grid),
        mesh=mesh,
        in_specs=in_specs,
        out_specs=out_specs,
        check_vma=False,
    )
```

```python
import functools

import jax
import jax.numpy as jnp
from jax import lax
from jax.experimental import pallas as pl
from jax.experimental.pallas import tpu as pltpu
from jax.sharding import PartitionSpec as P

commit_weight = 0.25
norm_eps = 1e-06
AXES = ("dp", "code")
PARTS = 4


class Grid:
    def __init__(self, n_dp, n_code):
        self.n_dp, self.n_code = n_dp, n_code
        self.outer = n_code // 4
        self.planes = (n_dp // 2) * self.outer
        self.total = n_dp * n_code

    def linear(self, r, i):
        dh, ch = r // self.outer, r % self.outer
        return (dh * 2 + i // 4) * self.n_code + ch * 4 + i % 4

    def perm(self, move):
        return [
            (self.linear(r, i), self.linear(*move(r, i)))
            for r in range(self.planes)
            for i in range(8)
        ]

    def flip(self, bit):
        return self.perm(lambda r, i: (r, i ^ bit))

    def turn(self, k):
        return self.perm(lambda r, i: (r // PARTS * PARTS + (r + k) % PARTS, i))

    def far(self, k):
        groups = self.planes // PARTS
        return self.perm(lambda r, i: ((r // PARTS + k) % groups * PARTS + r % PARTS, i))

    def order(self, x):
        rest = x.shape[2:]
        x = x.reshape(self.n_dp // 2, self.outer, 2, 4, *rest)
        return jnp.swapaxes(x, 1, 2).reshape(self.total, *rest)

    def place(self):
        dp, code = lax.axis_index("dp"), lax.axis_index("code")
        return (dp // 2) * self.outer + code // 4, (dp % 2) * 4 + code % 4


def send(x, perm):
    return lax.ppermute(x, AXES, perm)


def gather_planes(grid, own):
    zs = [send(own, grid.turn(k)) for k in range(1, PARTS)]
    x, y = send(own, grid.flip(2)), send(own, grid.flip(4))
    early = jnp.stack([own, x, y, send(x, grid.flip(4))])
    zs = jnp.stack(zs)
    return early, zs, send(zs, grid.flip(2)), send(zs, grid.flip(4))


def gather_places(grid, early, zs, xs, ys):
    second, first = send(ys[:2], grid.flip(2)), send(xs[2:], grid.flip(4))
    mine = [early, jnp.concatenate([zs, xs, ys]), jnp.concatenate([second, first])]
    return mine + [send(x, grid.flip(1)) for x in mine]


def vmem(count):
    return [pl.BlockSpec(memory_space=pltpu.VMEM)] * count


SMEM_SPEC = pl.BlockSpec(memory_space=pltpu.SMEM)
LIMIT = pltpu.CompilerParams(vmem_limit_bytes=40 << 20)


def cost(flops, nbytes):
    return pl.CostEstimate(flops=flops, bytes_accessed=nbytes, transcendentals=0)


def spread(x, grid):
    return lax.all_to_all(x, AXES, split_axis=0, concat_axis=0, tiled=True)


def token_slots(cap, pick, counts):
    lines, width = pick.shape
    devices = counts.shape[1]
    tokens = lines * width
    owner = pick // cap
    first = pick - owner * cap
    token = lax.broadcasted_iota(jnp.int32, (width, tokens), 1)
    wide = (token % width == lax.broadcasted_iota(jnp.int32, (width, tokens), 0)).astype(jnp.float32)
    wide = wide.astype(jnp.bfloat16)
    token = lax.broadcasted_iota(jnp.int32, (lines, tokens), 1)
    keep = token // width == lax.broadcasted_iota(jnp.int32, (lines, tokens), 0)

    def flat(x):
        x = x.astype(jnp.float32).astype(jnp.bfloat16)
        x = jnp.dot(x, wide, preferred_element_type=jnp.float32)
        return jnp.sum(jnp.where(keep, x, 0.0), axis=0, keepdims=True)

    owner, entry = flat(owner), flat(first)
    row = lax.broadcasted_iota(jnp.int32, (devices, devices), 0)
    col = lax.broadcasted_iota(jnp.int32, (devices, devices), 1)
    counts = jnp.where(row == col, counts.astype(jnp.float32), 0.0)
    counts = jnp.sum(counts, axis=1, keepdims=True)
    owner_id = lax.broadcasted_iota(jnp.int32, (devices, tokens), 0)
    count = jnp.sum(
        jnp.where(owner_id == owner.astype(jnp.int32), counts, 0.0), axis=0, keepdims=True
    )
    for _ in range(cap - 1):
        entry = jnp.where(entry >= count, entry - count, entry)
    return owner, entry


def fetch(sources, targets, sems):
    copies = [
        pltpu.make_async_copy(source, target, sems.at[n])
        for n, (source, target) in enumerate(zip(sources, targets))
    ]
    for copy in copies:
        copy.start()
    for copy in copies:
        copy.wait()


def token_kernel(cap, pick_hbm, counts_hbm, wanted_hbm, latents_hbm, slot_ref, parts_ref, ask_ref, *rest):
    pick_ref, counts_ref, wanted_ref, latents_ref, sems = rest
    fetch((pick_hbm, counts_hbm, wanted_hbm, latents_hbm), rest[:-1], sems)
    owner, entry = token_slots(cap, pick_ref[...], counts_ref[...])
    tokens, devices = owner.shape[1], counts_ref.shape[1]
    slots = devices * cap
    slot = (owner * cap + entry).astype(jnp.int32)
    slot_ref[...] = slot
    row = lax.broadcasted_iota(jnp.int32, (8, tokens), 0)
    parts_ref[...] = jnp.where(row == 0, owner, jnp.where(row == 1, entry, 0.0))
    hit = (lax.broadcasted_iota(jnp.int32, (slots, tokens), 0) == slot).astype(jnp.float32)
    uses = jnp.sum(hit, axis=1, keepdims=True)
    sums = jnp.dot(hit.astype(jnp.bfloat16), latents_ref[...], preferred_element_type=jnp.float32)
    zch = sums.shape[1]
    wanted = wanted_ref[...].astype(jnp.float32).T
    wanted = jnp.broadcast_to(wanted[:, None, :], (devices, cap, cap)).reshape(slots, cap)
    place = lax.broadcasted_iota(jnp.int32, (slots, cap), 0) % cap
    lane = lax.broadcasted_iota(jnp.int32, (slots, cap), 1)
    wanted = jnp.sum(jnp.where(lane == place, wanted, 0.0), axis=1, keepdims=True)
    lane = lax.broadcasted_iota(jnp.int32, (slots, 128), 1)
    last = jnp.where(lane == 0, uses, jnp.where(lane == 1, wanted, 0.0))
    ask_ref[:, :, :zch] = sums.reshape(devices, cap, zch)
    ask_ref[:, :, zch:] = last.reshape(devices, cap, 128)


def token_part(pick, counts, wanted, latents):
    cap, devices = wanted.shape
    tokens = pick.shape[0] * pick.shape[1]
    slots = devices * cap
    return pl.pallas_call(
        functools.partial(token_kernel, cap),
        out_shape=(
            jax.ShapeDtypeStruct((1, tokens), jnp.int32),
            jax.ShapeDtypeStruct((8, tokens), jnp.float32),
            jax.ShapeDtypeStruct((devices, cap, latents.shape[1] + 128), jnp.float32),
        ),
        in_specs=[pl.BlockSpec(memory_space=pltpu.HBM)] * 4,
        out_specs=tuple(vmem(3)),
        scratch_shapes=[pltpu.VMEM(x.shape, x.dtype) for x in (pick, counts, wanted, latents)]
        + [pltpu.SemaphoreType.DMA((4,))],
        compiler_params=pltpu.CompilerParams(vmem_limit_bytes=62 << 20),
        cost_estimate=cost(2 * slots * tokens * latents.shape[1], 2 << 20),
    )(pick, counts, wanted, latents)


def block_kernel(parts_ref, cot_ref, near_ref, far_ref):
    tokens, channels = cot_ref.shape
    wide = channels // 2
    place = lax.broadcasted_iota(jnp.int32, (16, wide), 0)
    extra = jnp.zeros((16, wide), jnp.float32)
    rows = [parts_ref[n : n + 1, m * wide : (m + 1) * wide] for n in range(2) for m in range(2)]
    for n, row in enumerate(rows):
        extra = jnp.where(place == n, row, extra)
    side = lax.axis_index("dp") % 2
    for ref, side in ((near_ref, side), (far_ref, 1 - side)):
        ref[:tokens] = cot_ref[:, pl.ds(pl.multiple_of(side * wide, wide), wide)]
        ref[tokens:] = extra.astype(jnp.bfloat16)


def block_part(parts, cots):
    tokens, channels = cots.shape
    return pl.pallas_call(
        block_kernel,
        out_shape=(jax.ShapeDtypeStruct((tokens + 16, channels // 2), jnp.bfloat16),) * 2,
        in_specs=vmem(2),
        out_specs=tuple(vmem(2)),
        compiler_params=LIMIT,
        cost_estimate=cost(0, 1 << 20),
    )(parts, cots)


def select_rows(asked, zch, entries):
    column = asked[:, zch + 1 : zch + 2].astype(jnp.int32)
    hit = column == lax.broadcasted_iota(jnp.int32, (asked.shape[0], entries), 1)
    return hit.astype(jnp.float32).astype(jnp.bfloat16)


def answer_kernel(grid, cap, asked_ref, codes_ref, out_ref):
    devices = grid.total
    entries, zch = codes_ref.shape
    select = select_rows(asked_ref[...].reshape(devices * cap, zch + 128), zch, entries)
    codes = jnp.dot(select, codes_ref[...], preferred_element_type=jnp.float32)
    whole = codes.reshape(devices, cap, zch)
    second = lax.broadcasted_iota(jnp.int32, (cap, 128), 1) >= 64
    turned = {}
    for v in range(2):
        part = codes[:, v * 128 : (v + 1) * 128]
        turned[v, 0] = part.reshape(devices, cap, 128)
        turned[v, 1] = pltpu.roll(part, 64, 1).reshape(devices, cap, 128)
    for r in range(grid.planes):
        for u in range(4):
            v, a = u // 2, u % 2
            slices = [
                jnp.where(
                    second,
                    turned[v, 1 - a][grid.linear(r, 2 * h + 1)],
                    turned[v, a][grid.linear(r, 2 * h)],
                )
                for h in range(4)
            ]
            for dest in (grid.linear(r, u), grid.linear(r, u + 4)):
                top = jnp.concatenate(slices[:3], axis=1)
                bottom = jnp.concatenate([slices[3], whole[dest]], axis=1)
                out_ref[dest] = jnp.concatenate([top, bottom], axis=0).astype(jnp.bfloat16)


def answer(grid, asked, codes):
    devices, cap, _ = asked.shape
    zch = codes.shape[1]
    return pl.pallas_call(
        functools.partial(answer_kernel, grid, cap),
        out_shape=jax.ShapeDtypeStruct((devices, 2 * cap, 384), jnp.bfloat16),
        in_specs=vmem(2),
        out_specs=vmem(1)[0],
        compiler_params=LIMIT,
        cost_estimate=cost(2 * devices * cap * codes.shape[0] * zch, 2 << 20),
    )(asked, codes)


def proj_kernel(place_ref, asked_ref, book_ref, codes_ref, keep_ref, send_ref, all_ref):
    entries, feat = book_ref.shape
    zch = codes_ref.shape[1]
    devices, cap, _ = asked_ref.shape
    asked = asked_ref[...].reshape(devices * cap, zch + 128)
    select = select_rows(asked, zch, entries)
    codes = jnp.dot(select, codes_ref[...], preferred_element_type=jnp.float32)
    rows = jnp.dot(select, book_ref[...], preferred_element_type=jnp.float32).astype(jnp.bfloat16)
    grads = 2.0 * (asked[:, zch : zch + 1] * codes - asked[:, :zch])
    upper = grads.astype(jnp.bfloat16)
    lower = (grads - upper.astype(jnp.float32)).astype(jnp.bfloat16)
    dims = (((0,), (0,)), ((), ()))
    total = lax.dot_general(rows, upper, dims, preferred_element_type=jnp.float32)
    all_ref[...] = total + lax.dot_general(rows, lower, dims, preferred_element_type=jnp.float32)
    core = place_ref[0] % 2
    keep_ref[...] = all_ref[:, pl.ds(pl.multiple_of(core * 128, 128), 128)]
    send_ref[...] = all_ref[:, pl.ds(pl.multiple_of((1 - core) * 128, 128), 128)]


def proj_part(place, asked, book, codes):
    feat, zch = book.shape[1], codes.shape[1]
    slots = asked.shape[0] * asked.shape[1]
    return pl.pallas_call(
        proj_kernel,
        out_shape=(jax.ShapeDtypeStruct((feat, 128), jnp.float32),) * 2,
        in_specs=[SMEM_SPEC] + vmem(3),
        out_specs=tuple(vmem(2)),
        scratch_shapes=[pltpu.VMEM((feat, zch), jnp.float32)],
        compiler_params=LIMIT,
        cost_estimate=cost(2 * slots * (book.shape[0] + 2 * zch) * feat, 4 << 20),
    )(place, asked, book, codes)


def proj_split_kernel(place_ref, kept_ref, got_ref, own_ref, *rest):
    send_refs, all_ref = rest[:-1], rest[-1]
    all_ref[...] = kept_ref[...] + got_ref[...]
    i = place_ref[0]
    size = all_ref.shape[0] // 4

    def quarter(place):
        start = (place // 2 % 2 * 2 + place // 4) * size
        return all_ref[pl.ds(pl.multiple_of(start, 8), size), :].reshape(own_ref.shape)

    own_ref[...] = quarter(i)
    for bits, send_ref in zip((2, 4, 6), send_refs):
        send_ref[...] = quarter(i ^ bits).astype(jnp.bfloat16)


def proj_split(place, kept, got):
    shape = (PARTS, kept.shape[0] // 16, 128)
    return pl.pallas_call(
        proj_split_kernel,
        out_shape=[jax.ShapeDtypeStruct(shape, jnp.float32)]
        + [jax.ShapeDtypeStruct(shape, jnp.bfloat16)] * 3,
        in_specs=[SMEM_SPEC] + vmem(2),
        out_specs=vmem(4),
        scratch_shapes=[pltpu.VMEM(kept.shape, jnp.float32)],
        compiler_params=LIMIT,
    )(place, kept, got)


def proj_place(i, q, prows):
    return (((i // 2) % 2) * 2 + i // 4) * PARTS * prows + q * prows, i % 2


def weights_kernel(grid, cap, place_ref, got_ref, *refs):
    cots, (acc_ref, xt_ref) = refs[:8], refs[8:]
    devices = grid.total
    slots = devices * cap
    tokens, channels = cots[0].shape
    tokens -= 16
    cut = tokens // 2
    i, part = place_ref[0], place_ref[1]
    got = got_ref[...].astype(jnp.float32)
    xt_ref[:384] = got[:, :cap].reshape(slots, 384).T
    xt_ref[384:] = got[:, cap:, :128].reshape(slots, 128).T
    wide = 64
    krows = 9 * wide // 2
    token = lax.broadcasted_iota(jnp.int32, (1, tokens), 1)
    line, cell = token // 16 % 16, token % 16
    slot_id = lax.broadcasted_iota(jnp.int32, (slots, tokens), 0)
    ones = (lax.broadcasted_iota(jnp.int32, (16, tokens), 0) == 0).astype(jnp.float32)
    cots = {j: cots[j % 2 * 4 + j // 2] for j in range(8)}
    for j in range(8):
        member = i ^ j
        xt = xt_ref[pl.ds(pl.multiple_of(member * wide, wide), wide), :].astype(jnp.bfloat16)
        last = cots[j][tokens:].astype(jnp.float32)
        last = last[0:2] * cap + last[2:4]
        slot = jnp.concatenate([last[0:1], last[1:2]], axis=1).astype(jnp.int32)
        hit = (slot_id == slot).astype(jnp.float32).astype(jnp.bfloat16)
        quant = jnp.dot(xt, hit, preferred_element_type=jnp.float32)
        taps = []
        for down in (-1, 0, 1):
            for right in (-1, 0, 1):
                shift = (-(down * 16 + right)) % tokens
                moved = quant if shift == 0 else pltpu.roll(quant, shift, 1)
                valid = (line + down >= 0) & (line + down < 16) & (cell + right >= 0) & (cell + right < 16)
                taps.append(moved * valid.astype(jnp.float32))
        taps = [x[: wide // 2] for x in taps] + [x[wide // 2 :] for x in taps]
        left = jnp.concatenate(taps + [ones], axis=0).astype(jnp.bfloat16)
        value = jnp.dot(left, cots[j][:tokens], preferred_element_type=jnp.float32)
        if j == 0:
            acc_ref[...] = value
        else:
            acc_ref[...] += value


def pack_kernel(krows, place_ref, acc_ref, *refs):
    proj_refs, (own_ref, *send_refs) = refs[:4], refs[4:]
    part = place_ref[1]

    def proj(q):
        return sum(ref[q].astype(jnp.float32) for ref in proj_refs)

    def piece(q):
        lanes = pl.ds(pl.multiple_of(q % 2 * 128, 128), 128)
        rows = pl.ds(pl.multiple_of(q // 2 * krows, 8), krows)
        return acc_ref[rows, lanes], acc_ref[2 * krows :, lanes]

    own_ref[:krows], own_ref[krows : krows + 16] = piece(part)
    own_ref[krows + 16 :] = proj(part)
    row = lax.broadcasted_iota(jnp.int32, (16, 128), 0)
    for k, send_ref in enumerate(send_refs, 1):
        value, last = piece((part + k) % PARTS)
        upper = last.astype(jnp.bfloat16).astype(jnp.float32)
        lower = (last - upper)[0:1]
        send_ref[:krows] = value.astype(jnp.bfloat16)
        send_ref[krows : krows + 16] = jnp.where(row == 1, lower, last).astype(jnp.bfloat16)
        send_ref[krows + 16 :] = proj((part + k) % PARTS).astype(jnp.bfloat16)


def group_weights(grid, place, got, cots, cap):
    channels = cots[0].shape[1]
    slots = grid.total * cap
    return pl.pallas_call(
        functools.partial(weights_kernel, grid, cap),
        out_shape=jax.ShapeDtypeStruct((9 * 64 + 16, channels), jnp.float32),
        in_specs=[SMEM_SPEC] + vmem(9),
        out_specs=vmem(1)[0],
        scratch_shapes=[pltpu.VMEM((512, slots), jnp.float32)],
        compiler_params=LIMIT,
        cost_estimate=cost(2 * 9 * 512 * 512 * channels, 8 << 20),
    )(place, got, *cots)


def pack(place, acc, proj):
    krows = (acc.shape[0] - 16) // 2
    height = krows + 16 + proj[0].shape[1]
    return pl.pallas_call(
        functools.partial(pack_kernel, krows),
        out_shape=[jax.ShapeDtypeStruct((height, 128), jnp.float32)]
        + [jax.ShapeDtypeStruct((height, 128), jnp.bfloat16)] * (PARTS - 1),
        in_specs=[SMEM_SPEC] + vmem(5),
        out_specs=vmem(PARTS),
        compiler_params=LIMIT,
    )(place, acc, *proj)


def combine_kernel(krows, own_ref, *refs):
    got_refs, out_ref = refs[:-1], refs[-1]
    total = own_ref[...]
    for ref in got_refs:
        total = total + ref[...].astype(jnp.float32)
    kernel = total[:krows]
    proj = total[krows + 16 :]
    bias = total[krows : krows + 1] + total[krows + 1 : krows + 2]
    row = lax.broadcasted_iota(jnp.int32, (16, own_ref.shape[1]), 0)
    extra = jnp.zeros(row.shape, jnp.float32)
    sums = (
        bias,
        jnp.sum(kernel * kernel, axis=0, keepdims=True),
        jnp.sum(proj * proj, axis=0, keepdims=True),
    )
    for n, value in enumerate(sums):
        upper = value.astype(jnp.bfloat16).astype(jnp.float32)
        middle = (value - upper).astype(jnp.bfloat16).astype(jnp.float32)
        for k, piece in enumerate((upper, middle, value - upper - middle)):
            extra = jnp.where(row == 3 * n + k, piece, extra)
    out_ref[:krows] = kernel.astype(jnp.bfloat16)
    out_ref[krows : krows + 16] = extra.astype(jnp.bfloat16)
    out_ref[krows + 16 :] = proj.astype(jnp.bfloat16)


def combine(krows, own, got):
    return pl.pallas_call(
        functools.partial(combine_kernel, krows),
        out_shape=jax.ShapeDtypeStruct(own.shape, jnp.bfloat16),
        in_specs=vmem(1 + len(got)),
        out_specs=vmem(1)[0],
        compiler_params=LIMIT,
    )(own, *got)


def reduce_planes(grid, own, sends, r):
    got = [send(s, grid.turn(k)) for k, s in enumerate(sends, 1)]
    groups = grid.planes // PARTS
    if groups > 1:
        own = own + sum(g.astype(jnp.float32) for g in got)
        rest = [own] + [send(own, grid.far(k)) for k in range(1, groups)]
        order = (r // PARTS - jnp.arange(groups)) % groups
        own = jnp.sum(jnp.take(jnp.stack(rest), order, axis=0), axis=0)
        got = []
    return own, got


def finish_kernel(krows, counts, place_ref, *refs):
    (kernel_ref, proj_ref, bias_ref, keep_ref), refs = refs[6:], refs[:6]
    i, part = place_ref[0], place_ref[1]
    wide = krows // 9
    prows = refs[0].shape[1] - krows - 16
    sources = []
    near = [(n, 2 * n, 0) for n in range(4)]
    middle = [(n, n // 3 * 2, n % 3 + 1) for n in range(9)]
    last = [(n, 6, n + 1) for n in range(3)]
    for m, ref in enumerate(refs):
        for n, bits, turn in (near, middle, last)[m % 3]:
            place = i ^ (bits + m // 3)
            q = (part + PARTS - turn) % PARTS
            sources.append((ref, n, place, q))
            keep_ref[place * PARTS + q] = ref[n, krows : krows + 16].astype(jnp.float32)
    kept = jnp.sum(keep_ref[...], axis=0)

    def factor(values, count):
        total = jnp.sum(jnp.sum(values, axis=0, keepdims=True), axis=1, keepdims=True)
        return 1.0 / jnp.sqrt(total / count + norm_eps)

    kfactor, pfactor = factor(kept[3:6], counts[0]), factor(kept[6:9], counts[1])
    for ref, n, place, q in sources:
        value = ref[n].astype(jnp.float32)
        lanes = pl.ds(pl.multiple_of(place // 4 * 256 + q % 2 * 128, 128), 128)
        start = place % 4 * 64 + q // 2 * 32
        kernel_ref[:, pl.ds(pl.multiple_of(start, 32), wide), lanes] = (
            value[:krows] * kfactor
        ).reshape(9, wide, 128)
        row, col = proj_place(place, q, prows)
        proj_ref[pl.ds(pl.multiple_of(row, 8), prows), pl.ds(pl.multiple_of(col * 128, 128), 128)] = (
            value[krows + 16 :] * pfactor
        )
    bias = [jnp.sum(keep_ref[n, 0:3], axis=0, keepdims=True) for n in (0, 1, 16, 17)]
    bias = jnp.concatenate(bias, axis=1)
    bias_ref[...] = bias * factor(bias * bias, counts[2])


def finish(place, blocks, zch, channels, feat):
    krows = 9 * zch // 8
    counts = (9 * zch * channels, feat * zch, channels)
    return pl.pallas_call(
        functools.partial(finish_kernel, krows, counts),
        out_shape=(
            jax.ShapeDtypeStruct((9, zch, channels), jnp.float32),
            jax.ShapeDtypeStruct((feat, zch), jnp.float32),
            jax.ShapeDtypeStruct((1, channels), jnp.float32),
        ),
        in_specs=[SMEM_SPEC] + vmem(6),
        out_specs=tuple(vmem(3)),
        scratch_shapes=[pltpu.VMEM((32, 16, 128), jnp.float32)],
        compiler_params=LIMIT,
    )(place, *blocks)


def gather_near(grid, near, far):
    return [near, send(near, grid.flip(2)), send(far, grid.flip(4)), send(far, grid.flip(6))]


def on_device(
    grid, codebook, projector, latents, wanted, wanted_count, token_pick, kernel, bias, cotangent
):
    devices = grid.total
    images, rows, width, zch = latents.shape
    channels = kernel.shape[3]
    feat = codebook.shape[1]
    cap = wanted.shape[2]
    slots = devices * cap
    tokens = images * rows * width
    r, i = grid.place()
    place = jnp.stack([i, r % PARTS]).astype(jnp.int32)
    slot, parts, ask = token_part(
        token_pick.reshape(images * rows, width),
        wanted_count,
        jnp.swapaxes(wanted.reshape(devices, cap), 0, 1),
        latents.reshape(tokens, zch),
    )
    near, far = block_part(parts, cotangent.reshape(tokens, channels))
    asked = spread(ask, grid)
    cots = gather_near(grid, near, far)
    local_codes = jnp.dot(codebook, projector, preferred_element_type=jnp.float32).astype(
        jnp.bfloat16
    )
    slot_ids = jnp.arange(slots, dtype=jnp.int32)
    onehot = (slot.reshape(tokens, 1) == slot_ids[None, :]).astype(jnp.bfloat16)
    replies = answer(grid, asked, local_codes)
    got = spread(replies, grid)
    asked, _, *cots = lax.optimization_barrier((asked, replies, *cots))
    cots = cots + [send(x, grid.flip(1)) for x in cots]
    kept, sent = proj_part(place, asked, codebook, local_codes)
    proj = proj_split(place, kept, send(sent, grid.flip(1)))
    cotangent, _ = lax.optimization_barrier((cotangent, replies))
    gains = [send(x, grid.flip(bits)) for x, bits in zip(proj[1:], (2, 4, 6))]
    acc = group_weights(grid, place, got, cots, cap)
    own, *sends = pack(place, acc, [proj[0]] + gains)
    codes = got[:, cap:, 128:].reshape(slots, zch)
    codes, own, *sends = lax.optimization_barrier((codes, own, *sends))
    own, received = reduce_planes(grid, own, sends, r)
    quant = jnp.dot(onehot, codes, preferred_element_type=jnp.float32).astype(jnp.bfloat16)
    quant = quant.reshape(images, rows, width, zch)
    quant_f = quant.astype(jnp.float32)
    latent_f = latents.astype(jnp.float32)
    padded = jnp.pad(quant, ((0, 0), (1, 1), (1, 1), (0, 0)))
    padded_grad = jnp.pad(cotangent, ((0, 0), (1, 1), (1, 1), (0, 0)))
    output = jnp.zeros((images, rows, width, channels), jnp.float32)
    grad_input = jnp.zeros((images, rows, width, zch), jnp.float32)
    for row_off in range(3):
        for col_off in range(3):
            window = padded[:, row_off : row_off + rows, col_off : col_off + width]
            output = output + jnp.einsum(
                "nhwc,co->nhwo",
                window,
                kernel[row_off, col_off],
                preferred_element_type=jnp.float32,
            )
            grad_window = padded_grad[
                :, 2 - row_off : 2 - row_off + rows, 2 - col_off : 2 - col_off + width
            ]
            grad_input = grad_input + jnp.einsum(
                "nhwo,co->nhwc",
                grad_window,
                kernel[row_off, col_off],
                preferred_element_type=jnp.float32,
            )
    hidden = (output + bias.astype(jnp.float32)).astype(jnp.bfloat16)
    grad_latents = (grad_input + 2.0 * commit_weight * (latent_f - quant_f)).astype(jnp.bfloat16)
    krows = 9 * zch // 8
    planes = gather_planes(grid, combine(krows, own, received))
    *planes, hidden, grad_latents = lax.optimization_barrier((*planes, hidden, grad_latents))
    blocks = gather_places(grid, *planes)
    kernel_step, proj_step, bias_step = finish(place, blocks, zch, channels, feat)
    kernel_step = kernel_step.reshape(3, 3, zch, channels)
    return (hidden, grad_latents, proj_step, kernel_step, bias_step.reshape(channels))


def solution(mesh):
    grid = Grid(mesh.shape["dp"], mesh.shape["code"])
    in_specs = (
        P(("dp", "code"), None),
        P(),
        P(("dp", "code"), None, None, None),
        P(("dp", "code"), None, None),
        P(("dp", "code"), None),
        P(("dp", "code"), None, None),
        P(),
        P(),
        P(("dp", "code"), None, None, None),
    )
    out_specs = (
        P(("dp", "code"), None, None, None),
        P(("dp", "code"), None, None, None),
        P(),
        P(),
        P(),
    )
    return jax.shard_map(
        functools.partial(on_device, grid),
        mesh=mesh,
        in_specs=in_specs,
        out_specs=out_specs,
        check_vma=False,
    )
```

```python
import functools

import jax
import jax.numpy as jnp
from jax import lax
from jax.experimental import pallas as pl
from jax.experimental.pallas import tpu as pltpu
from jax.sharding import PartitionSpec as P

commit_weight = 0.25
norm_eps = 1e-06
AXES = ("dp", "code")
PARTS = 4


class Grid:
    def __init__(self, n_dp, n_code):
        self.n_dp, self.n_code = n_dp, n_code
        self.outer = n_code // 4
        self.planes = (n_dp // 2) * self.outer
        self.total = n_dp * n_code

    def linear(self, r, i):
        dh, ch = r // self.outer, r % self.outer
        return (dh * 2 + i // 4) * self.n_code + ch * 4 + i % 4

    def perm(self, move):
        return [
            (self.linear(r, i), self.linear(*move(r, i)))
            for r in range(self.planes)
            for i in range(8)
        ]

    def flip(self, bit):
        return self.perm(lambda r, i: (r, i ^ bit))

    def turn(self, k):
        return self.perm(lambda r, i: (r // PARTS * PARTS + (r + k) % PARTS, i))

    def far(self, k):
        groups = self.planes // PARTS
        return self.perm(lambda r, i: ((r // PARTS + k) % groups * PARTS + r % PARTS, i))

    def order(self, x):
        rest = x.shape[2:]
        x = x.reshape(self.n_dp // 2, self.outer, 2, 4, *rest)
        return jnp.swapaxes(x, 1, 2).reshape(self.total, *rest)

    def place(self):
        dp, code = lax.axis_index("dp"), lax.axis_index("code")
        return (dp // 2) * self.outer + code // 4, (dp % 2) * 4 + code % 4


def send(x, perm):
    return lax.ppermute(x, AXES, perm)


def gather_planes(grid, own):
    zs = [send(own, grid.turn(k)) for k in range(1, PARTS)]
    x, y = send(own, grid.flip(2)), send(own, grid.flip(4))
    early = jnp.stack([own, x, y, send(own, grid.flip(6))])
    zs = jnp.stack(zs)
    return early, zs, send(zs, grid.flip(2)), send(zs, grid.flip(4))


def gather_places(grid, early, zs, xs, ys):
    count, height, wide = zs.shape
    cut = count * height // 2
    second = send(ys.reshape(-1, wide)[:cut], grid.flip(2))
    first = send(xs.reshape(-1, wide)[cut:], grid.flip(4))
    last = jnp.concatenate([second, first]).reshape(zs.shape)
    mine = [early, jnp.concatenate([zs, xs, ys]), last]
    return mine + [send(x, grid.flip(1)) for x in mine]


def vmem(count):
    return [pl.BlockSpec(memory_space=pltpu.VMEM)] * count


SMEM_SPEC = pl.BlockSpec(memory_space=pltpu.SMEM)
LIMIT = pltpu.CompilerParams(vmem_limit_bytes=40 << 20)


def cost(flops, nbytes):
    return pl.CostEstimate(flops=flops, bytes_accessed=nbytes, transcendentals=0)


def spread(x, grid):
    return lax.all_to_all(x, AXES, split_axis=0, concat_axis=0, tiled=True)


def token_slots(cap, pick, counts):
    lines, width = pick.shape
    devices = counts.shape[1]
    tokens = lines * width
    owner = pick // cap
    first = pick - owner * cap
    token = lax.broadcasted_iota(jnp.int32, (width, tokens), 1)
    wide = (token % width == lax.broadcasted_iota(jnp.int32, (width, tokens), 0)).astype(jnp.float32)
    wide = wide.astype(jnp.bfloat16)
    token = lax.broadcasted_iota(jnp.int32, (lines, tokens), 1)
    keep = token // width == lax.broadcasted_iota(jnp.int32, (lines, tokens), 0)

    def flat(x):
        x = x.astype(jnp.float32).astype(jnp.bfloat16)
        x = jnp.dot(x, wide, preferred_element_type=jnp.float32)
        return jnp.sum(jnp.where(keep, x, 0.0), axis=0, keepdims=True)

    owner, entry = flat(owner), flat(first)
    row = lax.broadcasted_iota(jnp.int32, (devices, devices), 0)
    col = lax.broadcasted_iota(jnp.int32, (devices, devices), 1)
    counts = jnp.where(row == col, counts.astype(jnp.float32), 0.0)
    counts = jnp.sum(counts, axis=1, keepdims=True)
    owner_id = lax.broadcasted_iota(jnp.int32, (devices, tokens), 0)
    count = jnp.sum(
        jnp.where(owner_id == owner.astype(jnp.int32), counts, 0.0), axis=0, keepdims=True
    )
    for _ in range(cap - 1):
        entry = jnp.where(entry >= count, entry - count, entry)
    return owner, entry


def fetch(sources, targets, sems):
    copies = [
        pltpu.make_async_copy(source, target, sems.at[n])
        for n, (source, target) in enumerate(zip(sources, targets))
    ]
    for copy in copies:
        copy.start()
    for copy in copies:
        copy.wait()


def token_kernel(cap, pick_hbm, counts_hbm, wanted_hbm, latents_hbm, slot_ref, parts_ref, ask_ref, *rest):
    pick_ref, counts_ref, wanted_ref, latents_ref, sems = rest
    fetch((pick_hbm, counts_hbm, wanted_hbm, latents_hbm), rest[:-1], sems)
    owner, entry = token_slots(cap, pick_ref[...], counts_ref[...])
    tokens, devices = owner.shape[1], counts_ref.shape[1]
    slots = devices * cap
    slot = (owner * cap + entry).astype(jnp.int32)
    slot_ref[...] = slot
    row = lax.broadcasted_iota(jnp.int32, (8, tokens), 0)
    parts_ref[...] = jnp.where(row == 0, owner, jnp.where(row == 1, entry, 0.0))
    hit = (lax.broadcasted_iota(jnp.int32, (slots, tokens), 0) == slot).astype(jnp.float32)
    uses = jnp.sum(hit, axis=1, keepdims=True)
    sums = jnp.dot(hit.astype(jnp.bfloat16), latents_ref[...], preferred_element_type=jnp.float32)
    zch = sums.shape[1]
    wanted = wanted_ref[...].astype(jnp.float32).T
    wanted = jnp.broadcast_to(wanted[:, None, :], (devices, cap, cap)).reshape(slots, cap)
    place = lax.broadcasted_iota(jnp.int32, (slots, cap), 0) % cap
    lane = lax.broadcasted_iota(jnp.int32, (slots, cap), 1)
    wanted = jnp.sum(jnp.where(lane == place, wanted, 0.0), axis=1, keepdims=True)
    lane = lax.broadcasted_iota(jnp.int32, (slots, 128), 1)
    last = jnp.where(lane == 0, uses, jnp.where(lane == 1, wanted, 0.0))
    ask_ref[:, :, :zch] = sums.reshape(devices, cap, zch)
    ask_ref[:, :, zch:] = last.reshape(devices, cap, 128)


def token_part(pick, counts, wanted, latents):
    cap, devices = wanted.shape
    tokens = pick.shape[0] * pick.shape[1]
    slots = devices * cap
    return pl.pallas_call(
        functools.partial(token_kernel, cap),
        out_shape=(
            jax.ShapeDtypeStruct((1, tokens), jnp.int32),
            jax.ShapeDtypeStruct((8, tokens), jnp.float32),
            jax.ShapeDtypeStruct((devices, cap, latents.shape[1] + 128), jnp.float32),
        ),
        in_specs=[pl.BlockSpec(memory_space=pltpu.HBM)] * 4,
        out_specs=tuple(vmem(3)),
        scratch_shapes=[pltpu.VMEM(x.shape, x.dtype) for x in (pick, counts, wanted, latents)]
        + [pltpu.SemaphoreType.DMA((4,))],
        compiler_params=pltpu.CompilerParams(vmem_limit_bytes=62 << 20),
        cost_estimate=cost(2 * slots * tokens * latents.shape[1], 2 << 20),
    )(pick, counts, wanted, latents)


def block_kernel(parts_ref, cot_ref, near_ref, far_ref):
    tokens, channels = cot_ref.shape
    wide = channels // 2
    place = lax.broadcasted_iota(jnp.int32, (16, wide), 0)
    extra = jnp.zeros((16, wide), jnp.float32)
    rows = [parts_ref[n : n + 1, m * wide : (m + 1) * wide] for n in range(2) for m in range(2)]
    for n, row in enumerate(rows):
        extra = jnp.where(place == n, row, extra)
    side = lax.axis_index("dp") % 2
    for ref, side in ((near_ref, side), (far_ref, 1 - side)):
        ref[:tokens] = cot_ref[:, pl.ds(pl.multiple_of(side * wide, wide), wide)]
        ref[tokens:] = extra.astype(jnp.bfloat16)


def block_part(parts, cots):
    tokens, channels = cots.shape
    return pl.pallas_call(
        block_kernel,
        out_shape=(jax.ShapeDtypeStruct((tokens + 16, channels // 2), jnp.bfloat16),) * 2,
        in_specs=vmem(2),
        out_specs=tuple(vmem(2)),
        compiler_params=LIMIT,
        cost_estimate=cost(0, 1 << 20),
    )(parts, cots)


def select_rows(asked, zch, entries):
    column = asked[:, zch + 1 : zch + 2].astype(jnp.int32)
    hit = column == lax.broadcasted_iota(jnp.int32, (asked.shape[0], entries), 1)
    return hit.astype(jnp.float32).astype(jnp.bfloat16)


def answer_kernel(grid, cap, asked_ref, codes_ref, out_ref):
    devices = grid.total
    entries, zch = codes_ref.shape
    select = select_rows(asked_ref[...].reshape(devices * cap, zch + 128), zch, entries)
    codes = jnp.dot(select, codes_ref[...], preferred_element_type=jnp.float32)
    whole = codes.reshape(devices, cap, zch)
    second = lax.broadcasted_iota(jnp.int32, (cap, 128), 1) >= 64
    turned = {}
    for v in range(2):
        part = codes[:, v * 128 : (v + 1) * 128]
        turned[v, 0] = part.reshape(devices, cap, 128)
        turned[v, 1] = pltpu.roll(part, 64, 1).reshape(devices, cap, 128)
    for r in range(grid.planes):
        for u in range(4):
            v, a = u // 2, u % 2
            slices = [
                jnp.where(
                    second,
                    turned[v, 1 - a][grid.linear(r, 2 * h + 1)],
                    turned[v, a][grid.linear(r, 2 * h)],
                )
                for h in range(4)
            ]
            for dest in (grid.linear(r, u), grid.linear(r, u + 4)):
                top = jnp.concatenate(slices[:3], axis=1)
                bottom = jnp.concatenate([slices[3], whole[dest]], axis=1)
                out_ref[dest] = jnp.concatenate([top, bottom], axis=0).astype(jnp.bfloat16)


def answer(grid, asked, codes):
    devices, cap, _ = asked.shape
    zch = codes.shape[1]
    return pl.pallas_call(
        functools.partial(answer_kernel, grid, cap),
        out_shape=jax.ShapeDtypeStruct((devices, 2 * cap, 384), jnp.bfloat16),
        in_specs=vmem(2),
        out_specs=vmem(1)[0],
        compiler_params=LIMIT,
        cost_estimate=cost(2 * devices * cap * codes.shape[0] * zch, 2 << 20),
    )(asked, codes)


def proj_kernel(place_ref, asked_ref, book_ref, codes_ref, keep_ref, send_ref, all_ref):
    entries, feat = book_ref.shape
    zch = codes_ref.shape[1]
    devices, cap, _ = asked_ref.shape
    asked = asked_ref[...].reshape(devices * cap, zch + 128)
    select = select_rows(asked, zch, entries)
    codes = jnp.dot(select, codes_ref[...], preferred_element_type=jnp.float32)
    rows = jnp.dot(select, book_ref[...], preferred_element_type=jnp.float32).astype(jnp.bfloat16)
    grads = 2.0 * (asked[:, zch : zch + 1] * codes - asked[:, :zch])
    upper = grads.astype(jnp.bfloat16)
    lower = (grads - upper.astype(jnp.float32)).astype(jnp.bfloat16)
    dims = (((0,), (0,)), ((), ()))
    total = lax.dot_general(rows, upper, dims, preferred_element_type=jnp.float32)
    all_ref[...] = total + lax.dot_general(rows, lower, dims, preferred_element_type=jnp.float32)
    core = place_ref[0] % 2
    keep_ref[...] = all_ref[:, pl.ds(pl.multiple_of(core * 128, 128), 128)]
    send_ref[...] = all_ref[:, pl.ds(pl.multiple_of((1 - core) * 128, 128), 128)]


def proj_part(place, asked, book, codes):
    feat, zch = book.shape[1], codes.shape[1]
    slots = asked.shape[0] * asked.shape[1]
    return pl.pallas_call(
        proj_kernel,
        out_shape=(jax.ShapeDtypeStruct((feat, 128), jnp.float32),) * 2,
        in_specs=[SMEM_SPEC] + vmem(3),
        out_specs=tuple(vmem(2)),
        scratch_shapes=[pltpu.VMEM((feat, zch), jnp.float32)],
        compiler_params=LIMIT,
        cost_estimate=cost(2 * slots * (book.shape[0] + 2 * zch) * feat, 4 << 20),
    )(place, asked, book, codes)


def proj_split_kernel(place_ref, kept_ref, got_ref, own_ref, *rest):
    send_refs, all_ref = rest[:-1], rest[-1]
    all_ref[...] = kept_ref[...] + got_ref[...]
    i = place_ref[0]
    size = all_ref.shape[0] // 4

    def quarter(place):
        start = (place // 2 % 2 * 2 + place // 4) * size
        return all_ref[pl.ds(pl.multiple_of(start, 8), size), :].reshape(own_ref.shape)

    own_ref[...] = quarter(i)
    for bits, send_ref in zip((2, 4, 6), send_refs):
        send_ref[...] = quarter(i ^ bits).astype(jnp.bfloat16)


def proj_split(place, kept, got):
    shape = (PARTS, kept.shape[0] // 16, 128)
    return pl.pallas_call(
        proj_split_kernel,
        out_shape=[jax.ShapeDtypeStruct(shape, jnp.float32)]
        + [jax.ShapeDtypeStruct(shape, jnp.bfloat16)] * 3,
        in_specs=[SMEM_SPEC] + vmem(2),
        out_specs=vmem(4),
        scratch_shapes=[pltpu.VMEM(kept.shape, jnp.float32)],
        compiler_params=LIMIT,
    )(place, kept, got)


def proj_place(i, q, prows):
    return (((i // 2) % 2) * 2 + i // 4) * PARTS * prows + q * prows, i % 2


def weights_kernel(grid, cap, place_ref, got_ref, *refs):
    cots, (acc_ref, xt_ref) = refs[:8], refs[8:]
    devices = grid.total
    slots = devices * cap
    tokens, channels = cots[0].shape
    tokens -= 16
    cut = tokens // 2
    i, part = place_ref[0], place_ref[1]
    got = got_ref[...].astype(jnp.float32)
    xt_ref[:384] = got[:, :cap].reshape(slots, 384).T
    xt_ref[384:] = got[:, cap:, :128].reshape(slots, 128).T
    wide = 64
    krows = 9 * wide // 2
    token = lax.broadcasted_iota(jnp.int32, (1, tokens), 1)
    line, cell = token // 16 % 16, token % 16
    slot_id = lax.broadcasted_iota(jnp.int32, (slots, tokens), 0)
    ones = (lax.broadcasted_iota(jnp.int32, (16, tokens), 0) == 0).astype(jnp.float32)
    cots = {j: cots[j % 2 * 4 + j // 2] for j in range(8)}
    for j in range(8):
        member = i ^ j
        xt = xt_ref[pl.ds(pl.multiple_of(member * wide, wide), wide), :].astype(jnp.bfloat16)
        last = cots[j][tokens:].astype(jnp.float32)
        last = last[0:2] * cap + last[2:4]
        slot = jnp.concatenate([last[0:1], last[1:2]], axis=1).astype(jnp.int32)
        hit = (slot_id == slot).astype(jnp.float32).astype(jnp.bfloat16)
        quant = jnp.dot(xt, hit, preferred_element_type=jnp.float32)
        taps = []
        for down in (-1, 0, 1):
            for right in (-1, 0, 1):
                shift = (-(down * 16 + right)) % tokens
                moved = quant if shift == 0 else pltpu.roll(quant, shift, 1)
                valid = (line + down >= 0) & (line + down < 16) & (cell + right >= 0) & (cell + right < 16)
                taps.append(moved * valid.astype(jnp.float32))
        taps = [x[: wide // 2] for x in taps] + [x[wide // 2 :] for x in taps]
        left = jnp.concatenate(taps + [ones], axis=0).astype(jnp.bfloat16)
        value = jnp.dot(left, cots[j][:tokens], preferred_element_type=jnp.float32)
        if j == 0:
            acc_ref[...] = value
        else:
            acc_ref[...] += value


def pack_kernel(krows, place_ref, acc_ref, *refs):
    proj_refs, (own_ref, *send_refs) = refs[:4], refs[4:]
    part = place_ref[1]

    def proj(q):
        return sum(ref[q].astype(jnp.float32) for ref in proj_refs)

    def piece(q):
        lanes = pl.ds(pl.multiple_of(q % 2 * 128, 128), 128)
        rows = pl.ds(pl.multiple_of(q // 2 * krows, 8), krows)
        return acc_ref[rows, lanes], acc_ref[2 * krows :, lanes]

    own_ref[:krows], own_ref[krows : krows + 16] = piece(part)
    own_ref[krows + 16 :] = proj(part)
    row = lax.broadcasted_iota(jnp.int32, (16, 128), 0)
    for k, send_ref in enumerate(send_refs, 1):
        value, last = piece((part + k) % PARTS)
        upper = last.astype(jnp.bfloat16).astype(jnp.float32)
        lower = (last - upper)[0:1]
        send_ref[:krows] = value.astype(jnp.bfloat16)
        send_ref[krows : krows + 16] = jnp.where(row == 1, lower, last).astype(jnp.bfloat16)
        send_ref[krows + 16 :] = proj((part + k) % PARTS).astype(jnp.bfloat16)


def group_weights(grid, place, got, cots, cap):
    channels = cots[0].shape[1]
    slots = grid.total * cap
    return pl.pallas_call(
        functools.partial(weights_kernel, grid, cap),
        out_shape=jax.ShapeDtypeStruct((9 * 64 + 16, channels), jnp.float32),
        in_specs=[SMEM_SPEC] + vmem(9),
        out_specs=vmem(1)[0],
        scratch_shapes=[pltpu.VMEM((512, slots), jnp.float32)],
        compiler_params=LIMIT,
        cost_estimate=cost(2 * 9 * 512 * 512 * channels, 8 << 20),
    )(place, got, *cots)


def pack(place, acc, proj):
    krows = (acc.shape[0] - 16) // 2
    height = krows + 16 + proj[0].shape[1]
    return pl.pallas_call(
        functools.partial(pack_kernel, krows),
        out_shape=[jax.ShapeDtypeStruct((height, 128), jnp.float32)]
        + [jax.ShapeDtypeStruct((height, 128), jnp.bfloat16)] * (PARTS - 1),
        in_specs=[SMEM_SPEC] + vmem(5),
        out_specs=vmem(PARTS),
        compiler_params=LIMIT,
    )(place, acc, *proj)


def combine_kernel(krows, own_ref, *refs):
    got_refs, out_ref = refs[:-1], refs[-1]
    total = own_ref[...]
    for ref in got_refs:
        total = total + ref[...].astype(jnp.float32)
    kernel = total[:krows]
    proj = total[krows + 16 :]
    bias = total[krows : krows + 1] + total[krows + 1 : krows + 2]
    row = lax.broadcasted_iota(jnp.int32, (16, own_ref.shape[1]), 0)
    extra = jnp.zeros(row.shape, jnp.float32)
    sums = (
        bias,
        jnp.sum(kernel * kernel, axis=0, keepdims=True),
        jnp.sum(proj * proj, axis=0, keepdims=True),
    )
    for n, value in enumerate(sums):
        upper = value.astype(jnp.bfloat16).astype(jnp.float32)
        middle = (value - upper).astype(jnp.bfloat16).astype(jnp.float32)
        for k, piece in enumerate((upper, middle, value - upper - middle)):
            extra = jnp.where(row == 3 * n + k, piece, extra)
    out_ref[:krows] = kernel.astype(jnp.bfloat16)
    out_ref[krows : krows + 16] = extra.astype(jnp.bfloat16)
    out_ref[krows + 16 :] = proj.astype(jnp.bfloat16)


def combine(krows, own, got):
    return pl.pallas_call(
        functools.partial(combine_kernel, krows),
        out_shape=jax.ShapeDtypeStruct(own.shape, jnp.bfloat16),
        in_specs=vmem(1 + len(got)),
        out_specs=vmem(1)[0],
        compiler_params=LIMIT,
    )(own, *got)


def reduce_planes(grid, own, sends, r):
    got = [send(s, grid.turn(k)) for k, s in enumerate(sends, 1)]
    groups = grid.planes // PARTS
    if groups > 1:
        own = own + sum(g.astype(jnp.float32) for g in got)
        rest = [own] + [send(own, grid.far(k)) for k in range(1, groups)]
        order = (r // PARTS - jnp.arange(groups)) % groups
        own = jnp.sum(jnp.take(jnp.stack(rest), order, axis=0), axis=0)
        got = []
    return own, got


def finish_kernel(krows, counts, place_ref, *refs):
    (kernel_ref, proj_ref, bias_ref, keep_ref), refs = refs[6:], refs[:6]
    i, part = place_ref[0], place_ref[1]
    wide = krows // 9
    prows = refs[0].shape[1] - krows - 16
    sources = []
    near = [(n, 2 * n, 0) for n in range(4)]
    middle = [(n, n // 3 * 2, n % 3 + 1) for n in range(9)]
    last = [(n, 6, n + 1) for n in range(3)]
    for m, ref in enumerate(refs):
        for n, bits, turn in (near, middle, last)[m % 3]:
            place = i ^ (bits + m // 3)
            q = (part + PARTS - turn) % PARTS
            sources.append((ref, n, place, q))
            keep_ref[place * PARTS + q] = ref[n, krows : krows + 16].astype(jnp.float32)
    kept = jnp.sum(keep_ref[...], axis=0)

    def factor(values, count):
        total = jnp.sum(jnp.sum(values, axis=0, keepdims=True), axis=1, keepdims=True)
        return 1.0 / jnp.sqrt(total / count + norm_eps)

    kfactor, pfactor = factor(kept[3:6], counts[0]), factor(kept[6:9], counts[1])
    for ref, n, place, q in sources:
        value = ref[n].astype(jnp.float32)
        lanes = pl.ds(pl.multiple_of(place // 4 * 256 + q % 2 * 128, 128), 128)
        start = place % 4 * 64 + q // 2 * 32
        kernel_ref[:, pl.ds(pl.multiple_of(start, 32), wide), lanes] = (
            value[:krows] * kfactor
        ).reshape(9, wide, 128)
        row, col = proj_place(place, q, prows)
        proj_ref[pl.ds(pl.multiple_of(row, 8), prows), pl.ds(pl.multiple_of(col * 128, 128), 128)] = (
            value[krows + 16 :] * pfactor
        )
    bias = [jnp.sum(keep_ref[n, 0:3], axis=0, keepdims=True) for n in (0, 1, 16, 17)]
    bias = jnp.concatenate(bias, axis=1)
    bias_ref[...] = bias * factor(bias * bias, counts[2])


def finish(place, blocks, zch, channels, feat):
    krows = 9 * zch // 8
    counts = (9 * zch * channels, feat * zch, channels)
    return pl.pallas_call(
        functools.partial(finish_kernel, krows, counts),
        out_shape=(
            jax.ShapeDtypeStruct((9, zch, channels), jnp.float32),
            jax.ShapeDtypeStruct((feat, zch), jnp.float32),
            jax.ShapeDtypeStruct((1, channels), jnp.float32),
        ),
        in_specs=[SMEM_SPEC] + vmem(6),
        out_specs=tuple(vmem(3)),
        scratch_shapes=[pltpu.VMEM((32, 16, 128), jnp.float32)],
        compiler_params=LIMIT,
    )(place, *blocks)


def gather_near(grid, near, far):
    return [near, send(near, grid.flip(2)), send(far, grid.flip(4)), send(far, grid.flip(6))]


def on_device(
    grid, codebook, projector, latents, wanted, wanted_count, token_pick, kernel, bias, cotangent
):
    devices = grid.total
    images, rows, width, zch = latents.shape
    channels = kernel.shape[3]
    feat = codebook.shape[1]
    cap = wanted.shape[2]
    slots = devices * cap
    tokens = images * rows * width
    r, i = grid.place()
    place = jnp.stack([i, r % PARTS]).astype(jnp.int32)
    slot, parts, ask = token_part(
        token_pick.reshape(images * rows, width),
        wanted_count,
        jnp.swapaxes(wanted.reshape(devices, cap), 0, 1),
        latents.reshape(tokens, zch),
    )
    near, far = block_part(parts, cotangent.reshape(tokens, channels))
    asked = spread(ask, grid)
    cots = gather_near(grid, near, far)
    local_codes = jnp.dot(codebook, projector, preferred_element_type=jnp.float32).astype(
        jnp.bfloat16
    )
    slot_ids = jnp.arange(slots, dtype=jnp.int32)
    onehot = (slot.reshape(tokens, 1) == slot_ids[None, :]).astype(jnp.bfloat16)
    replies = answer(grid, asked, local_codes)
    got = spread(replies, grid)
    asked, _, *cots = lax.optimization_barrier((asked, replies, *cots))
    cots = cots + [send(x, grid.flip(1)) for x in cots]
    kept, sent = proj_part(place, asked, codebook, local_codes)
    proj = proj_split(place, kept, send(sent, grid.flip(1)))
    cotangent, _ = lax.optimization_barrier((cotangent, replies))
    gains = [send(x, grid.flip(bits)) for x, bits in zip(proj[1:], (2, 4, 6))]
    acc = group_weights(grid, place, got, cots, cap)
    own, *sends = pack(place, acc, [proj[0]] + gains)
    codes = got[:, cap:, 128:].reshape(slots, zch)
    codes, own, *sends = lax.optimization_barrier((codes, own, *sends))
    own, received = reduce_planes(grid, own, sends, r)
    quant = jnp.dot(onehot, codes, preferred_element_type=jnp.float32).astype(jnp.bfloat16)
    quant = quant.reshape(images, rows, width, zch)
    quant_f = quant.astype(jnp.float32)
    latent_f = latents.astype(jnp.float32)
    padded = jnp.pad(quant, ((0, 0), (1, 1), (1, 1), (0, 0)))
    padded_grad = jnp.pad(cotangent, ((0, 0), (1, 1), (1, 1), (0, 0)))
    output = jnp.zeros((images, rows, width, channels), jnp.float32)
    grad_input = jnp.zeros((images, rows, width, zch), jnp.float32)
    for row_off in range(3):
        for col_off in range(3):
            window = padded[:, row_off : row_off + rows, col_off : col_off + width]
            output = output + jnp.einsum(
                "nhwc,co->nhwo",
                window,
                kernel[row_off, col_off],
                preferred_element_type=jnp.float32,
            )
            grad_window = padded_grad[
                :, 2 - row_off : 2 - row_off + rows, 2 - col_off : 2 - col_off + width
            ]
            grad_input = grad_input + jnp.einsum(
                "nhwo,co->nhwc",
                grad_window,
                kernel[row_off, col_off],
                preferred_element_type=jnp.float32,
            )
    hidden = (output + bias.astype(jnp.float32)).astype(jnp.bfloat16)
    grad_latents = (grad_input + 2.0 * commit_weight * (latent_f - quant_f)).astype(jnp.bfloat16)
    krows = 9 * zch // 8
    planes = gather_planes(grid, combine(krows, own, received))
    *planes, hidden, grad_latents = lax.optimization_barrier((*planes, hidden, grad_latents))
    blocks = gather_places(grid, *planes)
    kernel_step, proj_step, bias_step = finish(place, blocks, zch, channels, feat)
    kernel_step = kernel_step.reshape(3, 3, zch, channels)
    return (hidden, grad_latents, proj_step, kernel_step, bias_step.reshape(channels))


def solution(mesh):
    grid = Grid(mesh.shape["dp"], mesh.shape["code"])
    in_specs = (
        P(("dp", "code"), None),
        P(),
        P(("dp", "code"), None, None, None),
        P(("dp", "code"), None, None),
        P(("dp", "code"), None),
        P(("dp", "code"), None, None),
        P(),
        P(),
        P(("dp", "code"), None, None, None),
    )
    out_specs = (
        P(("dp", "code"), None, None, None),
        P(("dp", "code"), None, None, None),
        P(),
        P(),
        P(),
    )
    return jax.shard_map(
        functools.partial(on_device, grid),
        mesh=mesh,
        in_specs=in_specs,
        out_specs=out_specs,
        check_vma=False,
    )
```

```python
import functools

import jax
import jax.numpy as jnp
from jax import lax
from jax.experimental import pallas as pl
from jax.experimental.pallas import tpu as pltpu
from jax.sharding import PartitionSpec as P

commit_weight = 0.25
norm_eps = 1e-06
AXES = ("dp", "code")
PARTS = 4


class Grid:
    def __init__(self, n_dp, n_code):
        self.n_dp, self.n_code = n_dp, n_code
        self.outer = n_code // 4
        self.planes = (n_dp // 2) * self.outer
        self.total = n_dp * n_code

    def linear(self, r, i):
        dh, ch = r // self.outer, r % self.outer
        return (dh * 2 + i // 4) * self.n_code + ch * 4 + i % 4

    def perm(self, move):
        return [
            (self.linear(r, i), self.linear(*move(r, i)))
            for r in range(self.planes)
            for i in range(8)
        ]

    def flip(self, bit):
        return self.perm(lambda r, i: (r, i ^ bit))

    def turn(self, k):
        return self.perm(lambda r, i: (r // PARTS * PARTS + (r + k) % PARTS, i))

    def far(self, k):
        groups = self.planes // PARTS
        return self.perm(lambda r, i: ((r // PARTS + k) % groups * PARTS + r % PARTS, i))

    def order(self, x):
        rest = x.shape[2:]
        x = x.reshape(self.n_dp // 2, self.outer, 2, 4, *rest)
        return jnp.swapaxes(x, 1, 2).reshape(self.total, *rest)

    def place(self):
        dp, code = lax.axis_index("dp"), lax.axis_index("code")
        return (dp // 2) * self.outer + code // 4, (dp % 2) * 4 + code % 4


def send(x, perm):
    return lax.ppermute(x, AXES, perm)


def gather_planes(grid, own):
    zs = [send(own, grid.turn(k)) for k in range(1, PARTS)]
    x, y = send(own, grid.flip(2)), send(own, grid.flip(4))
    early = jnp.stack([own, x, y, send(own, grid.flip(6))])
    zs = jnp.stack(zs)
    return early, zs, send(zs, grid.flip(2)), send(zs, grid.flip(4))


def gather_places(grid, early, zs, xs, ys):
    count, height, wide = zs.shape
    cut = count * height // 2
    second = send(ys.reshape(-1, wide)[:cut], grid.flip(2))
    first = send(xs.reshape(-1, wide)[cut:], grid.flip(4))
    last = jnp.concatenate([second, first]).reshape(zs.shape)
    mine = [early, jnp.concatenate([zs, xs, ys]), last]
    return mine + [send(x, grid.flip(1)) for x in mine]


def vmem(count):
    return [pl.BlockSpec(memory_space=pltpu.VMEM)] * count


SMEM_SPEC = pl.BlockSpec(memory_space=pltpu.SMEM)
LIMIT = pltpu.CompilerParams(vmem_limit_bytes=40 << 20)


def cost(flops, nbytes):
    return pl.CostEstimate(flops=flops, bytes_accessed=nbytes, transcendentals=0)


def spread(x, grid):
    return lax.all_to_all(x, AXES, split_axis=0, concat_axis=0, tiled=True)


def token_slots(cap, pick, counts):
    lines, width = pick.shape
    devices = counts.shape[1]
    tokens = lines * width
    owner = pick // cap
    first = pick - owner * cap
    token = lax.broadcasted_iota(jnp.int32, (width, tokens), 1)
    wide = (token % width == lax.broadcasted_iota(jnp.int32, (width, tokens), 0)).astype(jnp.float32)
    wide = wide.astype(jnp.bfloat16)
    token = lax.broadcasted_iota(jnp.int32, (lines, tokens), 1)
    keep = token // width == lax.broadcasted_iota(jnp.int32, (lines, tokens), 0)

    def flat(x):
        x = x.astype(jnp.float32).astype(jnp.bfloat16)
        x = jnp.dot(x, wide, preferred_element_type=jnp.float32)
        return jnp.sum(jnp.where(keep, x, 0.0), axis=0, keepdims=True)

    owner, entry = flat(owner), flat(first)
    row = lax.broadcasted_iota(jnp.int32, (devices, devices), 0)
    col = lax.broadcasted_iota(jnp.int32, (devices, devices), 1)
    counts = jnp.where(row == col, counts.astype(jnp.float32), 0.0)
    counts = jnp.sum(counts, axis=1, keepdims=True)
    owner_id = lax.broadcasted_iota(jnp.int32, (devices, tokens), 0)
    count = jnp.sum(
        jnp.where(owner_id == owner.astype(jnp.int32), counts, 0.0), axis=0, keepdims=True
    )
    for _ in range(cap - 1):
        entry = jnp.where(entry >= count, entry - count, entry)
    return owner, entry


def fetch(sources, targets, sems):
    copies = [
        pltpu.make_async_copy(source, target, sems.at[n])
        for n, (source, target) in enumerate(zip(sources, targets))
    ]
    for copy in copies:
        copy.start()
    for copy in copies:
        copy.wait()


def token_kernel(cap, pick_hbm, counts_hbm, wanted_hbm, latents_hbm, slot_ref, parts_ref, ask_ref, *rest):
    pick_ref, counts_ref, wanted_ref, latents_ref, sems = rest
    fetch((pick_hbm, counts_hbm, wanted_hbm, latents_hbm), rest[:-1], sems)
    owner, entry = token_slots(cap, pick_ref[...], counts_ref[...])
    tokens, devices = owner.shape[1], counts_ref.shape[1]
    slots = devices * cap
    slot = (owner * cap + entry).astype(jnp.int32)
    slot_ref[...] = slot
    row = lax.broadcasted_iota(jnp.int32, (8, tokens), 0)
    parts_ref[...] = jnp.where(row == 0, owner, jnp.where(row == 1, entry, 0.0))
    hit = (lax.broadcasted_iota(jnp.int32, (slots, tokens), 0) == slot).astype(jnp.float32)
    uses = jnp.sum(hit, axis=1, keepdims=True)
    sums = jnp.dot(hit.astype(jnp.bfloat16), latents_ref[...], preferred_element_type=jnp.float32)
    zch = sums.shape[1]
    wanted = wanted_ref[...].astype(jnp.float32).T
    wanted = jnp.broadcast_to(wanted[:, None, :], (devices, cap, cap)).reshape(slots, cap)
    place = lax.broadcasted_iota(jnp.int32, (slots, cap), 0) % cap
    lane = lax.broadcasted_iota(jnp.int32, (slots, cap), 1)
    wanted = jnp.sum(jnp.where(lane == place, wanted, 0.0), axis=1, keepdims=True)
    lane = lax.broadcasted_iota(jnp.int32, (slots, 128), 1)
    last = jnp.where(lane == 0, uses, jnp.where(lane == 1, wanted, 0.0))
    ask_ref[:, :, :zch] = sums.reshape(devices, cap, zch)
    ask_ref[:, :, zch:] = last.reshape(devices, cap, 128)


def token_part(pick, counts, wanted, latents):
    cap, devices = wanted.shape
    tokens = pick.shape[0] * pick.shape[1]
    slots = devices * cap
    return pl.pallas_call(
        functools.partial(token_kernel, cap),
        out_shape=(
            jax.ShapeDtypeStruct((1, tokens), jnp.int32),
            jax.ShapeDtypeStruct((8, tokens), jnp.float32),
            jax.ShapeDtypeStruct((devices, cap, latents.shape[1] + 128), jnp.float32),
        ),
        in_specs=[pl.BlockSpec(memory_space=pltpu.HBM)] * 4,
        out_specs=tuple(vmem(3)),
        scratch_shapes=[pltpu.VMEM(x.shape, x.dtype) for x in (pick, counts, wanted, latents)]
        + [pltpu.SemaphoreType.DMA((4,))],
        compiler_params=pltpu.CompilerParams(vmem_limit_bytes=62 << 20),
        cost_estimate=cost(2 * slots * tokens * latents.shape[1], 2 << 20),
    )(pick, counts, wanted, latents)


def block_kernel(parts_ref, cot_ref, near_ref, far_ref):
    tokens, channels = cot_ref.shape
    wide = channels // 2
    place = lax.broadcasted_iota(jnp.int32, (16, wide), 0)
    extra = jnp.zeros((16, wide), jnp.float32)
    rows = [parts_ref[n : n + 1, m * wide : (m + 1) * wide] for n in range(2) for m in range(2)]
    for n, row in enumerate(rows):
        extra = jnp.where(place == n, row, extra)
    side = lax.axis_index("dp") % 2
    for ref, side in ((near_ref, side), (far_ref, 1 - side)):
        ref[:tokens] = cot_ref[:, pl.ds(pl.multiple_of(side * wide, wide), wide)]
        ref[tokens:] = extra.astype(jnp.bfloat16)


def block_part(parts, cots):
    tokens, channels = cots.shape
    return pl.pallas_call(
        block_kernel,
        out_shape=(jax.ShapeDtypeStruct((tokens + 16, channels // 2), jnp.bfloat16),) * 2,
        in_specs=vmem(2),
        out_specs=tuple(vmem(2)),
        compiler_params=LIMIT,
        cost_estimate=cost(0, 1 << 20),
    )(parts, cots)


def select_rows(asked, zch, entries):
    column = asked[:, zch + 1 : zch + 2].astype(jnp.int32)
    hit = column == lax.broadcasted_iota(jnp.int32, (asked.shape[0], entries), 1)
    return hit.astype(jnp.float32).astype(jnp.bfloat16)


def answer_kernel(grid, cap, asked_ref, codes_ref, out_ref):
    devices = grid.total
    entries, zch = codes_ref.shape
    select = select_rows(asked_ref[...].reshape(devices * cap, zch + 128), zch, entries)
    codes = jnp.dot(select, codes_ref[...], preferred_element_type=jnp.float32)
    whole = codes.reshape(devices, cap, zch)
    second = lax.broadcasted_iota(jnp.int32, (cap, 128), 1) >= 64
    turned = {}
    for v in range(2):
        part = codes[:, v * 128 : (v + 1) * 128]
        turned[v, 0] = part.reshape(devices, cap, 128)
        turned[v, 1] = pltpu.roll(part, 64, 1).reshape(devices, cap, 128)
    for r in range(grid.planes):
        for u in range(4):
            v, a = u // 2, u % 2
            slices = [
                jnp.where(
                    second,
                    turned[v, 1 - a][grid.linear(r, 2 * h + 1)],
                    turned[v, a][grid.linear(r, 2 * h)],
                )
                for h in range(4)
            ]
            for dest in (grid.linear(r, u), grid.linear(r, u + 4)):
                top = jnp.concatenate(slices[:3], axis=1)
                bottom = jnp.concatenate([slices[3], whole[dest]], axis=1)
                out_ref[dest] = jnp.concatenate([top, bottom], axis=0).astype(jnp.bfloat16)


def answer(grid, asked, codes):
    devices, cap, _ = asked.shape
    zch = codes.shape[1]
    return pl.pallas_call(
        functools.partial(answer_kernel, grid, cap),
        out_shape=jax.ShapeDtypeStruct((devices, 2 * cap, 384), jnp.bfloat16),
        in_specs=vmem(2),
        out_specs=vmem(1)[0],
        compiler_params=LIMIT,
        cost_estimate=cost(2 * devices * cap * codes.shape[0] * zch, 2 << 20),
    )(asked, codes)


def proj_kernel(place_ref, asked_ref, book_ref, codes_ref, keep_ref, send_ref, all_ref):
    entries, feat = book_ref.shape
    zch = codes_ref.shape[1]
    devices, cap, _ = asked_ref.shape
    asked = asked_ref[...].reshape(devices * cap, zch + 128)
    select = select_rows(asked, zch, entries)
    codes = jnp.dot(select, codes_ref[...], preferred_element_type=jnp.float32)
    rows = jnp.dot(select, book_ref[...], preferred_element_type=jnp.float32).astype(jnp.bfloat16)
    grads = 2.0 * (asked[:, zch : zch + 1] * codes - asked[:, :zch])
    upper = grads.astype(jnp.bfloat16)
    lower = (grads - upper.astype(jnp.float32)).astype(jnp.bfloat16)
    dims = (((0,), (0,)), ((), ()))
    total = lax.dot_general(rows, upper, dims, preferred_element_type=jnp.float32)
    all_ref[...] = total + lax.dot_general(rows, lower, dims, preferred_element_type=jnp.float32)
    core = place_ref[0] % 2
    keep_ref[...] = all_ref[:, pl.ds(pl.multiple_of(core * 128, 128), 128)]
    send_ref[...] = all_ref[:, pl.ds(pl.multiple_of((1 - core) * 128, 128), 128)]


def proj_part(place, asked, book, codes):
    feat, zch = book.shape[1], codes.shape[1]
    slots = asked.shape[0] * asked.shape[1]
    return pl.pallas_call(
        proj_kernel,
        out_shape=(jax.ShapeDtypeStruct((feat, 128), jnp.float32),) * 2,
        in_specs=[SMEM_SPEC] + vmem(3),
        out_specs=tuple(vmem(2)),
        scratch_shapes=[pltpu.VMEM((feat, zch), jnp.float32)],
        compiler_params=LIMIT,
        cost_estimate=cost(2 * slots * (book.shape[0] + 2 * zch) * feat, 4 << 20),
    )(place, asked, book, codes)


def proj_split_kernel(place_ref, kept_ref, got_ref, own_ref, *rest):
    send_refs, all_ref = rest[:-1], rest[-1]
    all_ref[...] = kept_ref[...] + got_ref[...]
    i = place_ref[0]
    size = all_ref.shape[0] // 4

    def quarter(place):
        start = (place // 2 % 2 * 2 + place // 4) * size
        return all_ref[pl.ds(pl.multiple_of(start, 8), size), :].reshape(own_ref.shape)

    own_ref[...] = quarter(i)
    for bits, send_ref in zip((2, 4, 6), send_refs):
        send_ref[...] = quarter(i ^ bits).astype(jnp.bfloat16)


def proj_split(place, kept, got):
    shape = (PARTS, kept.shape[0] // 16, 128)
    return pl.pallas_call(
        proj_split_kernel,
        out_shape=[jax.ShapeDtypeStruct(shape, jnp.float32)]
        + [jax.ShapeDtypeStruct(shape, jnp.bfloat16)] * 3,
        in_specs=[SMEM_SPEC] + vmem(2),
        out_specs=vmem(4),
        scratch_shapes=[pltpu.VMEM(kept.shape, jnp.float32)],
        compiler_params=LIMIT,
    )(place, kept, got)


def proj_place(i, q, prows):
    return (((i // 2) % 2) * 2 + i // 4) * PARTS * prows + q * prows, i % 2


def weights_kernel(grid, cap, place_ref, got_ref, *refs):
    cots, (acc_ref, xt_ref) = refs[:8], refs[8:]
    devices = grid.total
    slots = devices * cap
    tokens, channels = cots[0].shape
    tokens -= 16
    cut = tokens // 2
    i, part = place_ref[0], place_ref[1]
    got = got_ref[...].astype(jnp.float32)
    xt_ref[:384] = got[:, :cap].reshape(slots, 384).T
    xt_ref[384:] = got[:, cap:, :128].reshape(slots, 128).T
    wide = 64
    krows = 9 * wide // 2
    token = lax.broadcasted_iota(jnp.int32, (1, tokens), 1)
    line, cell = token // 16 % 16, token % 16
    slot_id = lax.broadcasted_iota(jnp.int32, (slots, tokens), 0)
    ones = (lax.broadcasted_iota(jnp.int32, (16, tokens), 0) == 0).astype(jnp.float32)
    cots = {j: cots[j % 2 * 4 + j // 2] for j in range(8)}
    for j in range(8):
        member = i ^ j
        xt = xt_ref[pl.ds(pl.multiple_of(member * wide, wide), wide), :].astype(jnp.bfloat16)
        last = cots[j][tokens:].astype(jnp.float32)
        last = last[0:2] * cap + last[2:4]
        slot = jnp.concatenate([last[0:1], last[1:2]], axis=1).astype(jnp.int32)
        hit = (slot_id == slot).astype(jnp.float32).astype(jnp.bfloat16)
        quant = jnp.dot(xt, hit, preferred_element_type=jnp.float32)
        taps = []
        for down in (-1, 0, 1):
            for right in (-1, 0, 1):
                shift = (-(down * 16 + right)) % tokens
                moved = quant if shift == 0 else pltpu.roll(quant, shift, 1)
                valid = (line + down >= 0) & (line + down < 16) & (cell + right >= 0) & (cell + right < 16)
                taps.append(moved * valid.astype(jnp.float32))
        taps = [x[: wide // 2] for x in taps] + [x[wide // 2 :] for x in taps]
        left = jnp.concatenate(taps + [ones], axis=0).astype(jnp.bfloat16)
        value = jnp.dot(left, cots[j][:tokens], preferred_element_type=jnp.float32)
        if j == 0:
            acc_ref[...] = value
        else:
            acc_ref[...] += value


def pack_kernel(krows, place_ref, acc_ref, *refs):
    proj_refs, (own_ref, *send_refs) = refs[:4], refs[4:]
    part = place_ref[1]

    def proj(q):
        return sum(ref[q].astype(jnp.float32) for ref in proj_refs)

    def piece(q):
        lanes = pl.ds(pl.multiple_of(q % 2 * 128, 128), 128)
        rows = pl.ds(pl.multiple_of(q // 2 * krows, 8), krows)
        return acc_ref[rows, lanes], acc_ref[2 * krows :, lanes]

    own_ref[:krows], own_ref[krows : krows + 16] = piece(part)
    own_ref[krows + 16 :] = proj(part)
    row = lax.broadcasted_iota(jnp.int32, (16, 128), 0)
    for k, send_ref in enumerate(send_refs, 1):
        value, last = piece((part + k) % PARTS)
        upper = last.astype(jnp.bfloat16).astype(jnp.float32)
        lower = (last - upper)[0:1]
        send_ref[:krows] = value.astype(jnp.bfloat16)
        send_ref[krows : krows + 16] = jnp.where(row == 1, lower, last).astype(jnp.bfloat16)
        send_ref[krows + 16 :] = proj((part + k) % PARTS).astype(jnp.bfloat16)


def group_weights(grid, place, got, cots, cap):
    channels = cots[0].shape[1]
    slots = grid.total * cap
    return pl.pallas_call(
        functools.partial(weights_kernel, grid, cap),
        out_shape=jax.ShapeDtypeStruct((9 * 64 + 16, channels), jnp.float32),
        in_specs=[SMEM_SPEC] + vmem(9),
        out_specs=vmem(1)[0],
        scratch_shapes=[pltpu.VMEM((512, slots), jnp.float32)],
        compiler_params=LIMIT,
        cost_estimate=cost(2 * 9 * 512 * 512 * channels, 8 << 20),
    )(place, got, *cots)


def pack(place, acc, proj):
    krows = (acc.shape[0] - 16) // 2
    height = krows + 16 + proj[0].shape[1]
    return pl.pallas_call(
        functools.partial(pack_kernel, krows),
        out_shape=[jax.ShapeDtypeStruct((height, 128), jnp.float32)]
        + [jax.ShapeDtypeStruct((height, 128), jnp.bfloat16)] * (PARTS - 1),
        in_specs=[SMEM_SPEC] + vmem(5),
        out_specs=vmem(PARTS),
        compiler_params=LIMIT,
    )(place, acc, *proj)


def combine_kernel(krows, own_ref, *refs):
    got_refs, out_ref = refs[:-1], refs[-1]
    total = own_ref[...]
    for ref in got_refs:
        total = total + ref[...].astype(jnp.float32)
    kernel = total[:krows]
    proj = total[krows + 16 :]
    bias = total[krows : krows + 1] + total[krows + 1 : krows + 2]
    row = lax.broadcasted_iota(jnp.int32, (16, own_ref.shape[1]), 0)
    extra = jnp.zeros(row.shape, jnp.float32)
    sums = (
        bias,
        jnp.sum(kernel * kernel, axis=0, keepdims=True),
        jnp.sum(proj * proj, axis=0, keepdims=True),
    )
    for n, value in enumerate(sums):
        upper = value.astype(jnp.bfloat16).astype(jnp.float32)
        middle = (value - upper).astype(jnp.bfloat16).astype(jnp.float32)
        for k, piece in enumerate((upper, middle, value - upper - middle)):
            extra = jnp.where(row == 3 * n + k, piece, extra)
    out_ref[:krows] = kernel.astype(jnp.bfloat16)
    out_ref[krows : krows + 16] = extra.astype(jnp.bfloat16)
    out_ref[krows + 16 :] = proj.astype(jnp.bfloat16)


def combine(krows, own, got):
    return pl.pallas_call(
        functools.partial(combine_kernel, krows),
        out_shape=jax.ShapeDtypeStruct(own.shape, jnp.bfloat16),
        in_specs=vmem(1 + len(got)),
        out_specs=vmem(1)[0],
        compiler_params=LIMIT,
    )(own, *got)


def reduce_planes(grid, own, sends, r):
    got = [send(s, grid.turn(k)) for k, s in enumerate(sends, 1)]
    groups = grid.planes // PARTS
    if groups > 1:
        own = own + sum(g.astype(jnp.float32) for g in got)
        rest = [own] + [send(own, grid.far(k)) for k in range(1, groups)]
        order = (r // PARTS - jnp.arange(groups)) % groups
        own = jnp.sum(jnp.take(jnp.stack(rest), order, axis=0), axis=0)
        got = []
    return own, got


def finish_kernel(krows, counts, place_ref, *refs):
    (kernel_ref, proj_ref, bias_ref, keep_ref), refs = refs[6:], refs[:6]
    i, part = place_ref[0], place_ref[1]
    wide = krows // 9
    prows = refs[0].shape[1] - krows - 16
    sources = []
    near = [(n, 2 * n, 0) for n in range(4)]
    middle = [(n, n // 3 * 2, n % 3 + 1) for n in range(9)]
    last = [(n, 6, n + 1) for n in range(3)]
    for m, ref in enumerate(refs):
        for n, bits, turn in (near, middle, last)[m % 3]:
            place = i ^ (bits + m // 3)
            q = (part + PARTS - turn) % PARTS
            sources.append((ref, n, place, q))
            keep_ref[place * PARTS + q] = ref[n, krows : krows + 16].astype(jnp.float32)
    kept = jnp.sum(keep_ref[...], axis=0)

    def factor(values, count):
        total = jnp.sum(jnp.sum(values, axis=0, keepdims=True), axis=1, keepdims=True)
        return 1.0 / jnp.sqrt(total / count + norm_eps)

    kfactor, pfactor = factor(kept[3:6], counts[0]), factor(kept[6:9], counts[1])
    for ref, n, place, q in sources:
        value = ref[n].astype(jnp.float32)
        lanes = pl.ds(pl.multiple_of(place // 4 * 256 + q % 2 * 128, 128), 128)
        start = place % 4 * 64 + q // 2 * 32
        kernel_ref[:, pl.ds(pl.multiple_of(start, 32), wide), lanes] = (
            value[:krows] * kfactor
        ).reshape(9, wide, 128)
        row, col = proj_place(place, q, prows)
        proj_ref[pl.ds(pl.multiple_of(row, 8), prows), pl.ds(pl.multiple_of(col * 128, 128), 128)] = (
            value[krows + 16 :] * pfactor
        )
    bias = [jnp.sum(keep_ref[n, 0:3], axis=0, keepdims=True) for n in (0, 1, 16, 17)]
    bias = jnp.concatenate(bias, axis=1)
    bias_ref[...] = bias * factor(bias * bias, counts[2])


def finish(place, blocks, zch, channels, feat):
    krows = 9 * zch // 8
    counts = (9 * zch * channels, feat * zch, channels)
    return pl.pallas_call(
        functools.partial(finish_kernel, krows, counts),
        out_shape=(
            jax.ShapeDtypeStruct((9, zch, channels), jnp.float32),
            jax.ShapeDtypeStruct((feat, zch), jnp.float32),
            jax.ShapeDtypeStruct((1, channels), jnp.float32),
        ),
        in_specs=[SMEM_SPEC] + vmem(6),
        out_specs=tuple(vmem(3)),
        scratch_shapes=[pltpu.VMEM((32, 16, 128), jnp.float32)],
        compiler_params=LIMIT,
    )(place, *blocks)


def gather_near(grid, near, far):
    return [near, send(near, grid.flip(2)), send(far, grid.flip(4)), send(far, grid.flip(6))]


def on_device(
    grid, codebook, projector, latents, wanted, wanted_count, token_pick, kernel, bias, cotangent
):
    devices = grid.total
    images, rows, width, zch = latents.shape
    channels = kernel.shape[3]
    feat = codebook.shape[1]
    cap = wanted.shape[2]
    slots = devices * cap
    tokens = images * rows * width
    r, i = grid.place()
    place = jnp.stack([i, r % PARTS]).astype(jnp.int32)
    slot, parts, ask = token_part(
        token_pick.reshape(images * rows, width),
        wanted_count,
        jnp.swapaxes(wanted.reshape(devices, cap), 0, 1),
        latents.reshape(tokens, zch),
    )
    near, far = block_part(parts, cotangent.reshape(tokens, channels))
    asked = spread(ask, grid)
    cots = gather_near(grid, near, far)
    local_codes = jnp.dot(codebook, projector, preferred_element_type=jnp.float32).astype(
        jnp.bfloat16
    )
    slot_ids = jnp.arange(slots, dtype=jnp.int32)
    onehot = (slot.reshape(tokens, 1) == slot_ids[None, :]).astype(jnp.bfloat16)
    replies = answer(grid, asked, local_codes)
    got = spread(replies, grid)
    asked, _ = lax.optimization_barrier((asked, replies))
    kept, sent = proj_part(place, asked, codebook, local_codes)
    kept, sent, *cots = lax.optimization_barrier((kept, sent, *cots))
    cots = cots + [send(x, grid.flip(1)) for x in cots]
    proj = proj_split(place, kept, send(sent, grid.flip(1)))
    cotangent, _ = lax.optimization_barrier((cotangent, replies))
    gains = [send(x, grid.flip(bits)) for x, bits in zip(proj[1:], (2, 4, 6))]
    acc = group_weights(grid, place, got, cots, cap)
    own, *sends = pack(place, acc, [proj[0]] + gains)
    codes = got[:, cap:, 128:].reshape(slots, zch)
    codes, own, *sends = lax.optimization_barrier((codes, own, *sends))
    own, received = reduce_planes(grid, own, sends, r)
    quant = jnp.dot(onehot, codes, preferred_element_type=jnp.float32).astype(jnp.bfloat16)
    quant = quant.reshape(images, rows, width, zch)
    quant_f = quant.astype(jnp.float32)
    latent_f = latents.astype(jnp.float32)
    padded = jnp.pad(quant, ((0, 0), (1, 1), (1, 1), (0, 0)))
    padded_grad = jnp.pad(cotangent, ((0, 0), (1, 1), (1, 1), (0, 0)))
    output = jnp.zeros((images, rows, width, channels), jnp.float32)
    grad_input = jnp.zeros((images, rows, width, zch), jnp.float32)
    for row_off in range(3):
        for col_off in range(3):
            window = padded[:, row_off : row_off + rows, col_off : col_off + width]
            output = output + jnp.einsum(
                "nhwc,co->nhwo",
                window,
                kernel[row_off, col_off],
                preferred_element_type=jnp.float32,
            )
            grad_window = padded_grad[
                :, 2 - row_off : 2 - row_off + rows, 2 - col_off : 2 - col_off + width
            ]
            grad_input = grad_input + jnp.einsum(
                "nhwo,co->nhwc",
                grad_window,
                kernel[row_off, col_off],
                preferred_element_type=jnp.float32,
            )
    hidden = (output + bias.astype(jnp.float32)).astype(jnp.bfloat16)
    grad_latents = (grad_input + 2.0 * commit_weight * (latent_f - quant_f)).astype(jnp.bfloat16)
    krows = 9 * zch // 8
    planes = gather_planes(grid, combine(krows, own, received))
    *planes, hidden, grad_latents = lax.optimization_barrier((*planes, hidden, grad_latents))
    blocks = gather_places(grid, *planes)
    kernel_step, proj_step, bias_step = finish(place, blocks, zch, channels, feat)
    kernel_step = kernel_step.reshape(3, 3, zch, channels)
    return (hidden, grad_latents, proj_step, kernel_step, bias_step.reshape(channels))


def solution(mesh):
    grid = Grid(mesh.shape["dp"], mesh.shape["code"])
    in_specs = (
        P(("dp", "code"), None),
        P(),
        P(("dp", "code"), None, None, None),
        P(("dp", "code"), None, None),
        P(("dp", "code"), None),
        P(("dp", "code"), None, None),
        P(),
        P(),
        P(("dp", "code"), None, None, None),
    )
    out_specs = (
        P(("dp", "code"), None, None, None),
        P(("dp", "code"), None, None, None),
        P(),
        P(),
        P(),
    )
    return jax.shard_map(
        functools.partial(on_device, grid),
        mesh=mesh,
        in_specs=in_specs,
        out_specs=out_specs,
        check_vma=False,
    )
```
